32 devices in a mesh: gz: 4 (over z), gx: 8 (over y, x, core).
Axes of the slice: x: 2, y: 2, z: 4, core: 2. Of those that a mesh axis runs over, the one named last changes fastest.
Arguments:
- strain: float32 [6, 2, 1024, 1024], P(None, None, 'gx', 'gz'), may hold values from -6 to 6
- labels: int32 [2, 1024, 1024], P(None, 'gx', 'gz'), may hold values 0 or 1
- normals: int32 [2, 64, 64], P(None, 'gx', 'gz'), may hold values from 0 to 7
- moduli: float32 [5], replicated, may hold values from 0.5 to 4
- mean_strain: float32 [6], replicated, may hold values from -4 to 4
Outputs:
- strain_next: float32 [6, 2, 1024, 1024], P(None, None, 'gx', 'gz')
- stress_next: float32 [6, 2, 1024, 1024], P(None, None, 'gx', 'gz')
The draws below stay inside these ranges and needn't reach their ends.
All inputs are finite; a program needn't handle non-finite values. No bound on the sum of `labels` on one device may be relied on, other than what follows from the above.
Results may differ from the reference program's by a relative error of at most 0.000082.
Values sent between devices are 32-bit elements; how exact they have to be, the bound alone decides.
No kernel may reach another device: no remote copies, remote signals or barrier semaphores. Data moves between devices by JAX's collectives and lax.ppermute only.
A program may use at most 128 MiB of HBM per device.

```python
import math
import jax
import jax.numpy as jnp
from jax import lax

NX = 1024
NZ = 1024
SECTIONS = 2
ANGLES = 8
BLK = 16


def place_ends(values, rng, low, top_value):
    longest = values.shape.index(max(values.shape))
    spots = []
    for shift in (0, 1):
        where = [jax.random.randint(jax.random.fold_in(rng, axis), (), 0, length) for axis, length in enumerate(values.shape)]
        where[longest] = (where[longest] + shift) % values.shape[longest]
        spots.append(tuple(where))
    return values.at[spots[0]].set(low).at[spots[1]].set(top_value)


def steps_of(stream_key, shape, shards, low, high):
    loudness, own = 1.0, jax.random.fold_in(stream_key, 6)
    for dim, shards_of in shards:
        heights = jnp.exp(jax.random.uniform(jax.random.fold_in(own, dim), (shards_of,), jnp.float32, low / len(shards), high / len(shards)))
        loudness = loudness * jnp.repeat(heights, shape[dim] // shards_of).reshape([-1 if axis == dim else 1 for axis in range(len(shape))])
    return loudness


def normal_values(key, shape, deviation, bound, split=(), kind=jnp.bfloat16):
    entries = jax.random.normal(key, shape, jnp.float32) * deviation
    if len(split) > 0:
        entries = steps_of(key, shape, split, -0.22, 0.18) * entries
    return jnp.clip(entries, min=-bound, max=bound).astype(kind)


def setup_inputs(seed: int = 0) -> dict:
    seeds = jax.random.split(jax.random.key(seed), 6)
    strain = normal_values(seeds[0], (6, SECTIONS, NX, NZ), 1.0, 6.0, ((2, 8), (3, 4)), jnp.float32)
    labels = place_ends((jax.random.randint(seeds[1], (SECTIONS, NX, NZ), 0, 5) < 2).astype(jnp.int32), jax.random.fold_in(seeds[1], 1), 0, 1)
    normals = place_ends(jax.random.randint(seeds[2], (SECTIONS, NX // BLK, NZ // BLK), 0, ANGLES), jax.random.fold_in(seeds[2], 1), 0, ANGLES - 1).astype(jnp.int32)
    moduli = jnp.clip(jnp.exp(jax.random.uniform(seeds[3], (5,), jnp.float32, math.log(0.5), math.log(4.0))), 0.5, 4.0)
    mean_strain = normal_values(seeds[4], (6,), 1.0, 4.0, (), jnp.float32)
    return dict(strain=strain, labels=labels, normals=normals, moduli=moduli, mean_strain=mean_strain)


def orientation(normals):
    tilt_angle = math.pi / ANGLES * normals.astype(jnp.float32)
    tilt_angle = jnp.repeat(jnp.repeat(tilt_angle, BLK, axis=1), BLK, axis=2)
    return (jnp.cos(tilt_angle), jnp.sin(tilt_angle))

def stress_law(strain_field, labels, cosine_tilt, sine_tilt, moduli):
    laminate = labels == 1
    lame_local = jnp.where(laminate, moduli[2], moduli[0])
    shear_local = jnp.where(laminate, moduli[3], moduli[1])
    trace_sum = strain_field[0] + strain_field[1] + strain_field[2]
    normal_part = cosine_tilt * cosine_tilt * strain_field[0] + sine_tilt * sine_tilt * strain_field[2] + 2.0 * cosine_tilt * sine_tilt * strain_field[4]
    laminate_term = moduli[4] * labels.astype(jnp.float32) * normal_part
    dyad = [cosine_tilt * cosine_tilt, None, sine_tilt * sine_tilt, None, cosine_tilt * sine_tilt, None]
    result = []
    for slot in range(6):
        value = 2.0 * shear_local * strain_field[slot]
        if slot < 3:
            value = value + lame_local * trace_sum
        if dyad[slot] is not None:
            value = value + laminate_term * dyad[slot]
        result.append(value)
    return jnp.stack(result)

def polarize(stresses, strain_field, lame_ref, shear_ref):
    trace_sum = strain_field[0] + strain_field[1] + strain_field[2]
    result = []
    for slot in range(6):
        value = stresses[slot] - 2.0 * shear_ref * strain_field[slot]
        if slot < 3:
            value = value - lame_ref * trace_sum
        result.append(value)
    return jnp.stack(result)

def green_apply(spectrum, unit_x, unit_z, lame_ref, shear_ref):
    coupling = (lame_ref + shear_ref) / (shear_ref * (lame_ref + 2.0 * shear_ref))
    traction_x = spectrum[0] * unit_x + spectrum[4] * unit_z
    traction_y = spectrum[5] * unit_x + spectrum[3] * unit_z
    traction_z = spectrum[4] * unit_x + spectrum[2] * unit_z
    normal_load = unit_x * traction_x + unit_z * traction_z
    half_inverse = 0.5 / shear_ref
    result = [2.0 * half_inverse * unit_x * traction_x - coupling * normal_load * unit_x * unit_x, jnp.zeros_like(traction_x), 2.0 * half_inverse * unit_z * traction_z - coupling * normal_load * unit_z * unit_z, half_inverse * unit_z * traction_y, half_inverse * (unit_z * traction_x + unit_x * traction_z) - coupling * normal_load * unit_x * unit_z, half_inverse * unit_x * traction_y]
    return -jnp.stack(result)

def signed_freq(length):
    counter = jnp.arange(length, dtype=jnp.int32)
    return jnp.where(counter < length // 2, counter, counter - length).astype(jnp.float32)

def reference(strain, labels, normals, moduli, mean_strain):
    cosine_tilt, sine_tilt = orientation(normals)
    lame_ref = 0.5 * (moduli[0] + moduli[2])
    shear_ref = 0.5 * (moduli[1] + moduli[3])
    stresses = stress_law(strain, labels, cosine_tilt, sine_tilt, moduli)
    polarized = polarize(stresses, strain, lame_ref, shear_ref)
    freq_x = signed_freq(NX)[:, None]
    freq_z = signed_freq(NZ)[None, :]
    radius_sq = freq_x * freq_x + freq_z * freq_z
    at_anchor = radius_sq == 0.0
    safe_radius = jnp.sqrt(jnp.where(at_anchor, 1.0, radius_sq))
    unit_x = freq_x / safe_radius
    unit_z = freq_z / safe_radius
    anchor_term = jnp.where(at_anchor, float(NX * NZ), 0.0)

    def one_section(section_index):
        part_field = lax.dynamic_index_in_dim(polarized, section_index, 1, keepdims=False)
        spectrum = jnp.fft.fft2(part_field, axes=(1, 2))
        real_part = green_apply(spectrum.real, unit_x, unit_z, lame_ref, shear_ref)
        real_part = real_part + mean_strain[:, None, None] * anchor_term[None]
        imag_part = green_apply(spectrum.imag, unit_x, unit_z, lame_ref, shear_ref)
        inverse = jnp.fft.ifft2(real_part + 1j * imag_part, axes=(1, 2)).real
        return inverse.astype(jnp.float32)
    sections_out = lax.map(one_section, jnp.arange(SECTIONS, dtype=jnp.int32))
    strain_next = jnp.moveaxis(sections_out, 0, 1)
    stress_next = stress_law(strain_next, labels, cosine_tilt, sine_tilt, moduli)
    return (strain_next, stress_next)
```

```python
import functools
import math

import jax
import jax.numpy as jnp
import numpy as np
from jax import lax
from jax.experimental import pallas as pl
from jax.experimental.pallas import tpu as pltpu
from jax.sharding import PartitionSpec as P

ANGLES = 8
XX, YY, ZZ, YZ, XZ, XY = range(6)
GROUPS = (
    ((XY, 0), (YZ, 0)),
    ((XX, 0), (ZZ, 0), (XZ, 0)),
    ((XX, 1), (ZZ, 1), (XZ, 1)),
    ((XY, 1), (YZ, 1)),
)
INPLANE = (1, 2)
F32, BF16 = jnp.float32, jnp.bfloat16
MIB = 1 << 20


def split_table(table):
    table = np.asarray(table, np.float32)
    high = table.astype(jnp.bfloat16)
    low = (table - high.astype(np.float32)).astype(jnp.bfloat16)
    return jnp.asarray(high), jnp.asarray(low)


def half_frequencies(length):
    quarter = length // 4
    return (
        4 * np.arange(quarter) + 1,
        4 * np.arange(quarter // 2),
        4 * np.arange(quarter // 2) + 2,
    )


def interleave(real, imag, slots):
    rows, count = real.shape
    both = np.stack([real.reshape(rows, -1, slots), imag.reshape(rows, -1, slots)], 2)
    return both.reshape(rows, 2 * count)


def z_tables(length, slots, scale):
    quarter = length // 4
    z = np.arange(quarter, dtype=np.int64)[:, None]
    ones, zeros, twos = half_frequencies(length)

    def angles(freqs):
        return 2.0 * math.pi / length * ((z * freqs[None, :]) % length)

    one, zero, two = angles(ones), angles(zeros), angles(twos)
    top = interleave(np.cos(one), -np.sin(one), slots)
    bottom = interleave(-np.sin(one), -np.cos(one), slots)
    forward_one = np.concatenate([top, bottom], 0)
    real, imag = np.cos(zero), -np.sin(zero)
    imag[:, 0] = np.where(np.arange(quarter) % 2 == 0, 1.0, -1.0)
    forward_zero = interleave(real, imag, slots)
    forward_two = interleave(np.cos(two), -np.sin(two), slots)
    weight = 2.0 * scale
    inverse_one = weight * np.concatenate(
        [interleave(np.cos(one), -np.sin(one), slots), interleave(np.sin(one), np.cos(one), slots)], 0
    ).T
    half = np.full(quarter // 2, weight)
    half[0] = scale
    inverse_zero = interleave(real * half, imag * half, slots).T
    inverse_two = weight * forward_two.T
    return (
        split_table(forward_one) + split_table(np.stack([forward_zero, forward_two])),
        split_table(inverse_one) + split_table(np.stack([inverse_zero, inverse_two])),
    )


def x_tables(length):
    quarter = length // 4
    k = np.arange(quarter, dtype=np.int64)
    forward, inverse = [], []
    for residue in range(4):
        angle = 2.0 * math.pi / length * (((4 * k[:, None] + residue) * k[None, :]) % length)
        forward.append(np.concatenate([np.cos(angle), np.sin(angle)], 0))
        inverse.append(np.concatenate([np.cos(angle.T), np.sin(angle.T)], 0))
    return split_table(np.stack(forward)) + split_table(np.stack(inverse))


def halves(value):
    high = value.astype(BF16)
    return high, (value - high.astype(F32)).astype(BF16)


def dot(left, right):
    return jnp.dot(left, right, preferred_element_type=F32)


def dot_right(value, high_table, low_table):
    high, low = halves(value)
    return dot(high, high_table) + (dot(low, high_table) + dot(high, low_table))


def dot_left(high_table, low_table, high, low):
    return dot(high_table, high) + (dot(high_table, low) + dot(low_table, high))


def tilt(normals, section, cells_z):
    blocks = normals[section].astype(F32)
    count = blocks.shape[1]
    size = cells_z // count
    owner = lax.broadcasted_iota(jnp.int32, (count, cells_z), 1) // size
    own = lax.broadcasted_iota(jnp.int32, (count, cells_z), 0)
    spread = jnp.where(owner == own, 1.0, 0.0).astype(F32)
    angle = (math.pi / ANGLES) * dot(blocks, spread)
    cosine, sine = jnp.cos(angle), jnp.sin(angle)
    return cosine * cosine, sine * sine, cosine * sine


def law(strain, label, squares, lame, shear, stiff):
    cc, ss, cs = squares
    laminate = label == 1
    lame_local = jnp.where(laminate, lame[1], lame[0])
    twice_shear = jnp.where(laminate, 2.0 * shear[1], 2.0 * shear[0])
    spherical = lame_local * (strain[XX] + strain[YY] + strain[ZZ])
    normal = cc * strain[XX] + ss * strain[ZZ] + 2.0 * cs * strain[XZ]
    normal = jnp.where(laminate, stiff, 0.0) * normal
    return {
        XX: twice_shear * strain[XX] + spherical + normal * cc,
        YY: twice_shear * strain[YY] + spherical,
        ZZ: twice_shear * strain[ZZ] + spherical + normal * ss,
        YZ: twice_shear * strain[YZ],
        XZ: twice_shear * strain[XZ] + normal * cs,
        XY: twice_shear * strain[XY],
    }


def row_of(squares, block, size):
    return [jnp.broadcast_to(s[block : block + 1], (size, s.shape[1])) for s in squares]


def polarize_kernel(moduli, strain, labels, normals, *rest):
    outs, held = rest[:-1], rest[-1]
    parts = len(GROUPS)
    place = lax.axis_index("gz")
    sections, cells_x, cells_z = labels.shape
    size = cells_x // normals.shape[1]
    lame_ref = 0.5 * (moduli[0] + moduli[2])
    shear_ref = 0.5 * (moduli[1] + moduli[3])
    lame = (moduli[0] - lame_ref, moduli[2] - lame_ref)
    shear = (moduli[1] - shear_ref, moduli[3] - shear_ref)
    for group, fields in enumerate(GROUPS):
        if len(fields) < 3:
            held[group, 2] = jnp.zeros((cells_x, cells_z), F32)
    for section in range(sections):
        squares = tilt(normals, section, cells_z)
        for block in range(cells_x // size):
            rows = pl.ds(block * size, size)
            local = [strain[c, section, rows, :] for c in range(6)]
            value = law(local, labels[section, rows, :], row_of(squares, block, size), lame, shear, moduli[4])
            for group, fields in enumerate(GROUPS):
                for slot, (component, of) in enumerate(fields):
                    if of == section:
                        held[group, slot, rows, :] = value[component]
    for step in range(parts):
        target = lax.rem(place + step, parts)
        outs[step][...] = held[target, 0:2]
        outs[parts + step][...] = held[target, 2:3]


def z_forward_kernel(one_h, one_l, two_h, two_l, *rest):
    parts = len(GROUPS)
    pairs, thirds, out, held = rest[:parts], rest[parts : 2 * parts], rest[-2], rest[-1]
    place = lax.axis_index("gz")
    for step in range(parts):
        source = lax.rem(place + parts - step, parts)
        held[source, 0:2] = pairs[step][...]
        held[source, 2:3] = thirds[step][...]
    fields, rows, width = held.shape[1:]
    lanes = out.shape[3]
    z0, z1, z2, z3 = (held[k].reshape(fields * rows, width) for k in range(parts))
    first = jnp.concatenate([z0 - z2, z1 - z3], 1)
    even, odd = z0 + z2, z1 + z3
    spectra = (
        dot_right(first, one_h[...], one_l[...]),
        dot_right(even + odd, two_h[0], two_l[0]),
        dot_right(even - odd, two_h[1], two_l[1]),
    )
    target = 0
    for spectrum in spectra:
        for k in range(spectrum.shape[1] // lanes):
            out[target] = spectrum[:, k * lanes : (k + 1) * lanes].reshape(fields, rows, lanes)
            target += 1


def quarter_turn(value, sign):
    lanes = value.shape[1]
    return jnp.concatenate(
        [pltpu.roll(value[:, k : k + 128], 64, 1) for k in range(0, lanes, 128)], 1
    ) * sign


def green_kernel(x_cells, z_cells, moduli, mean, fwd_h, fwd_l, inv_h, inv_l, data, out, low_s, high_s, field_s):
    sources, fields, rows, lanes = data.shape
    quarter = x_cells // 4
    per = quarter // rows
    slots = lanes // 2
    width = (fields + 1) * lanes
    place, mine = lax.axis_index("gz"), lax.axis_index("gx")
    inplane = functools.reduce(jnp.logical_or, [place == k for k in INPLANE])
    lame_ref = 0.5 * (moduli[0] + moduli[2])
    shear_ref = 0.5 * (moduli[1] + moduli[3])
    half_inverse = 0.5 / shear_ref
    coupling = (lame_ref + shear_ref) / (shear_ref * (lame_ref + 2.0 * shear_ref))
    c1 = jnp.where(inplane, coupling, 0.0)
    k1 = jnp.where(inplane, 2.0 * half_inverse, half_inverse)
    k2 = jnp.where(inplane, half_inverse, 0.0)
    ka = jnp.where(inplane, 0.0, half_inverse)
    lane_all = lax.broadcasted_iota(jnp.int32, (1, width), 1) % lanes
    sign_all = jnp.where(lane_all < slots, 1.0, -1.0)
    sign = sign_all[:, : fields * lanes]
    lane = lane_all[:, :lanes]

    block = [
        jnp.concatenate(
            [data[a * per : (a + 1) * per, f].reshape(quarter, lanes) for f in range(fields)], 1
        )
        for a in range(4)
    ]
    even, odd = block[0] + block[2], block[1] + block[3]
    diff, turned = block[0] - block[2], quarter_turn(block[1] - block[3], sign)
    for residue, value in enumerate((even + odd, diff + turned, even - odd, diff - turned)):
        high_s[residue, :, : fields * lanes], low_s[residue, :, : fields * lanes] = halves(value)

    order = mine * slots + lane % slots
    quarter_z = z_cells // 4
    kz = jnp.where(
        order < quarter_z,
        4 * order + 1,
        jnp.where(order < quarter_z + quarter_z // 2, 4 * (order - quarter_z), 4 * (order - quarter_z - quarter_z // 2) + 2),
    )
    special = jnp.logical_and(order == quarter_z, lane >= 0)
    kz = jnp.where(kz < z_cells // 2, kz, kz - z_cells).astype(F32)

    def coefficients(kx, kz, odd_mask):
        radius = kx * kx + kz * kz
        inverse = 1.0 / jnp.where(radius == 0.0, 1.0, radius)
        a, b = kx * kx * inverse, kz * kz * inverse
        d = kx * kz * inverse * odd_mask
        ab = a * b
        ca, cb = k2 - c1 * a, k2 - c1 * b
        return (
            a * (k1 - c1 * a),
            b * (k1 - c1 * b),
            ka * d - c1 * ab,
            d * ca,
            d * cb,
            k2 - 2.0 * c1 * ab,
        )

    def apply(m, s):
        m00, m11, m01, h02, h12, m22 = m
        return (
            -(m00 * s[0] + m01 * s[1] + 2.0 * (h02 * s[2])),
            -(m01 * s[0] + m11 * s[1] + 2.0 * (h12 * s[2])),
            -(h02 * s[0] + h12 * s[1] + m22 * s[2]),
        )

    for residue in range(4):
        both = dot_left(
            fwd_h[residue], fwd_l[residue], high_s[residue, :, : fields * lanes], low_s[residue, :, : fields * lanes]
        )
        spectrum = both[:quarter] + quarter_turn(both[quarter:], sign)
        s = [spectrum[:, f * lanes : (f + 1) * lanes] for f in range(fields)]
        kx = 4 * lax.broadcasted_iota(jnp.int32, (quarter, lanes), 0) + residue
        kx_edge = kx == x_cells // 2
        anchor = jnp.logical_and(kx == 0, special)
        kx = jnp.where(kx < x_cells // 2, kx, kx - x_cells).astype(F32)
        keep = jnp.where(kx_edge, 0.0, 1.0)
        new = apply(coefficients(kx, jnp.broadcast_to(kz, kx.shape), keep), s)
        real_lane = lane < slots
        new = [
            jnp.where(anchor, jnp.where(real_lane, float(x_cells * z_cells) * mean[f], 0.0), new[f])
            for f in range(fields)
        ]
        keep = jnp.where(kx_edge, 1.0, 0.0)
        edge = apply(coefficients(kx, jnp.full(kx.shape, -0.5 * z_cells, F32), keep), s)
        extra = edge[0]
        for f in range(1, fields):
            extra = jnp.where(lane % slots == f, pltpu.roll(edge[f], f, 1), extra)
        high_s[residue], low_s[residue] = halves(jnp.concatenate(list(new) + [extra], 1))

    for residue in range(4):
        both = dot_left(inv_h[residue], inv_l[residue], high_s[residue], low_s[residue])
        field_s[residue] = both[:quarter] - quarter_turn(both[quarter:], sign_all)
    h0, h1, h2, h3 = (field_s[k] for k in range(4))
    even, odd = h0 + h2, h1 + h3
    diff, turned = h0 - h2, quarter_turn(h1 - h3, sign_all)
    swap = jnp.logical_and(special, lane >= slots)
    for a, value in enumerate((even + odd, diff - turned, even - odd, diff + turned)):
        extra = value[:, fields * lanes :]
        for f in range(fields):
            moved = extra if f == 0 else pltpu.roll(extra, lanes - f, 1)
            final = jnp.where(swap, moved, value[:, f * lanes : (f + 1) * lanes])
            out[a * per : (a + 1) * per, f] = final.reshape(per, rows, lanes)


def z_inverse_kernel(one_h, one_l, two_h, two_l, data, *rest):
    outs, held = rest[:-1], rest[-1]
    parts = len(GROUPS)
    place = lax.axis_index("gz")
    sources, fields, rows, lanes = data.shape
    half = sources // 2
    fourth = sources // 4

    def columns(begin, end):
        return jnp.concatenate([data[k].reshape(fields * rows, lanes) for k in range(begin, end)], 1)

    first = dot_right(columns(0, half), one_h[...], one_l[...])
    zero = dot_right(columns(half, half + fourth), two_h[0], two_l[0])
    two = dot_right(columns(half + fourth, sources), two_h[1], two_l[1])
    width = zero.shape[1]
    real, imag = first[:, :width], first[:, width:]
    plus, minus = zero + two, zero - two
    for k, value in enumerate((plus + real, minus - imag, plus - real, minus + imag)):
        held[k] = value.reshape(fields, rows, width)
    for step in range(parts):
        target = lax.rem(place + step, parts)
        outs[step][...] = held[target, 0:2]
        outs[parts + step][...] = held[target, 2:3]


def stress_kernel(moduli, mean, labels, normals, *rest):
    parts = len(GROUPS)
    pairs, thirds = rest[:parts], rest[parts : 2 * parts]
    strain_out, stress_out, held = rest[2 * parts :]
    place = lax.axis_index("gz")
    sections, cells_x, cells_z = labels.shape
    size = cells_x // normals.shape[1]
    for step in range(parts):
        source = lax.rem(place + parts - step, parts)
        held[source, 0:2] = pairs[step][...]
        held[source, 2:3] = thirds[step][...]
    for section in range(sections):
        squares = tilt(normals, section, cells_z)
        for block in range(cells_x // size):
            rows = pl.ds(block * size, size)
            local = {YY: jnp.full((size, cells_z), mean[YY], F32)}
            for group, fields in enumerate(GROUPS):
                for slot, (component, of) in enumerate(fields):
                    if of == section:
                        local[component] = held[group, slot, rows, :]
            value = law(
                local,
                labels[section, rows, :],
                row_of(squares, block, size),
                (moduli[0], moduli[2]),
                (moduli[1], moduli[3]),
                moduli[4],
            )
            for component in range(6):
                strain_out[component, section, rows, :] = local[component]
                stress_out[component, section, rows, :] = value[component]


def call(kernel, outs, scratch, smem, args, limit, flops=0):
    vmem = pl.BlockSpec(memory_space=pltpu.VMEM)
    scalar = pl.BlockSpec(memory_space=pltpu.SMEM)
    moved = sum(a.size * a.dtype.itemsize for a in args) + sum(math.prod(o) * 4 for o in outs)
    return pl.pallas_call(
        kernel,
        out_shape=[jax.ShapeDtypeStruct(o, F32) for o in outs],
        in_specs=[scalar] * smem + [vmem] * (len(args) - smem),
        out_specs=[vmem] * len(outs),
        scratch_shapes=scratch,
        compiler_params=pltpu.CompilerParams(vmem_limit_bytes=limit * MIB),
        cost_estimate=pl.CostEstimate(flops=flops, bytes_accessed=moved, transcendentals=0),
    )(*args)


def shards(strain, labels, normals, moduli, mean_strain):
    parts = lax.axis_size("gz")
    x_devices = lax.axis_size("gx")
    _, sections, cells_x, cells_z = strain.shape
    x_total, z_total = cells_x * x_devices, cells_z * parts
    slots = z_total // 2 // x_devices
    lanes = 2 * slots
    z_fwd, z_inv = z_tables(z_total, slots, 1.0 / (x_total * z_total))
    x_tab = x_tables(x_total)
    pair, third = (2, cells_x, cells_z), (1, cells_x, cells_z)

    def travel(outs, sources, targets):
        pairs, thirds = list(outs[:parts]), list(outs[parts:])
        for step in range(1, parts):
            way = [(k, (k + step) % parts) for k in range(parts)]
            some = [(a, b) for a, b in way if a in sources and b in targets]
            pairs[step] = lax.ppermute(pairs[step], "gz", way)
            thirds[step] = lax.ppermute(thirds[step], "gz", some)
        return pairs + thirds

    everyone = range(parts)
    held = pltpu.VMEM((parts, 3, cells_x, cells_z), F32)
    sent = call(
        polarize_kernel, [pair] * parts + [third] * parts, [held], 1, (moduli, strain, labels, normals), 16
    )
    arrived = travel(sent, everyone, INPLANE)
    grid = (x_devices, 3, cells_x, lanes)
    (rows,) = call(z_forward_kernel, [grid], [held], 0, (*z_fwd, *arrived), 24)
    rows = lax.all_to_all(rows, "gx", 0, 0, tiled=True)
    index = lax.axis_index("gz")
    inplane = functools.reduce(jnp.logical_or, [index == k for k in INPLANE])
    mean = jnp.where(
        inplane,
        jnp.stack([mean_strain[XX], mean_strain[ZZ], mean_strain[XZ]]),
        jnp.stack([mean_strain[XY], mean_strain[YZ], mean_strain[XZ]]),
    )
    quarter = x_total // 4
    (rows,) = call(
        functools.partial(green_kernel, x_total, z_total),
        [grid],
        [
            pltpu.VMEM((4, quarter, 4 * lanes), BF16),
            pltpu.VMEM((4, quarter, 4 * lanes), BF16),
            pltpu.VMEM((4, quarter, 4 * lanes), F32),
        ],
        2,
        (moduli, mean, *x_tab, rows),
        32,
    )
    rows = lax.all_to_all(rows, "gx", 0, 0, tiled=True)
    sent = call(z_inverse_kernel, [pair] * parts + [third] * parts, [held], 0, (*z_inv, rows), 24)
    arrived = travel(sent, INPLANE, everyone)
    full = (6, sections, cells_x, cells_z)
    return tuple(
        call(stress_kernel, [full, full], [held], 2, (moduli, mean_strain, labels, normals, *arrived), 16)
    )


def orientation(normals, blk):
    tilt_angle = math.pi / ANGLES * normals.astype(jnp.float32)
    tilt_angle = jnp.repeat(jnp.repeat(tilt_angle, blk, axis=1), blk, axis=2)
    return (jnp.cos(tilt_angle), jnp.sin(tilt_angle))


def stress_law(strain_field, labels, cosine_tilt, sine_tilt, moduli):
    laminate = labels == 1
    lame_local = jnp.where(laminate, moduli[2], moduli[0])
    shear_local = jnp.where(laminate, moduli[3], moduli[1])
    trace_sum = strain_field[0] + strain_field[1] + strain_field[2]
    normal_part = (
        cosine_tilt * cosine_tilt * strain_field[0]
        + sine_tilt * sine_tilt * strain_field[2]
        + 2.0 * cosine_tilt * sine_tilt * strain_field[4]
    )
    laminate_term = moduli[4] * labels.astype(jnp.float32) * normal_part
    dyad = [
        cosine_tilt * cosine_tilt,
        None,
        sine_tilt * sine_tilt,
        None,
        cosine_tilt * sine_tilt,
        None,
    ]
    result = []
    for slot in range(6):
        value = 2.0 * shear_local * strain_field[slot]
        if slot < 3:
            value = value + lame_local * trace_sum
        if dyad[slot] is not None:
            value = value + laminate_term * dyad[slot]
        result.append(value)
    return jnp.stack(result)


def polarize(stresses, strain_field, lame_ref, shear_ref):
    trace_sum = strain_field[0] + strain_field[1] + strain_field[2]
    result = []
    for slot in range(6):
        value = stresses[slot] - 2.0 * shear_ref * strain_field[slot]
        if slot < 3:
            value = value - lame_ref * trace_sum
        result.append(value)
    return jnp.stack(result)


def green_apply(spectrum, unit_x, unit_z, lame_ref, shear_ref):
    coupling = (lame_ref + shear_ref) / (shear_ref * (lame_ref + 2.0 * shear_ref))
    traction_x = spectrum[0] * unit_x + spectrum[4] * unit_z
    traction_y = spectrum[5] * unit_x + spectrum[3] * unit_z
    traction_z = spectrum[4] * unit_x + spectrum[2] * unit_z
    normal_load = unit_x * traction_x + unit_z * traction_z
    half_inverse = 0.5 / shear_ref
    result = [
        2.0 * half_inverse * unit_x * traction_x - coupling * normal_load * unit_x * unit_x,
        jnp.zeros_like(traction_x),
        2.0 * half_inverse * unit_z * traction_z - coupling * normal_load * unit_z * unit_z,
        half_inverse * unit_z * traction_y,
        half_inverse * (unit_z * traction_x + unit_x * traction_z)
        - coupling * normal_load * unit_x * unit_z,
        half_inverse * unit_x * traction_y,
    ]
    return -jnp.stack(result)


def twiddle(left_ids, right_ids, length):
    product = left_ids[:, None] * right_ids[None, :] % length
    phase_angle = 2.0 * math.pi / length * product.astype(jnp.float32)
    return (jnp.cos(phase_angle), jnp.sin(phase_angle))


def contract(form, left_side, right_side):
    return jnp.einsum(
        form,
        left_side,
        right_side,
        precision=lax.Precision.HIGHEST,
        preferred_element_type=jnp.float32,
    )


def signed_value(counter, length):
    return jnp.where(counter < length // 2, counter, counter - length).astype(jnp.float32)


def shards_general(strain, labels, normals, moduli, mean_strain):
    z_devices = lax.axis_size("gz")
    x_devices = lax.axis_size("gx")
    z_index = lax.axis_index("gz")
    x_index = lax.axis_index("gx")
    sections = strain.shape[1]
    cells_x = strain.shape[2]
    cells_z = strain.shape[3]
    x_total = cells_x * x_devices
    z_total = cells_z * z_devices
    line_count = sections * cells_x
    kz_share = cells_z // x_devices
    cosine_tilt, sine_tilt = orientation(normals, strain.shape[2] // normals.shape[1])
    lame_ref = 0.5 * (moduli[0] + moduli[2])
    shear_ref = 0.5 * (moduli[1] + moduli[3])
    stresses = stress_law(strain, labels, cosine_tilt, sine_tilt, moduli)
    polarized = polarize(stresses, strain, lame_ref, shear_ref)
    flattened = polarized.reshape(6, line_count, cells_z)
    own_block = z_index * cells_z + jnp.arange(cells_z, dtype=jnp.int32)
    empty_sum = jnp.zeros((6, cells_z, line_count), jnp.float32)
    pieces = lax.all_gather(flattened, "gz", axis=2, tiled=True)
    z_ids = jnp.arange(pieces.shape[2], dtype=jnp.int32)
    cos_table, sin_table = twiddle(z_ids, own_block, z_total)
    real_part = contract("cmz,zk->ckm", pieces, cos_table)
    imag_part = (empty_sum, empty_sum)[1] - contract("cmz,zk->ckm", pieces, sin_table)
    real_rows, imag_rows = (
        lax.all_to_all(real_part, "gx", split_axis=1, concat_axis=2, tiled=True),
        lax.all_to_all(imag_part, "gx", split_axis=1, concat_axis=2, tiled=True),
    )
    grid_shape = (6, kz_share, x_devices, sections, cells_x)
    real_rows = real_rows.reshape(grid_shape)
    imag_rows = imag_rows.reshape(grid_shape)
    every_x = jnp.arange(x_total, dtype=jnp.int32)
    cos_x, sin_x = twiddle(every_x, every_x, x_total)
    cos_x = cos_x.reshape(x_devices, cells_x, x_total)
    sin_x = sin_x.reshape(x_devices, cells_x, x_total)
    spec_real = contract("ckgsx,gxq->cksq", real_rows, cos_x) + contract(
        "ckgsx,gxq->cksq", imag_rows, sin_x
    )
    spec_imag = contract("ckgsx,gxq->cksq", imag_rows, cos_x) - contract(
        "ckgsx,gxq->cksq", real_rows, sin_x
    )
    kz_ids = z_index * cells_z + x_index * kz_share + jnp.arange(kz_share, dtype=jnp.int32)
    freq_z = signed_value(kz_ids, z_total)[:, None, None]
    freq_x = signed_value(every_x, x_total)[None, None, :]
    radius_sq = freq_x * freq_x + freq_z * freq_z
    at_anchor = radius_sq == 0.0
    safe_radius = jnp.sqrt(jnp.where(at_anchor, 1.0, radius_sq))
    unit_x = freq_x / safe_radius
    unit_z = freq_z / safe_radius
    anchor_term = jnp.where(at_anchor, float(x_total * z_total), 0.0)
    new_real = green_apply(spec_real, unit_x, unit_z, lame_ref, shear_ref)
    new_real = new_real + mean_strain[:, None, None, None] * anchor_term[None]
    new_imag = green_apply(spec_imag, unit_x, unit_z, lame_ref, shear_ref)
    back_real = contract("cksq,gxq->ckgsx", new_real, cos_x) - contract(
        "cksq,gxq->ckgsx", new_imag, sin_x
    )
    back_imag = contract("cksq,gxq->ckgsx", new_real, sin_x) + contract(
        "cksq,gxq->ckgsx", new_imag, cos_x
    )
    back_real = back_real.reshape(6, kz_share, x_devices * line_count)
    back_imag = back_imag.reshape(6, kz_share, x_devices * line_count)
    real_part, imag_part = (
        lax.all_to_all(back_real, "gx", split_axis=2, concat_axis=1, tiled=True),
        lax.all_to_all(back_imag, "gx", split_axis=2, concat_axis=1, tiled=True),
    )
    z_ids = jnp.arange(lax.axis_size("gz") * cells_z, dtype=jnp.int32)
    cos_table, sin_table = twiddle(own_block, z_ids, z_total)
    summed = lax.psum_scatter(
        contract("ckm,kz->zcm", real_part, cos_table)
        - contract("ckm,kz->zcm", imag_part, sin_table),
        "gz",
        scatter_dimension=0,
        tiled=True,
    )
    field_lines = jnp.transpose(summed, (1, 2, 0))
    strain_next = (field_lines * (1.0 / (x_total * z_total))).reshape(6, sections, cells_x, cells_z)
    stress_next = stress_law(strain_next, labels, cosine_tilt, sine_tilt, moduli)
    return (strain_next, stress_next)


def solution(mesh):
    in_specs = (P(None, None, "gx", "gz"), P(None, "gx", "gz"), P(None, "gx", "gz"), P(), P())
    out_specs = (P(None, None, "gx", "gz"), P(None, None, "gx", "gz"))

    def run(strain, labels, normals, moduli, mean_strain):
        _, sections, x_total, z_total = strain.shape
        parts, x_devices = mesh.shape["gz"], mesh.shape["gx"]
        grouped = (
            sections == 2
            and parts == len(GROUPS)
            and x_devices % 8 == 0
            and z_total == 128 * x_devices
            and x_total % (128 * x_devices) == 0
        )
        body = shards if grouped else shards_general
        mapped = jax.shard_map(body, mesh=mesh, in_specs=in_specs, out_specs=out_specs, check_vma=False)
        return mapped(strain, labels, normals, moduli, mean_strain)

    return run
```

```python
import functools
import math

import jax
import jax.numpy as jnp
import numpy as np
from jax import lax
from jax.experimental import pallas as pl
from jax.experimental.pallas import tpu as pltpu
from jax.sharding import PartitionSpec as P

ANGLES = 8
XX, YY, ZZ, YZ, XZ, XY = range(6)
GROUPS = (
    ((XY, 0), (YZ, 0)),
    ((XX, 0), (ZZ, 0), (XZ, 0)),
    ((XX, 1), (ZZ, 1), (XZ, 1)),
    ((XY, 1), (YZ, 1)),
)
INPLANE = (1, 2)
FIELDS = 3
CHUNKS = ((2, 0), (1,))
F32, BF16 = jnp.float32, jnp.bfloat16
MIB = 1 << 20


def split_table(table):
    table = np.asarray(table, np.float32)
    high = table.astype(jnp.bfloat16)
    low = (table - high.astype(np.float32)).astype(jnp.bfloat16)
    return jnp.asarray(np.stack([high, low]))


def half_frequencies(length):
    quarter = length // 4
    return (
        4 * np.arange(quarter) + 1,
        4 * np.arange(quarter // 2),
        4 * np.arange(quarter // 2) + 2,
    )


def interleave(real, imag, slots):
    rows, count = real.shape
    both = np.stack([real.reshape(rows, -1, slots), imag.reshape(rows, -1, slots)], 2)
    return both.reshape(rows, 2 * count)


def z_tables(length, slots, scale):
    quarter = length // 4
    z = np.arange(quarter, dtype=np.int64)[:, None]
    ones, zeros, twos = half_frequencies(length)

    def angles(freqs):
        return 2.0 * math.pi / length * ((z * freqs[None, :]) % length)

    one, zero, two = angles(ones), angles(zeros), angles(twos)
    top = interleave(np.cos(one), -np.sin(one), slots)
    bottom = interleave(-np.sin(one), -np.cos(one), slots)
    forward_one = np.concatenate([top, bottom], 0)
    real, imag = np.cos(zero), -np.sin(zero)
    imag[:, 0] = np.where(np.arange(quarter) % 2 == 0, 1.0, -1.0)
    forward_zero = interleave(real, imag, slots)
    forward_two = interleave(np.cos(two), -np.sin(two), slots)
    weight = 2.0 * scale
    inverse_one = weight * np.concatenate(
        [interleave(np.cos(one), -np.sin(one), slots), interleave(np.sin(one), np.cos(one), slots)], 0
    ).T
    half = np.full(quarter // 2, weight)
    half[0] = scale
    inverse_zero = interleave(real * half, imag * half, slots).T
    inverse_two = weight * forward_two.T

    def pack(first, second, third):
        return split_table(np.concatenate([first, np.concatenate([second, third], 1)], 0))

    return pack(forward_one, forward_zero, forward_two), pack(inverse_one, inverse_zero, inverse_two)


def x_tables(length):
    quarter = length // 4
    k = np.arange(quarter, dtype=np.int64)
    angle = 2.0 * math.pi / quarter * ((k[:, None] * k[None, :]) % quarter)
    turn = 2.0 * math.pi / length * k
    columns = [f(residue * turn) for residue in (1, 2, 3) for f in (np.cos, np.sin)]
    twiddles = jnp.asarray(np.stack(columns + columns[:2], 1).astype(np.float32))
    return split_table(np.concatenate([np.cos(angle), np.sin(angle)], 0)), twiddles


def halves(value):
    high = value.astype(BF16)
    return high, (value - high.astype(F32)).astype(BF16)


def dot(left, right):
    return jnp.dot(left, right, preferred_element_type=F32)


def dot_right(value, table, part):
    big = table.shape[2]
    half = big // 2
    rows = slice(0, big) if part == 0 else slice(big, big + half)
    columns = slice(0, big) if part == 0 else slice((part - 1) * half, part * half)
    high_table, low_table = table[0, rows, columns], table[1, rows, columns]
    high, low = halves(value)
    return dot(high, high_table) + (dot(low, high_table) + dot(high, low_table))


def dot_left(table, value):
    high, low = halves(value)
    return dot(table[0], high) + (dot(table[0], low) + dot(table[1], high))


def tilt(normals, section, cells_z):
    blocks = normals[section].astype(F32)
    count = blocks.shape[1]
    size = cells_z // count
    owner = lax.broadcasted_iota(jnp.int32, (count, cells_z), 1) // size
    own = lax.broadcasted_iota(jnp.int32, (count, cells_z), 0)
    spread = jnp.where(owner == own, 1.0, 0.0).astype(F32)
    angle = (math.pi / ANGLES) * dot(blocks, spread)
    cosine, sine = jnp.cos(angle), jnp.sin(angle)
    return cosine * cosine, sine * sine, cosine * sine


def law(strain, label, squares, lame, shear, stiff):
    cc, ss, cs = squares
    laminate = label == 1
    lame_local = jnp.where(laminate, lame[1], lame[0])
    twice_shear = jnp.where(laminate, 2.0 * shear[1], 2.0 * shear[0])
    spherical = lame_local * (strain[XX] + strain[YY] + strain[ZZ])
    normal = cc * strain[XX] + ss * strain[ZZ] + 2.0 * cs * strain[XZ]
    normal = jnp.where(laminate, stiff, 0.0) * normal
    return {
        XX: twice_shear * strain[XX] + spherical + normal * cc,
        YY: twice_shear * strain[YY] + spherical,
        ZZ: twice_shear * strain[ZZ] + spherical + normal * ss,
        YZ: twice_shear * strain[YZ],
        XZ: twice_shear * strain[XZ] + normal * cs,
        XY: twice_shear * strain[XY],
    }


def row_of(squares, block, size):
    return [jnp.broadcast_to(s[block : block + 1], (size, s.shape[1])) for s in squares]


def polarize_kernel(moduli_h, strain_h, labels_h, normals_h, *rest):
    outs, (held, strain, labels, normals, moduli, sems) = rest[:-6], rest[-6:]
    sections, cells_x, cells_z = labels.shape
    copies = [
        pltpu.make_async_copy(moduli_h, moduli, sems.at[0]),
        pltpu.make_async_copy(normals_h, normals, sems.at[1]),
    ]
    for k in range(sections):
        copies.append(pltpu.make_async_copy(labels_h.at[k], labels.at[k], sems.at[2 + 2 * k]))
        copies.append(pltpu.make_async_copy(strain_h.at[:, k], strain.at[:, k], sems.at[3 + 2 * k]))
    for copy in copies:
        copy.start()
    for copy in copies[:2]:
        copy.wait()
    parts = len(GROUPS)
    place = lax.axis_index("gz")
    size = cells_x // normals.shape[1]
    lame_ref = 0.5 * (moduli[0] + moduli[2])
    shear_ref = 0.5 * (moduli[1] + moduli[3])
    lame = (moduli[0] - lame_ref, moduli[2] - lame_ref)
    shear = (moduli[1] - shear_ref, moduli[3] - shear_ref)
    for group, fields in enumerate(GROUPS):
        if len(fields) < 3:
            held[group, 2] = jnp.zeros((cells_x, cells_z), F32)
    for section in range(sections):
        copies[2 + 2 * section].wait()
        copies[3 + 2 * section].wait()
        squares = tilt(normals, section, cells_z)
        for block in range(cells_x // size):
            rows = pl.ds(block * size, size)
            local = [strain[c, section, rows, :] for c in range(6)]
            value = law(local, labels[section, rows, :], row_of(squares, block, size), lame, shear, moduli[4])
            for group, fields in enumerate(GROUPS):
                for slot, (component, of) in enumerate(fields):
                    if of == section:
                        held[group, slot, rows, :] = value[component]
    for step in range(parts):
        target = lax.rem(place + step, parts)
        for slot in range(FIELDS):
            outs[slot * parts + step][...] = held[target, slot]


def z_forward_kernel(table, *rest):
    parts = len(GROUPS)
    size = (len(rest) - 1) // parts
    arrived, out, held, sems = rest[: size * parts], *rest[size * parts :][:2], rest[size * parts + 2 :]
    place = lax.axis_index("gz")
    copies = []
    for step in range(parts):
        source = lax.rem(place + parts - step, parts)
        for slot in range(size):
            block = arrived[slot * parts + step]
            if sems:
                copies.append(pltpu.make_async_copy(block, held.at[source, slot], sems[0].at[len(copies)]))
            else:
                held[source, slot] = block[...]
    for copy in copies:
        copy.start()
    for copy in copies:
        copy.wait()
    fields, rows, width = held.shape[1:]
    lanes = out.shape[3]
    z0, z1, z2, z3 = (held[k].reshape(fields * rows, width) for k in range(parts))
    first = jnp.concatenate([z0 - z2, z1 - z3], 1)
    even, odd = z0 + z2, z1 + z3
    spectra = (
        dot_right(first, table, 0),
        dot_right(even + odd, table, 1),
        dot_right(even - odd, table, 2),
    )
    target = 0
    for spectrum in spectra:
        for k in range(spectrum.shape[1] // lanes):
            out[target] = spectrum[:, k * lanes : (k + 1) * lanes].reshape(fields, rows, lanes)
            target += 1


def swap(value):
    lanes = value.shape[1]
    return jnp.concatenate([pltpu.roll(value[:, k : k + 128], 64, 1) for k in range(0, lanes, 128)], 1)


def turn_sign(width):
    lane = lax.broadcasted_iota(jnp.int32, (1, width), 1) % 128
    return jnp.where(lane < 64, 1.0, -1.0).astype(F32)


def twiddle(twiddles, residue, value, sign):
    if residue == 0:
        return value
    pick = 2 * (residue - 1)
    quarter = value.shape[0]
    cosine = jnp.broadcast_to(twiddles[:, pick : pick + 1], (quarter, 128))
    sine = jnp.broadcast_to(twiddles[:, pick + 1 : pick + 2], (quarter, 128)) * sign[:, :128]
    pieces = []
    for k in range(0, value.shape[1], 128):
        piece = value[:, k : k + 128]
        pieces.append(cosine * piece + sine * pltpu.roll(piece, 64, 1))
    return jnp.concatenate(pieces, 1)


def x_forward(data, table, twiddles):
    sources, fields, rows, lanes = data.shape
    quarter = sources * rows // 4
    per = sources // 4
    sign = turn_sign(fields * lanes)
    block = [
        jnp.concatenate([data[a * per : (a + 1) * per, f].reshape(quarter, lanes) for f in range(fields)], 1)
        for a in range(4)
    ]
    even, odd = block[0] + block[2], block[1] + block[3]
    diff, turned = block[0] - block[2], sign * swap(block[1] - block[3])
    for residue, value in enumerate((even + odd, diff + turned, even - odd, diff - turned)):
        both = dot_left(table, twiddle(twiddles, residue, value, sign))
        yield both[:quarter] + sign * swap(both[quarter:])


def x_inverse(spectra, table, twiddles, is_special, out):
    sources, fields, rows, lanes = out.shape
    quarter = sources * rows // 4
    per = sources // 4
    sign = turn_sign((fields + 1) * lanes)
    parts = []
    for residue in range(4):
        both = dot_left(table, spectra(residue))
        parts.append(twiddle(twiddles, residue, both[:quarter] - sign * swap(both[quarter:]), -sign))
    h0, h1, h2, h3 = parts
    even, odd = h0 + h2, h1 + h3
    diff, turned = h0 - h2, sign * swap(h1 - h3)
    lane = lax.broadcasted_iota(jnp.int32, (1, lanes), 1)
    edge = jnp.logical_and(is_special, lane == lanes // 2)
    for a, value in enumerate((even + odd, diff - turned, even - odd, diff + turned)):
        extra = value[:, fields * lanes :]
        for f in range(fields):
            moved = extra if f == 0 else pltpu.roll(extra, lanes - f, 1)
            final = jnp.where(edge, moved, value[:, f * lanes : (f + 1) * lanes])
            out[a * per : (a + 1) * per, f] = final.reshape(per, rows, lanes)


def holds_edge(slots, z_cells):
    return lax.axis_index("gx") * slots == z_cells // 4


def x_forward_kernel(table, twiddles, data_h, out, data, sem):
    copy = pltpu.make_async_copy(data_h, data, sem)
    copy.start()
    copy.wait()
    fields, lanes = data.shape[1], data.shape[3]
    for residue, spectrum in enumerate(x_forward(data, table, twiddles)):
        for f in range(fields):
            out[residue, f] = spectrum[:, f * lanes : (f + 1) * lanes]


def x_inverse_kernel(z_cells, table, twiddles, data_h, out, data, sem):
    copy = pltpu.make_async_copy(data_h, data, sem)
    copy.start()
    copy.wait()
    special = holds_edge(out.shape[3] // 2, z_cells)
    x_inverse(lambda residue: data[residue], table, twiddles, special, out)


def green_kernel(x_cells, z_cells, chunks, moduli, mean, table, twiddles, done, data, out, rest_h, own, new, rest_out, sem):
    rest_chunk, own_chunk = chunks
    lanes = data.shape[3]
    slots = lanes // 2
    quarter = x_cells // 4
    place, mine = lax.axis_index("gz"), lax.axis_index("gx")
    inplane = functools.reduce(jnp.logical_or, [place == k for k in INPLANE])
    lame_ref = 0.5 * (moduli[0] + moduli[2])
    shear_ref = 0.5 * (moduli[1] + moduli[3])
    half_inverse = 0.5 / shear_ref
    coupling = (lame_ref + shear_ref) / (shear_ref * (lame_ref + 2.0 * shear_ref))
    c1 = jnp.where(inplane, coupling, 0.0)
    k1 = jnp.where(inplane, 2.0 * half_inverse, half_inverse)
    k2 = jnp.where(inplane, half_inverse, 0.0)
    ka = jnp.where(inplane, 0.0, half_inverse)
    total = float(x_cells * z_cells)
    means = (
        total * jnp.where(inplane, mean[XX], mean[XY]),
        total * jnp.where(inplane, mean[ZZ], mean[YZ]),
        total * mean[XZ],
    )

    for residue, spectrum in enumerate(x_forward(data, table, twiddles)):
        for slot in range(len(own_chunk)):
            own[residue, slot] = spectrum[:, slot * lanes : (slot + 1) * lanes]

    def load(field, residue, rows):
        if field in own_chunk:
            return own[residue, own_chunk.index(field), rows, :]
        return done[residue, rest_chunk.index(field), rows, :]

    def store(chunk, residue, rows, block, value):
        columns = slice(block * lanes, (block + 1) * lanes)
        if chunk is own_chunk:
            new[residue, rows, columns] = value
        else:
            rest_out[residue, rows, columns] = value

    def green(kx, kz, odd_kx, s):
        radius = kx * kx + kz * kz
        inverse = 1.0 / jnp.where(radius == 0.0, 1.0, radius)
        a, b = kx * kx * inverse, kz * kz * inverse
        d = odd_kx * kz * inverse
        ab = c1 * (a * b)
        ca, cb = c1 * a, c1 * b
        h02, h12 = d * (ca - k2), d * (cb - k2)
        m01 = ab - ka * d
        twice = 2.0 * s[2]
        return (
            a * (ca - k1) * s[0] + m01 * s[1] + h02 * twice,
            m01 * s[0] + b * (cb - k1) * s[1] + h12 * twice,
            h02 * s[0] + h12 * s[1] + (2.0 * ab - k2) * s[2],
        )

    lane = lax.broadcasted_iota(jnp.int32, (1, lanes), 1)
    slot_of = lane % slots
    order = mine * slots + slot_of
    zeros_at, twos_at = z_cells // 4, z_cells // 4 + z_cells // 8
    kz = jnp.where(
        order < zeros_at,
        4 * order + 1,
        jnp.where(order < twos_at, 4 * (order - zeros_at), 4 * (order - twos_at) + 2),
    )
    kz = jnp.where(kz < z_cells // 2, kz, kz - z_cells).astype(F32)
    special = order == zeros_at
    size = 32
    for start in range(0, quarter, size):
        rows = pl.ds(start, size)
        row = lax.broadcasted_iota(jnp.int32, (size, lanes), 0) + start
        full_kz = jnp.broadcast_to(kz, (size, lanes))
        edge = [None] * FIELDS
        for residue in range(4):
            s = [load(f, residue, rows) for f in range(FIELDS)]
            for f in range(FIELDS):
                moved = s[f] if residue == 0 else pltpu.roll(s[f], residue, 1)
                edge[f] = moved if residue == 0 else jnp.where(slot_of == residue, moved, edge[f])
            count = 4 * row + residue
            kx = jnp.where(count < x_cells // 2, count, count - x_cells).astype(F32)
            odd_kx = jnp.where(count == x_cells // 2, 0.0, kx) if residue == 0 else kx
            fresh = list(green(kx, full_kz, odd_kx, s))
            if residue == 0 and start == 0:
                anchor = jnp.logical_and(row == 0, special)
                for f in range(FIELDS):
                    fresh[f] = jnp.where(anchor, jnp.where(lane < slots, means[f], 0.0), fresh[f])
            for chunk in chunks:
                for block, f in enumerate(chunk):
                    store(chunk, residue, rows, block, fresh[f])
        count = 4 * row + slot_of
        kx = jnp.where(count < x_cells // 2, count, count - x_cells).astype(F32)
        odd_kx = jnp.where(count == x_cells // 2, kx, 0.0)
        fresh = green(kx, jnp.full((size, lanes), -0.5 * z_cells, F32), odd_kx, edge)
        for residue in range(4):
            for chunk in chunks:
                extra = None
                for block, f in enumerate(chunk):
                    shift = (block - residue) % lanes
                    moved = fresh[f] if shift == 0 else pltpu.roll(fresh[f], shift, 1)
                    extra = moved if block == 0 else jnp.where(slot_of == block, moved, extra)
                store(chunk, residue, rows, len(chunk), extra)
    copy = pltpu.make_async_copy(rest_out, rest_h, sem)
    copy.start()
    x_inverse(lambda residue: new[residue], table, twiddles, holds_edge(slots, z_cells), out)
    copy.wait()


def z_inverse_kernel(table, data, *rest):
    outs, held = rest[:-1], rest[-1]
    parts = len(GROUPS)
    place = lax.axis_index("gz")
    sources, fields, rows, lanes = data.shape
    half = sources // 2
    fourth = sources // 4

    def columns(begin, end):
        return jnp.concatenate([data[k].reshape(fields * rows, lanes) for k in range(begin, end)], 1)

    first = dot_right(columns(0, half), table, 0)
    zero = dot_right(columns(half, half + fourth), table, 1)
    two = dot_right(columns(half + fourth, sources), table, 2)
    width = zero.shape[1]
    real, imag = first[:, :width], first[:, width:]
    plus, minus = zero + two, zero - two
    for k, value in enumerate((plus + real, minus - imag, plus - real, minus + imag)):
        held[k] = value.reshape(fields, rows, width)
    for step in range(parts):
        target = lax.rem(place + step, parts)
        for slot in range(fields):
            outs[slot * parts + step][...] = held[target, slot]


def stress_kernel(moduli, mean, labels, normals, *rest):
    parts = len(GROUPS)
    arrived, (strain_to, stress_to, held, strain_out, stress_out, sems) = rest[:-6], rest[-6:]
    place = lax.axis_index("gz")
    sections, cells_x, cells_z = labels.shape
    size = cells_x // normals.shape[1]
    for step in range(parts):
        source = lax.rem(place + parts - step, parts)
        for slot in range(FIELDS):
            held[source, slot] = arrived[slot * parts + step][...]
    copies = []
    for section in range(sections):
        squares = tilt(normals, section, cells_z)
        for block in range(cells_x // size):
            rows = pl.ds(block * size, size)
            local = {YY: jnp.full((size, cells_z), mean[YY], F32)}
            for group, fields in enumerate(GROUPS):
                for slot, (component, of) in enumerate(fields):
                    if of == section:
                        local[component] = held[group, slot, rows, :]
            value = law(
                local,
                labels[section, rows, :],
                row_of(squares, block, size),
                (moduli[0], moduli[2]),
                (moduli[1], moduli[3]),
                moduli[4],
            )
            for component in range(6):
                strain_out[component, section, rows, :] = local[component]
                stress_out[component, section, rows, :] = value[component]
        for k, (here, there) in enumerate(((strain_out, strain_to), (stress_out, stress_to))):
            copy = pltpu.make_async_copy(here.at[:, section], there.at[:, section], sems.at[2 * section + k])
            copy.start()
            copies.append(copy)
    for copy in copies:
        copy.wait()


def call(kernel, outs, scratch, args, limit, hbm=(), smem=0, hbm_out=()):
    def space(k):
        return pltpu.HBM if k in hbm else pltpu.SMEM if k < smem else pltpu.VMEM

    args = [pltpu.with_memory_space_constraint(a, pltpu.HBM) if k in hbm else a for k, a in enumerate(args)]
    moved = sum(a.size * a.dtype.itemsize for a in args) + sum(math.prod(o) * 4 for o in outs)
    return pl.pallas_call(
        kernel,
        out_shape=[
            pltpu.HBM(o, F32) if k in hbm_out else jax.ShapeDtypeStruct(o, F32) for k, o in enumerate(outs)
        ],
        in_specs=[pl.BlockSpec(memory_space=space(k)) for k in range(len(args))],
        out_specs=[
            pl.BlockSpec(memory_space=pltpu.HBM if k in hbm_out else pltpu.VMEM) for k in range(len(outs))
        ],
        scratch_shapes=scratch,
        compiler_params=pltpu.CompilerParams(vmem_limit_bytes=limit * MIB),
        cost_estimate=pl.CostEstimate(flops=0, bytes_accessed=moved, transcendentals=0),
    )(*args)


def shards(strain, labels, normals, moduli, mean_strain):
    parts = lax.axis_size("gz")
    x_devices = lax.axis_size("gx")
    _, sections, cells_x, cells_z = strain.shape
    x_total, z_total = cells_x * x_devices, cells_z * parts
    slots = z_total // 2 // x_devices
    lanes = 2 * slots
    z_fwd, z_inv = z_tables(z_total, slots, 1.0 / (x_total * z_total))
    x_tab = x_tables(x_total)
    block = (cells_x, cells_z)
    everyone = range(parts)

    def travel(field, blocks, gather):
        ends = INPLANE if field == 2 else everyone
        moved = [blocks[0]]
        for step in range(1, parts):
            way = [(k, (k + step) % parts) for k in range(parts)]
            way = [(a, b) for a, b in way if (b if gather else a) in ends]
            moved.append(lax.ppermute(blocks[step], "gz", way))
        return moved

    def held(fields):
        return pltpu.VMEM((parts, fields, cells_x, cells_z), F32)

    blocks = call(
        polarize_kernel,
        [block] * (FIELDS * parts),
        [
            held(FIELDS),
            pltpu.VMEM(strain.shape, F32),
            pltpu.VMEM(labels.shape, jnp.int32),
            pltpu.VMEM(normals.shape, jnp.int32),
            pltpu.SMEM(moduli.shape, F32),
            pltpu.SemaphoreType.DMA((2 + 2 * sections,)),
        ],
        (moduli, strain, labels, normals),
        16,
        range(4),
    )
    blocks = {f: list(blocks[f * parts : (f + 1) * parts]) for f in range(FIELDS)}
    rows, spectrum = [], None
    quarter = x_total // 4
    for chunk in CHUNKS:
        args = [a for f in chunk for a in travel(f, blocks.pop(f), True)]
        args, blocks, rows = lax.optimization_barrier((args, blocks, rows))
        grid = (x_devices, len(chunk), cells_x, lanes)
        scratch, hbm = [held(len(chunk))], ()
        if rows:
            scratch.append(pltpu.SemaphoreType.DMA((len(args),)))
            hbm = range(1, 1 + len(args))
        (piece,) = call(z_forward_kernel, [grid], scratch, (z_fwd, *args), 24, hbm)
        rows.append(lax.all_to_all(piece, "gx", 0, 0, tiled=True))
    size = len(CHUNKS[0])
    copied = [pltpu.VMEM(rows[0].shape, F32), pltpu.SemaphoreType.DMA]
    (spectrum,) = call(x_forward_kernel, [(4, size, quarter, lanes)], copied, (*x_tab, rows[0]), 24, (2,))
    last, rest = call(
        functools.partial(green_kernel, x_total, z_total, CHUNKS),
        [rows[1].shape, (4, quarter, (size + 1) * lanes)],
        [
            pltpu.VMEM((4, len(CHUNKS[1]), quarter, lanes), F32),
            pltpu.VMEM((4, quarter, (len(CHUNKS[1]) + 1) * lanes), F32),
            pltpu.VMEM((4, quarter, (size + 1) * lanes), F32),
            pltpu.SemaphoreType.DMA,
        ],
        (moduli, mean_strain, *x_tab, spectrum, rows[1]),
        32,
        smem=2,
        hbm_out=(1,),
    )

    def to_z(chunk, piece):
        size = len(chunk)
        blocks = call(z_inverse_kernel, [block] * (size * parts), [held(size)], (z_inv, piece), 24)
        return list(blocks)

    def from_groups(chunk, blocks):
        for slot, f in enumerate(chunk):
            arrived[f] = travel(f, blocks[slot * parts : (slot + 1) * parts], False)

    arrived = {}
    last = lax.all_to_all(last, "gx", 0, 0, tiled=True)
    copied = [pltpu.VMEM(rest.shape, F32), pltpu.SemaphoreType.DMA]
    (rest,) = call(functools.partial(x_inverse_kernel, z_total), [rows[0].shape], copied, (*x_tab, rest), 24, (2,))
    blocks = to_z(CHUNKS[1], last)
    rest, blocks = lax.optimization_barrier((rest, blocks))
    rest = lax.all_to_all(rest, "gx", 0, 0, tiled=True)
    from_groups(CHUNKS[1], blocks)
    from_groups(CHUNKS[0], to_z(CHUNKS[0], rest))
    full = (6, sections, cells_x, cells_z)
    args = [a for f in range(FIELDS) for a in arrived[f]]
    return tuple(
        call(
            stress_kernel,
            [full, full],
            [held(FIELDS), pltpu.VMEM(full, F32), pltpu.VMEM(full, F32), pltpu.SemaphoreType.DMA((2 * sections,))],
            (moduli, mean_strain, labels, normals, *args),
            24,
            smem=2,
            hbm_out=(0, 1),
        )
    )


def orientation(normals, blk):
    tilt_angle = math.pi / ANGLES * normals.astype(jnp.float32)
    tilt_angle = jnp.repeat(jnp.repeat(tilt_angle, blk, axis=1), blk, axis=2)
    return (jnp.cos(tilt_angle), jnp.sin(tilt_angle))


def stress_law(strain_field, labels, cosine_tilt, sine_tilt, moduli):
    laminate = labels == 1
    lame_local = jnp.where(laminate, moduli[2], moduli[0])
    shear_local = jnp.where(laminate, moduli[3], moduli[1])
    trace_sum = strain_field[0] + strain_field[1] + strain_field[2]
    normal_part = (
        cosine_tilt * cosine_tilt * strain_field[0]
        + sine_tilt * sine_tilt * strain_field[2]
        + 2.0 * cosine_tilt * sine_tilt * strain_field[4]
    )
    laminate_term = moduli[4] * labels.astype(jnp.float32) * normal_part
    dyad = [
        cosine_tilt * cosine_tilt,
        None,
        sine_tilt * sine_tilt,
        None,
        cosine_tilt * sine_tilt,
        None,
    ]
    result = []
    for slot in range(6):
        value = 2.0 * shear_local * strain_field[slot]
        if slot < 3:
            value = value + lame_local * trace_sum
        if dyad[slot] is not None:
            value = value + laminate_term * dyad[slot]
        result.append(value)
    return jnp.stack(result)


def polarize(stresses, strain_field, lame_ref, shear_ref):
    trace_sum = strain_field[0] + strain_field[1] + strain_field[2]
    result = []
    for slot in range(6):
        value = stresses[slot] - 2.0 * shear_ref * strain_field[slot]
        if slot < 3:
            value = value - lame_ref * trace_sum
        result.append(value)
    return jnp.stack(result)


def green_apply(spectrum, unit_x, unit_z, lame_ref, shear_ref):
    coupling = (lame_ref + shear_ref) / (shear_ref * (lame_ref + 2.0 * shear_ref))
    traction_x = spectrum[0] * unit_x + spectrum[4] * unit_z
    traction_y = spectrum[5] * unit_x + spectrum[3] * unit_z
    traction_z = spectrum[4] * unit_x + spectrum[2] * unit_z
    normal_load = unit_x * traction_x + unit_z * traction_z
    half_inverse = 0.5 / shear_ref
    result = [
        2.0 * half_inverse * unit_x * traction_x - coupling * normal_load * unit_x * unit_x,
        jnp.zeros_like(traction_x),
        2.0 * half_inverse * unit_z * traction_z - coupling * normal_load * unit_z * unit_z,
        half_inverse * unit_z * traction_y,
        half_inverse * (unit_z * traction_x + unit_x * traction_z)
        - coupling * normal_load * unit_x * unit_z,
        half_inverse * unit_x * traction_y,
    ]
    return -jnp.stack(result)


def phases(left_ids, right_ids, length):
    product = left_ids[:, None] * right_ids[None, :] % length
    phase_angle = 2.0 * math.pi / length * product.astype(jnp.float32)
    return (jnp.cos(phase_angle), jnp.sin(phase_angle))


def contract(form, left_side, right_side):
    return jnp.einsum(
        form,
        left_side,
        right_side,
        precision=lax.Precision.HIGHEST,
        preferred_element_type=jnp.float32,
    )


def signed_value(counter, length):
    return jnp.where(counter < length // 2, counter, counter - length).astype(jnp.float32)


def shards_general(strain, labels, normals, moduli, mean_strain):
    z_devices = lax.axis_size("gz")
    x_devices = lax.axis_size("gx")
    z_index = lax.axis_index("gz")
    x_index = lax.axis_index("gx")
    sections = strain.shape[1]
    cells_x = strain.shape[2]
    cells_z = strain.shape[3]
    x_total = cells_x * x_devices
    z_total = cells_z * z_devices
    line_count = sections * cells_x
    kz_share = cells_z // x_devices
    cosine_tilt, sine_tilt = orientation(normals, strain.shape[2] // normals.shape[1])
    lame_ref = 0.5 * (moduli[0] + moduli[2])
    shear_ref = 0.5 * (moduli[1] + moduli[3])
    stresses = stress_law(strain, labels, cosine_tilt, sine_tilt, moduli)
    polarized = polarize(stresses, strain, lame_ref, shear_ref)
    flattened = polarized.reshape(6, line_count, cells_z)
    own_block = z_index * cells_z + jnp.arange(cells_z, dtype=jnp.int32)
    empty_sum = jnp.zeros((6, cells_z, line_count), jnp.float32)
    pieces = lax.all_gather(flattened, "gz", axis=2, tiled=True)
    z_ids = jnp.arange(pieces.shape[2], dtype=jnp.int32)
    cos_table, sin_table = phases(z_ids, own_block, z_total)
    real_part = contract("cmz,zk->ckm", pieces, cos_table)
    imag_part = (empty_sum, empty_sum)[1] - contract("cmz,zk->ckm", pieces, sin_table)
    real_rows, imag_rows = (
        lax.all_to_all(real_part, "gx", split_axis=1, concat_axis=2, tiled=True),
        lax.all_to_all(imag_part, "gx", split_axis=1, concat_axis=2, tiled=True),
    )
    grid_shape = (6, kz_share, x_devices, sections, cells_x)
    real_rows = real_rows.reshape(grid_shape)
    imag_rows = imag_rows.reshape(grid_shape)
    every_x = jnp.arange(x_total, dtype=jnp.int32)
    cos_x, sin_x = phases(every_x, every_x, x_total)
    cos_x = cos_x.reshape(x_devices, cells_x, x_total)
    sin_x = sin_x.reshape(x_devices, cells_x, x_total)
    spec_real = contract("ckgsx,gxq->cksq", real_rows, cos_x) + contract(
        "ckgsx,gxq->cksq", imag_rows, sin_x
    )
    spec_imag = contract("ckgsx,gxq->cksq", imag_rows, cos_x) - contract(
        "ckgsx,gxq->cksq", real_rows, sin_x
    )
    kz_ids = z_index * cells_z + x_index * kz_share + jnp.arange(kz_share, dtype=jnp.int32)
    freq_z = signed_value(kz_ids, z_total)[:, None, None]
    freq_x = signed_value(every_x, x_total)[None, None, :]
    radius_sq = freq_x * freq_x + freq_z * freq_z
    at_anchor = radius_sq == 0.0
    safe_radius = jnp.sqrt(jnp.where(at_anchor, 1.0, radius_sq))
    unit_x = freq_x / safe_radius
    unit_z = freq_z / safe_radius
    anchor_term = jnp.where(at_anchor, float(x_total * z_total), 0.0)
    new_real = green_apply(spec_real, unit_x, unit_z, lame_ref, shear_ref)
    new_real = new_real + mean_strain[:, None, None, None] * anchor_term[None]
    new_imag = green_apply(spec_imag, unit_x, unit_z, lame_ref, shear_ref)
    back_real = contract("cksq,gxq->ckgsx", new_real, cos_x) - contract(
        "cksq,gxq->ckgsx", new_imag, sin_x
    )
    back_imag = contract("cksq,gxq->ckgsx", new_real, sin_x) + contract(
        "cksq,gxq->ckgsx", new_imag, cos_x
    )
    back_real = back_real.reshape(6, kz_share, x_devices * line_count)
    back_imag = back_imag.reshape(6, kz_share, x_devices * line_count)
    real_part, imag_part = (
        lax.all_to_all(back_real, "gx", split_axis=2, concat_axis=1, tiled=True),
        lax.all_to_all(back_imag, "gx", split_axis=2, concat_axis=1, tiled=True),
    )
    z_ids = jnp.arange(lax.axis_size("gz") * cells_z, dtype=jnp.int32)
    cos_table, sin_table = phases(own_block, z_ids, z_total)
    summed = lax.psum_scatter(
        contract("ckm,kz->zcm", real_part, cos_table)
        - contract("ckm,kz->zcm", imag_part, sin_table),
        "gz",
        scatter_dimension=0,
        tiled=True,
    )
    field_lines = jnp.transpose(summed, (1, 2, 0))
    strain_next = (field_lines * (1.0 / (x_total * z_total))).reshape(6, sections, cells_x, cells_z)
    stress_next = stress_law(strain_next, labels, cosine_tilt, sine_tilt, moduli)
    return (strain_next, stress_next)


def solution(mesh):
    in_specs = (P(None, None, "gx", "gz"), P(None, "gx", "gz"), P(None, "gx", "gz"), P(), P())
    out_specs = (P(None, None, "gx", "gz"), P(None, None, "gx", "gz"))

    def run(strain, labels, normals, moduli, mean_strain):
        _, sections, x_total, z_total = strain.shape
        parts, x_devices = mesh.shape["gz"], mesh.shape["gx"]
        grouped = (
            sections == 2
            and parts == len(GROUPS)
            and x_devices % 8 == 0
            and z_total == 128 * x_devices
            and x_total % (128 * x_devices) == 0
        )
        body = shards if grouped else shards_general
        mapped = jax.shard_map(body, mesh=mesh, in_specs=in_specs, out_specs=out_specs, check_vma=False)
        return mapped(strain, labels, normals, moduli, mean_strain)

    return run
```

```python
import functools
import math

import jax
import jax.numpy as jnp
import numpy as np
from jax import lax
from jax.experimental import pallas as pl
from jax.experimental.pallas import tpu as pltpu
from jax.sharding import PartitionSpec as P

ANGLES = 8
XX, YY, ZZ, YZ, XZ, XY = range(6)
GROUPS = (
    ((XY, 0), (YZ, 0)),
    ((XX, 0), (ZZ, 0), (XZ, 0)),
    ((XX, 1), (ZZ, 1), (XZ, 1)),
    ((XY, 1), (YZ, 1)),
)
INPLANE = (1, 2)
FIELDS = 3
CHUNKS = ((0, 2), (1,))
F32, BF16 = jnp.float32, jnp.bfloat16
MIB = 1 << 20


def split_table(table):
    table = np.asarray(table, np.float32)
    high = table.astype(jnp.bfloat16)
    low = (table - high.astype(np.float32)).astype(jnp.bfloat16)
    return jnp.asarray(np.stack([high, low]))


def half_frequencies(length):
    quarter = length // 4
    return (
        4 * np.arange(quarter) + 1,
        4 * np.arange(quarter // 2),
        4 * np.arange(quarter // 2) + 2,
    )


def interleave(real, imag, slots):
    rows, count = real.shape
    both = np.stack([real.reshape(rows, -1, slots), imag.reshape(rows, -1, slots)], 2)
    return both.reshape(rows, 2 * count)


def z_tables(length, slots, scale):
    quarter = length // 4
    z = np.arange(quarter, dtype=np.int64)[:, None]
    ones, zeros, twos = half_frequencies(length)

    def angles(freqs):
        return 2.0 * math.pi / length * ((z * freqs[None, :]) % length)

    one, zero, two = angles(ones), angles(zeros), angles(twos)
    top = interleave(np.cos(one), -np.sin(one), slots)
    bottom = interleave(-np.sin(one), -np.cos(one), slots)
    forward_one = np.concatenate([top, bottom], 0)
    real, imag = np.cos(zero), -np.sin(zero)
    imag[:, 0] = np.where(np.arange(quarter) % 2 == 0, 1.0, -1.0)
    forward_zero = interleave(real, imag, slots)
    forward_two = interleave(np.cos(two), -np.sin(two), slots)
    weight = 2.0 * scale
    inverse_one = weight * np.concatenate(
        [interleave(np.cos(one), -np.sin(one), slots), interleave(np.sin(one), np.cos(one), slots)], 0
    ).T
    half = np.full(quarter // 2, weight)
    half[0] = scale
    inverse_zero = interleave(real * half, imag * half, slots).T
    inverse_two = weight * forward_two.T

    def pack(first, second, third):
        return split_table(np.concatenate([first, np.concatenate([second, third], 1)], 0))

    return pack(forward_one, forward_zero, forward_two), pack(inverse_one, inverse_zero, inverse_two)


def x_tables(length):
    quarter = length // 4
    k = np.arange(quarter, dtype=np.int64)
    angle = 2.0 * math.pi / quarter * ((k[:, None] * k[None, :]) % quarter)
    turn = 2.0 * math.pi / length * k
    columns = [f(residue * turn) for residue in (1, 2, 3) for f in (np.cos, np.sin)]
    twiddles = jnp.asarray(np.stack(columns + columns[:2], 1).astype(np.float32))
    return split_table(np.concatenate([np.cos(angle), np.sin(angle)], 0)), twiddles


def halves(value):
    high = value.astype(BF16)
    return high, (value - high.astype(F32)).astype(BF16)


def dot(left, right):
    return jnp.dot(left, right, preferred_element_type=F32)


def dot_right(value, table, part):
    big = table.shape[2]
    half = big // 2
    rows = slice(0, big) if part == 0 else slice(big, big + half)
    columns = slice(0, big) if part == 0 else slice((part - 1) * half, part * half)
    high_table, low_table = table[0, rows, columns], table[1, rows, columns]
    high, low = halves(value)
    return dot(high, high_table) + (dot(low, high_table) + dot(high, low_table))


def dot_left(table, value):
    high, low = halves(value)
    return dot(table[0], high) + (dot(table[0], low) + dot(table[1], high))


def tilt(normals, section, cells_z):
    blocks = normals[section].astype(F32)
    count = blocks.shape[1]
    size = cells_z // count
    owner = lax.broadcasted_iota(jnp.int32, (count, cells_z), 1) // size
    own = lax.broadcasted_iota(jnp.int32, (count, cells_z), 0)
    spread = jnp.where(owner == own, 1.0, 0.0).astype(F32)
    angle = (math.pi / ANGLES) * dot(blocks, spread)
    cosine, sine = jnp.cos(angle), jnp.sin(angle)
    return cosine * cosine, sine * sine, cosine * sine


def law(strain, label, squares, lame, shear, stiff):
    cc, ss, cs = squares
    laminate = label == 1
    lame_local = jnp.where(laminate, lame[1], lame[0])
    twice_shear = jnp.where(laminate, 2.0 * shear[1], 2.0 * shear[0])
    spherical = lame_local * (strain[XX] + strain[YY] + strain[ZZ])
    normal = cc * strain[XX] + ss * strain[ZZ] + 2.0 * cs * strain[XZ]
    normal = jnp.where(laminate, stiff, 0.0) * normal
    return {
        XX: twice_shear * strain[XX] + spherical + normal * cc,
        YY: twice_shear * strain[YY] + spherical,
        ZZ: twice_shear * strain[ZZ] + spherical + normal * ss,
        YZ: twice_shear * strain[YZ],
        XZ: twice_shear * strain[XZ] + normal * cs,
        XY: twice_shear * strain[XY],
    }


def row_of(squares, block, size):
    return [jnp.broadcast_to(s[block : block + 1], (size, s.shape[1])) for s in squares]


def polarize_kernel(moduli_h, strain_h, labels_h, normals_h, *rest):
    outs, (held, strain, labels, normals, moduli, sems) = rest[:-6], rest[-6:]
    sections, cells_x, cells_z = labels.shape
    copies = [
        pltpu.make_async_copy(moduli_h, moduli, sems.at[0]),
        pltpu.make_async_copy(normals_h, normals, sems.at[1]),
    ]
    for k in range(sections):
        copies.append(pltpu.make_async_copy(labels_h.at[k], labels.at[k], sems.at[2 + 2 * k]))
        copies.append(pltpu.make_async_copy(strain_h.at[:, k], strain.at[:, k], sems.at[3 + 2 * k]))
    for copy in copies:
        copy.start()
    for copy in copies[:2]:
        copy.wait()
    parts = len(GROUPS)
    place = lax.axis_index("gz")
    size = cells_x // normals.shape[1]
    lame_ref = 0.5 * (moduli[0] + moduli[2])
    shear_ref = 0.5 * (moduli[1] + moduli[3])
    lame = (moduli[0] - lame_ref, moduli[2] - lame_ref)
    shear = (moduli[1] - shear_ref, moduli[3] - shear_ref)
    for group, fields in enumerate(GROUPS):
        if len(fields) < 3:
            held[group, 2] = jnp.zeros((cells_x, cells_z), F32)
    for section in range(sections):
        copies[2 + 2 * section].wait()
        copies[3 + 2 * section].wait()
        squares = tilt(normals, section, cells_z)
        for block in range(cells_x // size):
            rows = pl.ds(block * size, size)
            local = [strain[c, section, rows, :] for c in range(6)]
            value = law(local, labels[section, rows, :], row_of(squares, block, size), lame, shear, moduli[4])
            for group, fields in enumerate(GROUPS):
                for slot, (component, of) in enumerate(fields):
                    if of == section:
                        held[group, slot, rows, :] = value[component]
    for step in range(parts):
        target = lax.rem(place + step, parts)
        for slot in range(FIELDS):
            outs[slot * parts + step][...] = held[target, slot]


def z_forward_kernel(table, *rest):
    parts = len(GROUPS)
    arrived, (out, held) = rest[:-2], rest[-2:]
    place = lax.axis_index("gz")
    for step in range(parts):
        source = lax.rem(place + parts - step, parts)
        for slot in range(held.shape[1]):
            held[source, slot] = arrived[slot * parts + step][...]
    fields, rows, width = held.shape[1:]
    lanes = out.shape[3]
    z0, z1, z2, z3 = (held[k].reshape(fields * rows, width) for k in range(parts))
    first = jnp.concatenate([z0 - z2, z1 - z3], 1)
    even, odd = z0 + z2, z1 + z3
    spectra = (
        dot_right(first, table, 0),
        dot_right(even + odd, table, 1),
        dot_right(even - odd, table, 2),
    )
    target = 0
    for spectrum in spectra:
        for k in range(spectrum.shape[1] // lanes):
            out[target] = spectrum[:, k * lanes : (k + 1) * lanes].reshape(fields, rows, lanes)
            target += 1


def swap(value):
    lanes = value.shape[1]
    return jnp.concatenate([pltpu.roll(value[:, k : k + 128], 64, 1) for k in range(0, lanes, 128)], 1)


def turn_sign(width):
    lane = lax.broadcasted_iota(jnp.int32, (1, width), 1) % 128
    return jnp.where(lane < 64, 1.0, -1.0).astype(F32)


def twiddle(twiddles, residue, value, sign):
    if residue == 0:
        return value
    pick = 2 * (residue - 1)
    quarter = value.shape[0]
    cosine = jnp.broadcast_to(twiddles[:, pick : pick + 1], (quarter, 128))
    sine = jnp.broadcast_to(twiddles[:, pick + 1 : pick + 2], (quarter, 128)) * sign[:, :128]
    pieces = []
    for k in range(0, value.shape[1], 128):
        piece = value[:, k : k + 128]
        pieces.append(cosine * piece + sine * pltpu.roll(piece, 64, 1))
    return jnp.concatenate(pieces, 1)


def x_forward(data, table, twiddles):
    sources, fields, rows, lanes = data.shape
    quarter = sources * rows // 4
    per = sources // 4
    sign = turn_sign(fields * lanes)
    block = [
        jnp.concatenate([data[a * per : (a + 1) * per, f].reshape(quarter, lanes) for f in range(fields)], 1)
        for a in range(4)
    ]
    even, odd = block[0] + block[2], block[1] + block[3]
    diff, turned = block[0] - block[2], sign * swap(block[1] - block[3])
    for residue, value in enumerate((even + odd, diff + turned, even - odd, diff - turned)):
        both = dot_left(table, twiddle(twiddles, residue, value, sign))
        yield both[:quarter] + sign * swap(both[quarter:])


def x_inverse(spectra, table, twiddles, is_special, out):
    sources, fields, rows, lanes = out.shape
    quarter = sources * rows // 4
    per = sources // 4
    sign = turn_sign((fields + 1) * lanes)
    parts = []
    for residue in range(4):
        both = dot_left(table, spectra(residue))
        parts.append(twiddle(twiddles, residue, both[:quarter] - sign * swap(both[quarter:]), -sign))
    h0, h1, h2, h3 = parts
    even, odd = h0 + h2, h1 + h3
    diff, turned = h0 - h2, sign * swap(h1 - h3)
    lane = lax.broadcasted_iota(jnp.int32, (1, lanes), 1)
    edge = jnp.logical_and(is_special, lane == lanes // 2)
    for a, value in enumerate((even + odd, diff - turned, even - odd, diff + turned)):
        extra = value[:, fields * lanes :]
        for f in range(fields):
            moved = extra if f == 0 else pltpu.roll(extra, lanes - f, 1)
            final = jnp.where(edge, moved, value[:, f * lanes : (f + 1) * lanes])
            out[a * per : (a + 1) * per, f] = final.reshape(per, rows, lanes)


def holds_edge(slots, z_cells):
    return lax.axis_index("gx") * slots == z_cells // 4


def x_forward_kernel(table, twiddles, data_h, out, data, sem):
    copy = pltpu.make_async_copy(data_h, data, sem)
    copy.start()
    copy.wait()
    fields, lanes = data.shape[1], data.shape[3]
    for residue, spectrum in enumerate(x_forward(data, table, twiddles)):
        for f in range(fields):
            out[residue, f] = spectrum[:, f * lanes : (f + 1) * lanes]


def x_inverse_kernel(z_cells, table, twiddles, data_h, out, data, sem):
    copy = pltpu.make_async_copy(data_h, data, sem)
    copy.start()
    copy.wait()
    special = holds_edge(out.shape[3] // 2, z_cells)
    x_inverse(lambda residue: data[residue], table, twiddles, special, out)


def green_kernel(x_cells, z_cells, chunks, moduli, mean, table, twiddles, done, data, out, rest_h, own, new, rest_out, sem):
    rest_chunk, own_chunk = chunks
    lanes = data.shape[3]
    slots = lanes // 2
    quarter = x_cells // 4
    place, mine = lax.axis_index("gz"), lax.axis_index("gx")
    inplane = functools.reduce(jnp.logical_or, [place == k for k in INPLANE])
    lame_ref = 0.5 * (moduli[0] + moduli[2])
    shear_ref = 0.5 * (moduli[1] + moduli[3])
    half_inverse = 0.5 / shear_ref
    coupling = (lame_ref + shear_ref) / (shear_ref * (lame_ref + 2.0 * shear_ref))
    c1 = jnp.where(inplane, coupling, 0.0)
    k1 = jnp.where(inplane, 2.0 * half_inverse, half_inverse)
    k2 = jnp.where(inplane, half_inverse, 0.0)
    ka = jnp.where(inplane, 0.0, half_inverse)
    total = float(x_cells * z_cells)
    means = (
        total * jnp.where(inplane, mean[XX], mean[XY]),
        total * jnp.where(inplane, mean[ZZ], mean[YZ]),
        total * mean[XZ],
    )

    for residue, spectrum in enumerate(x_forward(data, table, twiddles)):
        for slot in range(len(own_chunk)):
            own[residue, slot] = spectrum[:, slot * lanes : (slot + 1) * lanes]

    def load(field, residue, rows):
        if field in own_chunk:
            return own[residue, own_chunk.index(field), rows, :]
        return done[residue, rest_chunk.index(field), rows, :]

    def store(chunk, residue, rows, block, value):
        columns = slice(block * lanes, (block + 1) * lanes)
        if chunk is own_chunk:
            new[residue, rows, columns] = value
        else:
            rest_out[residue, rows, columns] = value

    def green(kx, kz, odd_kx, s):
        radius = kx * kx + kz * kz
        inverse = 1.0 / jnp.where(radius == 0.0, 1.0, radius)
        a, b = kx * kx * inverse, kz * kz * inverse
        d = odd_kx * kz * inverse
        ab = c1 * (a * b)
        ca, cb = c1 * a, c1 * b
        h02, h12 = d * (ca - k2), d * (cb - k2)
        m01 = ab - ka * d
        twice = 2.0 * s[2]
        return (
            a * (ca - k1) * s[0] + m01 * s[1] + h02 * twice,
            m01 * s[0] + b * (cb - k1) * s[1] + h12 * twice,
            h02 * s[0] + h12 * s[1] + (2.0 * ab - k2) * s[2],
        )

    lane = lax.broadcasted_iota(jnp.int32, (1, lanes), 1)
    slot_of = lane % slots
    order = mine * slots + slot_of
    zeros_at, twos_at = z_cells // 4, z_cells // 4 + z_cells // 8
    kz = jnp.where(
        order < zeros_at,
        4 * order + 1,
        jnp.where(order < twos_at, 4 * (order - zeros_at), 4 * (order - twos_at) + 2),
    )
    kz = jnp.where(kz < z_cells // 2, kz, kz - z_cells).astype(F32)
    special = order == zeros_at
    size = 32
    for start in range(0, quarter, size):
        rows = pl.ds(start, size)
        row = lax.broadcasted_iota(jnp.int32, (size, lanes), 0) + start
        full_kz = jnp.broadcast_to(kz, (size, lanes))
        edge = [None] * FIELDS
        for residue in range(4):
            s = [load(f, residue, rows) for f in range(FIELDS)]
            for f in range(FIELDS):
                moved = s[f] if residue == 0 else pltpu.roll(s[f], residue, 1)
                edge[f] = moved if residue == 0 else jnp.where(slot_of == residue, moved, edge[f])
            count = 4 * row + residue
            kx = jnp.where(count < x_cells // 2, count, count - x_cells).astype(F32)
            odd_kx = jnp.where(count == x_cells // 2, 0.0, kx) if residue == 0 else kx
            fresh = list(green(kx, full_kz, odd_kx, s))
            if residue == 0 and start == 0:
                anchor = jnp.logical_and(row == 0, special)
                for f in range(FIELDS):
                    fresh[f] = jnp.where(anchor, jnp.where(lane < slots, means[f], 0.0), fresh[f])
            for chunk in chunks:
                for block, f in enumerate(chunk):
                    store(chunk, residue, rows, block, fresh[f])
        count = 4 * row + slot_of
        kx = jnp.where(count < x_cells // 2, count, count - x_cells).astype(F32)
        odd_kx = jnp.where(count == x_cells // 2, kx, 0.0)
        fresh = green(kx, jnp.full((size, lanes), -0.5 * z_cells, F32), odd_kx, edge)
        for residue in range(4):
            for chunk in chunks:
                extra = None
                for block, f in enumerate(chunk):
                    shift = (block - residue) % lanes
                    moved = fresh[f] if shift == 0 else pltpu.roll(fresh[f], shift, 1)
                    extra = moved if block == 0 else jnp.where(slot_of == block, moved, extra)
                store(chunk, residue, rows, len(chunk), extra)
    copy = pltpu.make_async_copy(rest_out, rest_h, sem)
    copy.start()
    x_inverse(lambda residue: new[residue], table, twiddles, holds_edge(slots, z_cells), out)
    copy.wait()


def z_inverse_kernel(table, data, *rest):
    outs, held = rest[:-1], rest[-1]
    parts = len(GROUPS)
    place = lax.axis_index("gz")
    sources, fields, rows, lanes = data.shape
    half = sources // 2
    fourth = sources // 4

    def columns(begin, end):
        return jnp.concatenate([data[k].reshape(fields * rows, lanes) for k in range(begin, end)], 1)

    first = dot_right(columns(0, half), table, 0)
    zero = dot_right(columns(half, half + fourth), table, 1)
    two = dot_right(columns(half + fourth, sources), table, 2)
    width = zero.shape[1]
    real, imag = first[:, :width], first[:, width:]
    plus, minus = zero + two, zero - two
    for k, value in enumerate((plus + real, minus - imag, plus - real, minus + imag)):
        held[k] = value.reshape(fields, rows, width)
    for step in range(parts):
        target = lax.rem(place + step, parts)
        for slot in range(fields):
            outs[slot * parts + step][...] = held[target, slot]


def stress_kernel(moduli, mean, labels, normals, *rest):
    parts = len(GROUPS)
    arrived, (strain_to, stress_to, held, strain_out, stress_out, sems) = rest[:-6], rest[-6:]
    place = lax.axis_index("gz")
    sections, cells_x, cells_z = labels.shape
    size = cells_x // normals.shape[1]
    for step in range(parts):
        source = lax.rem(place + parts - step, parts)
        for slot in range(FIELDS):
            held[source, slot] = arrived[slot * parts + step][...]
    copies = []
    for section in range(sections):
        squares = tilt(normals, section, cells_z)
        for block in range(cells_x // size):
            rows = pl.ds(block * size, size)
            local = {YY: jnp.full((size, cells_z), mean[YY], F32)}
            for group, fields in enumerate(GROUPS):
                for slot, (component, of) in enumerate(fields):
                    if of == section:
                        local[component] = held[group, slot, rows, :]
            value = law(
                local,
                labels[section, rows, :],
                row_of(squares, block, size),
                (moduli[0], moduli[2]),
                (moduli[1], moduli[3]),
                moduli[4],
            )
            for component in range(6):
                strain_out[component, section, rows, :] = local[component]
                stress_out[component, section, rows, :] = value[component]
        for k, (here, there) in enumerate(((strain_out, strain_to), (stress_out, stress_to))):
            copy = pltpu.make_async_copy(here.at[:, section], there.at[:, section], sems.at[2 * section + k])
            copy.start()
            copies.append(copy)
    for copy in copies:
        copy.wait()


def call(kernel, outs, scratch, args, limit, hbm=(), smem=0, hbm_out=()):
    def space(k):
        return pltpu.HBM if k in hbm else pltpu.SMEM if k < smem else pltpu.VMEM

    args = [pltpu.with_memory_space_constraint(a, pltpu.HBM) if k in hbm else a for k, a in enumerate(args)]
    moved = sum(a.size * a.dtype.itemsize for a in args) + sum(math.prod(o) * 4 for o in outs)
    return pl.pallas_call(
        kernel,
        out_shape=[
            pltpu.HBM(o, F32) if k in hbm_out else jax.ShapeDtypeStruct(o, F32) for k, o in enumerate(outs)
        ],
        in_specs=[pl.BlockSpec(memory_space=space(k)) for k in range(len(args))],
        out_specs=[
            pl.BlockSpec(memory_space=pltpu.HBM if k in hbm_out else pltpu.VMEM) for k in range(len(outs))
        ],
        scratch_shapes=scratch,
        compiler_params=pltpu.CompilerParams(vmem_limit_bytes=limit * MIB),
        cost_estimate=pl.CostEstimate(flops=0, bytes_accessed=moved, transcendentals=0),
    )(*args)


def shards(strain, labels, normals, moduli, mean_strain):
    parts = lax.axis_size("gz")
    x_devices = lax.axis_size("gx")
    _, sections, cells_x, cells_z = strain.shape
    x_total, z_total = cells_x * x_devices, cells_z * parts
    slots = z_total // 2 // x_devices
    lanes = 2 * slots
    z_fwd, z_inv = z_tables(z_total, slots, 1.0 / (x_total * z_total))
    x_tab = x_tables(x_total)
    block = (cells_x, cells_z)
    everyone = range(parts)

    def travel(field, blocks, gather):
        ends = INPLANE if field == 2 else everyone
        moved = [blocks[0]]
        for step in range(1, parts):
            way = [(k, (k + step) % parts) for k in range(parts)]
            way = [(a, b) for a, b in way if (b if gather else a) in ends]
            moved.append(lax.ppermute(blocks[step], "gz", way))
        return moved

    def held(fields):
        return pltpu.VMEM((parts, fields, cells_x, cells_z), F32)

    blocks = call(
        polarize_kernel,
        [block] * (FIELDS * parts),
        [
            held(FIELDS),
            pltpu.VMEM(strain.shape, F32),
            pltpu.VMEM(labels.shape, jnp.int32),
            pltpu.VMEM(normals.shape, jnp.int32),
            pltpu.SMEM(moduli.shape, F32),
            pltpu.SemaphoreType.DMA((2 + 2 * sections,)),
        ],
        (moduli, strain, labels, normals),
        16,
        range(4),
    )
    blocks = {f: list(blocks[f * parts : (f + 1) * parts]) for f in range(FIELDS)}
    rows, spectrum = [], None
    quarter = x_total // 4
    for chunk in CHUNKS:
        args = [a for f in chunk for a in travel(f, blocks.pop(f), True)]
        args, blocks, rows = lax.optimization_barrier((args, blocks, rows))
        grid = (x_devices, len(chunk), cells_x, lanes)
        (piece,) = call(z_forward_kernel, [grid], [held(len(chunk))], (z_fwd, *args), 16)
        rows.append(lax.all_to_all(piece, "gx", 0, 0, tiled=True))
    size = len(CHUNKS[0])
    copied = [pltpu.VMEM(rows[0].shape, F32), pltpu.SemaphoreType.DMA]
    (spectrum,) = call(x_forward_kernel, [(4, size, quarter, lanes)], copied, (*x_tab, rows[0]), 24, (2,))
    last, rest = call(
        functools.partial(green_kernel, x_total, z_total, CHUNKS),
        [rows[1].shape, (4, quarter, (size + 1) * lanes)],
        [
            pltpu.VMEM((4, len(CHUNKS[1]), quarter, lanes), F32),
            pltpu.VMEM((4, quarter, (len(CHUNKS[1]) + 1) * lanes), F32),
            pltpu.VMEM((4, quarter, (size + 1) * lanes), F32),
            pltpu.SemaphoreType.DMA,
        ],
        (moduli, mean_strain, *x_tab, spectrum, rows[1]),
        32,
        smem=2,
        hbm_out=(1,),
    )

    def to_z(chunk, piece):
        size = len(chunk)
        blocks = call(z_inverse_kernel, [block] * (size * parts), [held(size)], (z_inv, piece), 24)
        return list(blocks)

    def from_groups(chunk, blocks):
        for slot, f in enumerate(chunk):
            arrived[f] = travel(f, blocks[slot * parts : (slot + 1) * parts], False)

    arrived = {}
    last = lax.all_to_all(last, "gx", 0, 0, tiled=True)
    copied = [pltpu.VMEM(rest.shape, F32), pltpu.SemaphoreType.DMA]
    (rest,) = call(functools.partial(x_inverse_kernel, z_total), [rows[0].shape], copied, (*x_tab, rest), 24, (2,))
    blocks = to_z(CHUNKS[1], last)
    rest, blocks = lax.optimization_barrier((rest, blocks))
    rest = lax.all_to_all(rest, "gx", 0, 0, tiled=True)
    from_groups(CHUNKS[1], blocks)
    from_groups(CHUNKS[0], to_z(CHUNKS[0], rest))
    full = (6, sections, cells_x, cells_z)
    args = [a for f in range(FIELDS) for a in arrived[f]]
    return tuple(
        call(
            stress_kernel,
            [full, full],
            [held(FIELDS), pltpu.VMEM(full, F32), pltpu.VMEM(full, F32), pltpu.SemaphoreType.DMA((2 * sections,))],
            (moduli, mean_strain, labels, normals, *args),
            24,
            smem=2,
            hbm_out=(0, 1),
        )
    )


def orientation(normals, blk):
    tilt_angle = math.pi / ANGLES * normals.astype(jnp.float32)
    tilt_angle = jnp.repeat(jnp.repeat(tilt_angle, blk, axis=1), blk, axis=2)
    return (jnp.cos(tilt_angle), jnp.sin(tilt_angle))


def stress_law(strain_field, labels, cosine_tilt, sine_tilt, moduli):
    laminate = labels == 1
    lame_local = jnp.where(laminate, moduli[2], moduli[0])
    shear_local = jnp.where(laminate, moduli[3], moduli[1])
    trace_sum = strain_field[0] + strain_field[1] + strain_field[2]
    normal_part = (
        cosine_tilt * cosine_tilt * strain_field[0]
        + sine_tilt * sine_tilt * strain_field[2]
        + 2.0 * cosine_tilt * sine_tilt * strain_field[4]
    )
    laminate_term = moduli[4] * labels.astype(jnp.float32) * normal_part
    dyad = [
        cosine_tilt * cosine_tilt,
        None,
        sine_tilt * sine_tilt,
        None,
        cosine_tilt * sine_tilt,
        None,
    ]
    result = []
    for slot in range(6):
        value = 2.0 * shear_local * strain_field[slot]
        if slot < 3:
            value = value + lame_local * trace_sum
        if dyad[slot] is not None:
            value = value + laminate_term * dyad[slot]
        result.append(value)
    return jnp.stack(result)


def polarize(stresses, strain_field, lame_ref, shear_ref):
    trace_sum = strain_field[0] + strain_field[1] + strain_field[2]
    result = []
    for slot in range(6):
        value = stresses[slot] - 2.0 * shear_ref * strain_field[slot]
        if slot < 3:
            value = value - lame_ref * trace_sum
        result.append(value)
    return jnp.stack(result)


def green_apply(spectrum, unit_x, unit_z, lame_ref, shear_ref):
    coupling = (lame_ref + shear_ref) / (shear_ref * (lame_ref + 2.0 * shear_ref))
    traction_x = spectrum[0] * unit_x + spectrum[4] * unit_z
    traction_y = spectrum[5] * unit_x + spectrum[3] * unit_z
    traction_z = spectrum[4] * unit_x + spectrum[2] * unit_z
    normal_load = unit_x * traction_x + unit_z * traction_z
    half_inverse = 0.5 / shear_ref
    result = [
        2.0 * half_inverse * unit_x * traction_x - coupling * normal_load * unit_x * unit_x,
        jnp.zeros_like(traction_x),
        2.0 * half_inverse * unit_z * traction_z - coupling * normal_load * unit_z * unit_z,
        half_inverse * unit_z * traction_y,
        half_inverse * (unit_z * traction_x + unit_x * traction_z)
        - coupling * normal_load * unit_x * unit_z,
        half_inverse * unit_x * traction_y,
    ]
    return -jnp.stack(result)


def phases(left_ids, right_ids, length):
    product = left_ids[:, None] * right_ids[None, :] % length
    phase_angle = 2.0 * math.pi / length * product.astype(jnp.float32)
    return (jnp.cos(phase_angle), jnp.sin(phase_angle))


def contract(form, left_side, right_side):
    return jnp.einsum(
        form,
        left_side,
        right_side,
        precision=lax.Precision.HIGHEST,
        preferred_element_type=jnp.float32,
    )


def signed_value(counter, length):
    return jnp.where(counter < length // 2, counter, counter - length).astype(jnp.float32)


def shards_general(strain, labels, normals, moduli, mean_strain):
    z_devices = lax.axis_size("gz")
    x_devices = lax.axis_size("gx")
    z_index = lax.axis_index("gz")
    x_index = lax.axis_index("gx")
    sections = strain.shape[1]
    cells_x = strain.shape[2]
    cells_z = strain.shape[3]
    x_total = cells_x * x_devices
    z_total = cells_z * z_devices
    line_count = sections * cells_x
    kz_share = cells_z // x_devices
    cosine_tilt, sine_tilt = orientation(normals, strain.shape[2] // normals.shape[1])
    lame_ref = 0.5 * (moduli[0] + moduli[2])
    shear_ref = 0.5 * (moduli[1] + moduli[3])
    stresses = stress_law(strain, labels, cosine_tilt, sine_tilt, moduli)
    polarized = polarize(stresses, strain, lame_ref, shear_ref)
    flattened = polarized.reshape(6, line_count, cells_z)
    own_block = z_index * cells_z + jnp.arange(cells_z, dtype=jnp.int32)
    empty_sum = jnp.zeros((6, cells_z, line_count), jnp.float32)
    pieces = lax.all_gather(flattened, "gz", axis=2, tiled=True)
    z_ids = jnp.arange(pieces.shape[2], dtype=jnp.int32)
    cos_table, sin_table = phases(z_ids, own_block, z_total)
    real_part = contract("cmz,zk->ckm", pieces, cos_table)
    imag_part = (empty_sum, empty_sum)[1] - contract("cmz,zk->ckm", pieces, sin_table)
    real_rows, imag_rows = (
        lax.all_to_all(real_part, "gx", split_axis=1, concat_axis=2, tiled=True),
        lax.all_to_all(imag_part, "gx", split_axis=1, concat_axis=2, tiled=True),
    )
    grid_shape = (6, kz_share, x_devices, sections, cells_x)
    real_rows = real_rows.reshape(grid_shape)
    imag_rows = imag_rows.reshape(grid_shape)
    every_x = jnp.arange(x_total, dtype=jnp.int32)
    cos_x, sin_x = phases(every_x, every_x, x_total)
    cos_x = cos_x.reshape(x_devices, cells_x, x_total)
    sin_x = sin_x.reshape(x_devices, cells_x, x_total)
    spec_real = contract("ckgsx,gxq->cksq", real_rows, cos_x) + contract(
        "ckgsx,gxq->cksq", imag_rows, sin_x
    )
    spec_imag = contract("ckgsx,gxq->cksq", imag_rows, cos_x) - contract(
        "ckgsx,gxq->cksq", real_rows, sin_x
    )
    kz_ids = z_index * cells_z + x_index * kz_share + jnp.arange(kz_share, dtype=jnp.int32)
    freq_z = signed_value(kz_ids, z_total)[:, None, None]
    freq_x = signed_value(every_x, x_total)[None, None, :]
    radius_sq = freq_x * freq_x + freq_z * freq_z
    at_anchor = radius_sq == 0.0
    safe_radius = jnp.sqrt(jnp.where(at_anchor, 1.0, radius_sq))
    unit_x = freq_x / safe_radius
    unit_z = freq_z / safe_radius
    anchor_term = jnp.where(at_anchor, float(x_total * z_total), 0.0)
    new_real = green_apply(spec_real, unit_x, unit_z, lame_ref, shear_ref)
    new_real = new_real + mean_strain[:, None, None, None] * anchor_term[None]
    new_imag = green_apply(spec_imag, unit_x, unit_z, lame_ref, shear_ref)
    back_real = contract("cksq,gxq->ckgsx", new_real, cos_x) - contract(
        "cksq,gxq->ckgsx", new_imag, sin_x
    )
    back_imag = contract("cksq,gxq->ckgsx", new_real, sin_x) + contract(
        "cksq,gxq->ckgsx", new_imag, cos_x
    )
    back_real = back_real.reshape(6, kz_share, x_devices * line_count)
    back_imag = back_imag.reshape(6, kz_share, x_devices * line_count)
    real_part, imag_part = (
        lax.all_to_all(back_real, "gx", split_axis=2, concat_axis=1, tiled=True),
        lax.all_to_all(back_imag, "gx", split_axis=2, concat_axis=1, tiled=True),
    )
    z_ids = jnp.arange(lax.axis_size("gz") * cells_z, dtype=jnp.int32)
    cos_table, sin_table = phases(own_block, z_ids, z_total)
    summed = lax.psum_scatter(
        contract("ckm,kz->zcm", real_part, cos_table)
        - contract("ckm,kz->zcm", imag_part, sin_table),
        "gz",
        scatter_dimension=0,
        tiled=True,
    )
    field_lines = jnp.transpose(summed, (1, 2, 0))
    strain_next = (field_lines * (1.0 / (x_total * z_total))).reshape(6, sections, cells_x, cells_z)
    stress_next = stress_law(strain_next, labels, cosine_tilt, sine_tilt, moduli)
    return (strain_next, stress_next)


def solution(mesh):
    in_specs = (P(None, None, "gx", "gz"), P(None, "gx", "gz"), P(None, "gx", "gz"), P(), P())
    out_specs = (P(None, None, "gx", "gz"), P(None, None, "gx", "gz"))

    def run(strain, labels, normals, moduli, mean_strain):
        _, sections, x_total, z_total = strain.shape
        parts, x_devices = mesh.shape["gz"], mesh.shape["gx"]
        grouped = (
            sections == 2
            and parts == len(GROUPS)
            and x_devices % 8 == 0
            and z_total == 128 * x_devices
            and x_total % (128 * x_devices) == 0
        )
        body = shards if grouped else shards_general
        mapped = jax.shard_map(body, mesh=mesh, in_specs=in_specs, out_specs=out_specs, check_vma=False)
        return mapped(strain, labels, normals, moduli, mean_strain)

    return run
```

```python
import functools
import math

import jax
import jax.numpy as jnp
import numpy as np
from jax import lax
from jax.experimental import pallas as pl
from jax.experimental.pallas import tpu as pltpu
from jax.sharding import PartitionSpec as P

ANGLES = 8
XX, YY, ZZ, YZ, XZ, XY = range(6)
GROUPS = (
    ((XY, 0), (YZ, 0)),
    ((XX, 0), (ZZ, 0), (XZ, 0)),
    ((XX, 1), (ZZ, 1), (XZ, 1)),
    ((XY, 1), (YZ, 1)),
)
INPLANE = (1, 2)
FIELDS = 3
CHUNKS = ((0, 2), (1,))
F32, BF16 = jnp.float32, jnp.bfloat16
MIB = 1 << 20


def split_table(table):
    table = np.asarray(table, np.float32)
    high = table.astype(jnp.bfloat16)
    low = (table - high.astype(np.float32)).astype(jnp.bfloat16)
    return jnp.asarray(np.stack([high, low]))


def half_frequencies(length):
    quarter = length // 4
    return (
        4 * np.arange(quarter) + 1,
        4 * np.arange(quarter // 2),
        4 * np.arange(quarter // 2) + 2,
    )


def interleave(real, imag, slots):
    rows, count = real.shape
    both = np.stack([real.reshape(rows, -1, slots), imag.reshape(rows, -1, slots)], 2)
    return both.reshape(rows, 2 * count)


def z_tables(length, slots, scale):
    quarter = length // 4
    z = np.arange(quarter, dtype=np.int64)[:, None]
    ones, zeros, twos = half_frequencies(length)

    def angles(freqs):
        return 2.0 * math.pi / length * ((z * freqs[None, :]) % length)

    one, zero, two = angles(ones), angles(zeros), angles(twos)
    top = interleave(np.cos(one), -np.sin(one), slots)
    bottom = interleave(-np.sin(one), -np.cos(one), slots)
    forward_one = np.concatenate([top, bottom], 0)
    real, imag = np.cos(zero), -np.sin(zero)
    imag[:, 0] = np.where(np.arange(quarter) % 2 == 0, 1.0, -1.0)
    forward_zero = interleave(real, imag, slots)
    forward_two = interleave(np.cos(two), -np.sin(two), slots)
    weight = 2.0 * scale
    inverse_one = weight * np.concatenate(
        [interleave(np.cos(one), -np.sin(one), slots), interleave(np.sin(one), np.cos(one), slots)], 0
    ).T
    half = np.full(quarter // 2, weight)
    half[0] = scale
    inverse_zero = interleave(real * half, imag * half, slots).T
    inverse_two = weight * forward_two.T

    def pack(first, second, third):
        return split_table(np.concatenate([first, np.concatenate([second, third], 1)], 0))

    return pack(forward_one, forward_zero, forward_two), pack(inverse_one, inverse_zero, inverse_two)


def x_tables(length):
    quarter = length // 4
    k = np.arange(quarter, dtype=np.int64)
    angle = 2.0 * math.pi / quarter * ((k[:, None] * k[None, :]) % quarter)
    turn = 2.0 * math.pi / length * k
    columns = [f(residue * turn) for residue in (1, 2, 3) for f in (np.cos, np.sin)]
    twiddles = jnp.asarray(np.stack(columns + columns[:2], 1).astype(np.float32))
    return split_table(np.concatenate([np.cos(angle), np.sin(angle)], 0)), twiddles


def halves(value):
    high = value.astype(BF16)
    return high, (value - high.astype(F32)).astype(BF16)


def dot(left, right):
    return jnp.dot(left, right, preferred_element_type=F32)


def dot_right(value, table, part):
    big = table.shape[2]
    half = big // 2
    rows = slice(0, big) if part == 0 else slice(big, big + half)
    columns = slice(0, big) if part == 0 else slice((part - 1) * half, part * half)
    high_table, low_table = table[0, rows, columns], table[1, rows, columns]
    high, low = halves(value)
    return dot(high, high_table) + (dot(low, high_table) + dot(high, low_table))


def dot_left(table, value):
    high, low = halves(value)
    return dot(table[0], high) + (dot(table[0], low) + dot(table[1], high))


def tilt(normals, section, cells_z):
    blocks = normals[section].astype(F32)
    count = blocks.shape[1]
    size = cells_z // count
    owner = lax.broadcasted_iota(jnp.int32, (count, cells_z), 1) // size
    own = lax.broadcasted_iota(jnp.int32, (count, cells_z), 0)
    spread = jnp.where(owner == own, 1.0, 0.0).astype(F32)
    angle = (math.pi / ANGLES) * dot(blocks, spread)
    cosine, sine = jnp.cos(angle), jnp.sin(angle)
    return cosine * cosine, sine * sine, cosine * sine


def law(strain, label, squares, lame, shear, stiff):
    cc, ss, cs = squares
    laminate = label == 1
    lame_local = jnp.where(laminate, lame[1], lame[0])
    twice_shear = jnp.where(laminate, 2.0 * shear[1], 2.0 * shear[0])
    spherical = lame_local * (strain[XX] + strain[YY] + strain[ZZ])
    normal = cc * strain[XX] + ss * strain[ZZ] + 2.0 * cs * strain[XZ]
    normal = jnp.where(laminate, stiff, 0.0) * normal
    return {
        XX: twice_shear * strain[XX] + spherical + normal * cc,
        YY: twice_shear * strain[YY] + spherical,
        ZZ: twice_shear * strain[ZZ] + spherical + normal * ss,
        YZ: twice_shear * strain[YZ],
        XZ: twice_shear * strain[XZ] + normal * cs,
        XY: twice_shear * strain[XY],
    }


def row_of(squares, block, size):
    return [jnp.broadcast_to(s[block : block + 1], (size, s.shape[1])) for s in squares]


def polarize_kernel(moduli_h, strain_h, labels_h, normals_h, *rest):
    outs, (held, strain, labels, normals, moduli, sems) = rest[:-6], rest[-6:]
    sections, cells_x, cells_z = labels.shape
    copies = [
        pltpu.make_async_copy(moduli_h, moduli, sems.at[0]),
        pltpu.make_async_copy(normals_h, normals, sems.at[1]),
    ]
    for k in range(sections):
        copies.append(pltpu.make_async_copy(labels_h.at[k], labels.at[k], sems.at[2 + 2 * k]))
        copies.append(pltpu.make_async_copy(strain_h.at[:, k], strain.at[:, k], sems.at[3 + 2 * k]))
    for copy in copies:
        copy.start()
    for copy in copies[:2]:
        copy.wait()
    parts = len(GROUPS)
    place = lax.axis_index("gz")
    size = cells_x // normals.shape[1]
    lame_ref = 0.5 * (moduli[0] + moduli[2])
    shear_ref = 0.5 * (moduli[1] + moduli[3])
    lame = (moduli[0] - lame_ref, moduli[2] - lame_ref)
    shear = (moduli[1] - shear_ref, moduli[3] - shear_ref)
    for group, fields in enumerate(GROUPS):
        if len(fields) < 3:
            held[group, 2] = jnp.zeros((cells_x, cells_z), F32)
    for section in range(sections):
        copies[2 + 2 * section].wait()
        copies[3 + 2 * section].wait()
        squares = tilt(normals, section, cells_z)
        for block in range(cells_x // size):
            rows = pl.ds(block * size, size)
            local = [strain[c, section, rows, :] for c in range(6)]
            value = law(local, labels[section, rows, :], row_of(squares, block, size), lame, shear, moduli[4])
            for group, fields in enumerate(GROUPS):
                for slot, (component, of) in enumerate(fields):
                    if of == section:
                        held[group, slot, rows, :] = value[component]
    for step in range(parts):
        target = lax.rem(place + step, parts)
        for slot in range(FIELDS):
            outs[slot * parts + step][...] = held[target, slot]


def deal(blocks, own, swapped):
    mine = lax.axis_index("gx")
    chip, core = mine // 2, lax.rem(mine, 2)
    for step in range(own.shape[0]):
        there = 2 * lax.bitwise_xor(chip, step)
        own[step] = blocks[there + core, 0]
        swapped[step] = blocks[there + 1 - core, 0]


def collect(own, got, moved, blocks):
    mine = lax.axis_index("gx")
    chip, core = mine // 2, lax.rem(mine, 2)
    for step in range(own.shape[0]):
        there = 2 * lax.bitwise_xor(chip, step)
        blocks[there + core, 0] = own[0] if step == 0 else moved[step - 1][0]
        blocks[there + 1 - core, 0] = got[0] if step == 0 else moved[step - 1][1]


def merge_kernel(own, got, *outs):
    for k, out in enumerate(outs):
        out[0] = own[k + 1]
        out[1] = got[k + 1]


def z_forward_deal_kernel(table, *rest):
    arrived, (own, swapped, held, blocks) = rest[:-4], rest[-4:]
    z_forward_kernel(table, *arrived, blocks, held)
    deal(blocks, own, swapped)


def z_inverse_collect_kernel(table, own, got, *rest):
    chips = own.shape[0]
    moved, outs, (held, blocks) = rest[: chips - 1], rest[chips - 1 : -2], rest[-2:]
    collect(own, got, moved, blocks)
    z_inverse_kernel(table, blocks, *outs, held)


def z_forward_kernel(table, *rest):
    parts = len(GROUPS)
    arrived, (out, held) = rest[:-2], rest[-2:]
    place = lax.axis_index("gz")
    for step in range(parts):
        source = lax.rem(place + parts - step, parts)
        for slot in range(held.shape[1]):
            held[source, slot] = arrived[slot * parts + step][...]
    fields, rows, width = held.shape[1:]
    lanes = out.shape[3]
    z0, z1, z2, z3 = (held[k].reshape(fields * rows, width) for k in range(parts))
    first = jnp.concatenate([z0 - z2, z1 - z3], 1)
    even, odd = z0 + z2, z1 + z3
    spectra = (
        dot_right(first, table, 0),
        dot_right(even + odd, table, 1),
        dot_right(even - odd, table, 2),
    )
    target = 0
    for spectrum in spectra:
        for k in range(spectrum.shape[1] // lanes):
            out[target] = spectrum[:, k * lanes : (k + 1) * lanes].reshape(fields, rows, lanes)
            target += 1


def swap(value):
    lanes = value.shape[1]
    return jnp.concatenate([pltpu.roll(value[:, k : k + 128], 64, 1) for k in range(0, lanes, 128)], 1)


def turn_sign(width):
    lane = lax.broadcasted_iota(jnp.int32, (1, width), 1) % 128
    return jnp.where(lane < 64, 1.0, -1.0).astype(F32)


def twiddle(twiddles, residue, value, sign):
    if residue == 0:
        return value
    pick = 2 * (residue - 1)
    quarter = value.shape[0]
    cosine = jnp.broadcast_to(twiddles[:, pick : pick + 1], (quarter, 128))
    sine = jnp.broadcast_to(twiddles[:, pick + 1 : pick + 2], (quarter, 128)) * sign[:, :128]
    pieces = []
    for k in range(0, value.shape[1], 128):
        piece = value[:, k : k + 128]
        pieces.append(cosine * piece + sine * pltpu.roll(piece, 64, 1))
    return jnp.concatenate(pieces, 1)


def x_forward(data, table, twiddles):
    sources, fields, rows, lanes = data.shape
    quarter = sources * rows // 4
    per = sources // 4
    sign = turn_sign(fields * lanes)
    block = [
        jnp.concatenate([data[a * per : (a + 1) * per, f].reshape(quarter, lanes) for f in range(fields)], 1)
        for a in range(4)
    ]
    even, odd = block[0] + block[2], block[1] + block[3]
    diff, turned = block[0] - block[2], sign * swap(block[1] - block[3])
    for residue, value in enumerate((even + odd, diff + turned, even - odd, diff - turned)):
        both = dot_left(table, twiddle(twiddles, residue, value, sign))
        yield both[:quarter] + sign * swap(both[quarter:])


def x_inverse(spectra, table, twiddles, is_special, out):
    sources, fields, rows, lanes = out.shape
    quarter = sources * rows // 4
    per = sources // 4
    sign = turn_sign((fields + 1) * lanes)
    parts = []
    for residue in range(4):
        both = dot_left(table, spectra(residue))
        parts.append(twiddle(twiddles, residue, both[:quarter] - sign * swap(both[quarter:]), -sign))
    h0, h1, h2, h3 = parts
    even, odd = h0 + h2, h1 + h3
    diff, turned = h0 - h2, sign * swap(h1 - h3)
    lane = lax.broadcasted_iota(jnp.int32, (1, lanes), 1)
    edge = jnp.logical_and(is_special, lane == lanes // 2)
    for a, value in enumerate((even + odd, diff - turned, even - odd, diff + turned)):
        extra = value[:, fields * lanes :]
        for f in range(fields):
            moved = extra if f == 0 else pltpu.roll(extra, lanes - f, 1)
            final = jnp.where(edge, moved, value[:, f * lanes : (f + 1) * lanes])
            out[a * per : (a + 1) * per, f] = final.reshape(per, rows, lanes)


def holds_edge(slots, z_cells):
    return lax.axis_index("gx") * slots == z_cells // 4


def x_forward_kernel(table, twiddles, data_h, out, data, sem):
    copy = pltpu.make_async_copy(data_h, data, sem)
    copy.start()
    copy.wait()
    fields, lanes = data.shape[1], data.shape[3]
    for residue, spectrum in enumerate(x_forward(data, table, twiddles)):
        for f in range(fields):
            out[residue, f] = spectrum[:, f * lanes : (f + 1) * lanes]


def x_inverse_kernel(z_cells, table, twiddles, data_h, out, data, sem):
    copy = pltpu.make_async_copy(data_h, data, sem)
    copy.start()
    copy.wait()
    special = holds_edge(out.shape[3] // 2, z_cells)
    x_inverse(lambda residue: data[residue], table, twiddles, special, out)


def green_kernel(x_cells, z_cells, chunks, moduli, mean, table, twiddles, done, own_in, got, *rest):
    chips = own_in.shape[0]
    moved, rest = rest[: chips - 1], rest[chips - 1 :]
    own_out, swapped, rest_h, data, out, own, new, rest_out, sem = rest
    collect(own_in, got, moved, data)
    rest_chunk, own_chunk = chunks
    lanes = data.shape[3]
    slots = lanes // 2
    quarter = x_cells // 4
    place, mine = lax.axis_index("gz"), lax.axis_index("gx")
    inplane = functools.reduce(jnp.logical_or, [place == k for k in INPLANE])
    lame_ref = 0.5 * (moduli[0] + moduli[2])
    shear_ref = 0.5 * (moduli[1] + moduli[3])
    half_inverse = 0.5 / shear_ref
    coupling = (lame_ref + shear_ref) / (shear_ref * (lame_ref + 2.0 * shear_ref))
    c1 = jnp.where(inplane, coupling, 0.0)
    k1 = jnp.where(inplane, 2.0 * half_inverse, half_inverse)
    k2 = jnp.where(inplane, half_inverse, 0.0)
    ka = jnp.where(inplane, 0.0, half_inverse)
    total = float(x_cells * z_cells)
    means = (
        total * jnp.where(inplane, mean[XX], mean[XY]),
        total * jnp.where(inplane, mean[ZZ], mean[YZ]),
        total * mean[XZ],
    )

    for residue, spectrum in enumerate(x_forward(data, table, twiddles)):
        for slot in range(len(own_chunk)):
            own[residue, slot] = spectrum[:, slot * lanes : (slot + 1) * lanes]

    def load(field, residue, rows):
        if field in own_chunk:
            return own[residue, own_chunk.index(field), rows, :]
        return done[residue, rest_chunk.index(field), rows, :]

    def store(chunk, residue, rows, block, value):
        columns = slice(block * lanes, (block + 1) * lanes)
        if chunk is own_chunk:
            new[residue, rows, columns] = value
        else:
            rest_out[residue, rows, columns] = value

    def green(kx, kz, odd_kx, s):
        radius = kx * kx + kz * kz
        inverse = 1.0 / jnp.where(radius == 0.0, 1.0, radius)
        a, b = kx * kx * inverse, kz * kz * inverse
        d = odd_kx * kz * inverse
        ab = c1 * (a * b)
        ca, cb = c1 * a, c1 * b
        h02, h12 = d * (ca - k2), d * (cb - k2)
        m01 = ab - ka * d
        twice = 2.0 * s[2]
        return (
            a * (ca - k1) * s[0] + m01 * s[1] + h02 * twice,
            m01 * s[0] + b * (cb - k1) * s[1] + h12 * twice,
            h02 * s[0] + h12 * s[1] + (2.0 * ab - k2) * s[2],
        )

    lane = lax.broadcasted_iota(jnp.int32, (1, lanes), 1)
    slot_of = lane % slots
    order = mine * slots + slot_of
    zeros_at, twos_at = z_cells // 4, z_cells // 4 + z_cells // 8
    kz = jnp.where(
        order < zeros_at,
        4 * order + 1,
        jnp.where(order < twos_at, 4 * (order - zeros_at), 4 * (order - twos_at) + 2),
    )
    kz = jnp.where(kz < z_cells // 2, kz, kz - z_cells).astype(F32)
    special = order == zeros_at
    size = 32
    for start in range(0, quarter, size):
        rows = pl.ds(start, size)
        row = lax.broadcasted_iota(jnp.int32, (size, lanes), 0) + start
        full_kz = jnp.broadcast_to(kz, (size, lanes))
        edge = [None] * FIELDS
        for residue in range(4):
            s = [load(f, residue, rows) for f in range(FIELDS)]
            for f in range(FIELDS):
                moved = s[f] if residue == 0 else pltpu.roll(s[f], residue, 1)
                edge[f] = moved if residue == 0 else jnp.where(slot_of == residue, moved, edge[f])
            count = 4 * row + residue
            kx = jnp.where(count < x_cells // 2, count, count - x_cells).astype(F32)
            odd_kx = jnp.where(count == x_cells // 2, 0.0, kx) if residue == 0 else kx
            fresh = list(green(kx, full_kz, odd_kx, s))
            if residue == 0 and start == 0:
                anchor = jnp.logical_and(row == 0, special)
                for f in range(FIELDS):
                    fresh[f] = jnp.where(anchor, jnp.where(lane < slots, means[f], 0.0), fresh[f])
            for chunk in chunks:
                for block, f in enumerate(chunk):
                    store(chunk, residue, rows, block, fresh[f])
        count = 4 * row + slot_of
        kx = jnp.where(count < x_cells // 2, count, count - x_cells).astype(F32)
        odd_kx = jnp.where(count == x_cells // 2, kx, 0.0)
        fresh = green(kx, jnp.full((size, lanes), -0.5 * z_cells, F32), odd_kx, edge)
        for residue in range(4):
            for chunk in chunks:
                extra = None
                for block, f in enumerate(chunk):
                    shift = (block - residue) % lanes
                    moved = fresh[f] if shift == 0 else pltpu.roll(fresh[f], shift, 1)
                    extra = moved if block == 0 else jnp.where(slot_of == block, moved, extra)
                store(chunk, residue, rows, len(chunk), extra)
    copy = pltpu.make_async_copy(rest_out, rest_h, sem)
    copy.start()
    x_inverse(lambda residue: new[residue], table, twiddles, holds_edge(slots, z_cells), out)
    deal(out, own_out, swapped)
    copy.wait()


def z_inverse_kernel(table, data, *rest):
    outs, held = rest[:-1], rest[-1]
    parts = len(GROUPS)
    place = lax.axis_index("gz")
    sources, fields, rows, lanes = data.shape
    half = sources // 2
    fourth = sources // 4

    def columns(begin, end):
        return jnp.concatenate([data[k].reshape(fields * rows, lanes) for k in range(begin, end)], 1)

    first = dot_right(columns(0, half), table, 0)
    zero = dot_right(columns(half, half + fourth), table, 1)
    two = dot_right(columns(half + fourth, sources), table, 2)
    width = zero.shape[1]
    real, imag = first[:, :width], first[:, width:]
    plus, minus = zero + two, zero - two
    for k, value in enumerate((plus + real, minus - imag, plus - real, minus + imag)):
        held[k] = value.reshape(fields, rows, width)
    for step in range(parts):
        target = lax.rem(place + step, parts)
        for slot in range(fields):
            outs[slot * parts + step][...] = held[target, slot]


def stress_kernel(moduli, mean, labels, normals, *rest):
    parts = len(GROUPS)
    arrived, (strain_to, stress_to, held, strain_out, stress_out, sems) = rest[:-6], rest[-6:]
    place = lax.axis_index("gz")
    sections, cells_x, cells_z = labels.shape
    size = cells_x // normals.shape[1]
    for step in range(parts):
        source = lax.rem(place + parts - step, parts)
        for slot in range(FIELDS):
            held[source, slot] = arrived[slot * parts + step][...]
    copies = []
    for section in range(sections):
        squares = tilt(normals, section, cells_z)
        for block in range(cells_x // size):
            rows = pl.ds(block * size, size)
            local = {YY: jnp.full((size, cells_z), mean[YY], F32)}
            for group, fields in enumerate(GROUPS):
                for slot, (component, of) in enumerate(fields):
                    if of == section:
                        local[component] = held[group, slot, rows, :]
            value = law(
                local,
                labels[section, rows, :],
                row_of(squares, block, size),
                (moduli[0], moduli[2]),
                (moduli[1], moduli[3]),
                moduli[4],
            )
            for component in range(6):
                strain_out[component, section, rows, :] = local[component]
                stress_out[component, section, rows, :] = value[component]
        for k, (here, there) in enumerate(((strain_out, strain_to), (stress_out, stress_to))):
            copy = pltpu.make_async_copy(here.at[:, section], there.at[:, section], sems.at[2 * section + k])
            copy.start()
            copies.append(copy)
    for copy in copies:
        copy.wait()


def call(kernel, outs, scratch, args, limit, hbm=(), smem=0, hbm_out=()):
    def space(k):
        return pltpu.HBM if k in hbm else pltpu.SMEM if k < smem else pltpu.VMEM

    args = [pltpu.with_memory_space_constraint(a, pltpu.HBM) if k in hbm else a for k, a in enumerate(args)]
    moved = sum(a.size * a.dtype.itemsize for a in args) + sum(math.prod(o) * 4 for o in outs)
    return pl.pallas_call(
        kernel,
        out_shape=[
            pltpu.HBM(o, F32) if k in hbm_out else jax.ShapeDtypeStruct(o, F32) for k, o in enumerate(outs)
        ],
        in_specs=[pl.BlockSpec(memory_space=space(k)) for k in range(len(args))],
        out_specs=[
            pl.BlockSpec(memory_space=pltpu.HBM if k in hbm_out else pltpu.VMEM) for k in range(len(outs))
        ],
        scratch_shapes=scratch,
        compiler_params=pltpu.CompilerParams(vmem_limit_bytes=limit * MIB),
        cost_estimate=pl.CostEstimate(flops=0, bytes_accessed=moved, transcendentals=0),
    )(*args)


def shards(strain, labels, normals, moduli, mean_strain):
    parts = lax.axis_size("gz")
    x_devices = lax.axis_size("gx")
    _, sections, cells_x, cells_z = strain.shape
    x_total, z_total = cells_x * x_devices, cells_z * parts
    slots = z_total // 2 // x_devices
    lanes = 2 * slots
    z_fwd, z_inv = z_tables(z_total, slots, 1.0 / (x_total * z_total))
    x_tab = x_tables(x_total)
    block = (cells_x, cells_z)
    everyone = range(parts)

    def travel(field, blocks, gather):
        ends = INPLANE if field == 2 else everyone
        moved = [blocks[0]]
        for step in range(1, parts):
            way = [(k, (k + step) % parts) for k in range(parts)]
            way = [(a, b) for a, b in way if (b if gather else a) in ends]
            moved.append(lax.ppermute(blocks[step], "gz", way))
        return moved

    def held(fields):
        return pltpu.VMEM((parts, fields, cells_x, cells_z), F32)

    blocks = call(
        polarize_kernel,
        [block] * (FIELDS * parts),
        [
            held(FIELDS),
            pltpu.VMEM(strain.shape, F32),
            pltpu.VMEM(labels.shape, jnp.int32),
            pltpu.VMEM(normals.shape, jnp.int32),
            pltpu.SMEM(moduli.shape, F32),
            pltpu.SemaphoreType.DMA((2 + 2 * sections,)),
        ],
        (moduli, strain, labels, normals),
        16,
        range(4),
    )
    blocks = {f: list(blocks[f * parts : (f + 1) * parts]) for f in range(FIELDS)}
    quarter = x_total // 4
    chips = x_devices // 2
    early, late = CHUNKS
    size = len(early)
    grid = (x_devices, size, cells_x, lanes)
    tile = (chips, cells_x, lanes)
    tiles = pltpu.VMEM((x_devices, 1, cells_x, lanes), F32)

    def exchange(own, swapped, after):
        got = lax.ppermute(swapped, "gx", [(k, k ^ 1) for k in range(x_devices)])
        merged = call(merge_kernel, [(2, cells_x, lanes)] * (chips - 1), [], (own, got), 8)
        merged, after = lax.optimization_barrier((merged, after))
        moved = [
            lax.ppermute(block, "gx", [(k, k ^ (2 * step)) for k in range(x_devices)])
            for step, block in enumerate(merged, 1)
        ]
        return (own, got, *moved), after

    args = [a for f in early for a in travel(f, blocks[f], True)]
    args, blocks = lax.optimization_barrier((args, blocks))
    (rows,) = call(z_forward_kernel, [grid], [held(size)], (z_fwd, *args), 16)
    rows = lax.all_to_all(rows, "gx", 0, 0, tiled=True)
    args = travel(late[0], blocks[late[0]], True)
    args, rows = lax.optimization_barrier((args, rows))
    own, swapped = call(z_forward_deal_kernel, [tile] * 2, [held(1), tiles], (z_fwd, *args), 16)
    last, rows = exchange(own, swapped, rows)
    copied = [pltpu.VMEM(grid, F32), pltpu.SemaphoreType.DMA]
    (spectrum,) = call(x_forward_kernel, [(4, size, quarter, lanes)], copied, (*x_tab, rows), 24, (2,))
    own, swapped, rest = call(
        functools.partial(green_kernel, x_total, z_total, CHUNKS),
        [tile, tile, (4, quarter, (size + 1) * lanes)],
        [
            tiles,
            tiles,
            pltpu.VMEM((4, 1, quarter, lanes), F32),
            pltpu.VMEM((4, quarter, 2 * lanes), F32),
            pltpu.VMEM((4, quarter, (size + 1) * lanes), F32),
            pltpu.SemaphoreType.DMA,
        ],
        (moduli, mean_strain, *x_tab, spectrum, *last),
        32,
        smem=2,
        hbm_out=(2,),
    )
    last, rest = exchange(own, swapped, rest)
    copied = [pltpu.VMEM(rest.shape, F32), pltpu.SemaphoreType.DMA]
    (rest,) = call(functools.partial(x_inverse_kernel, z_total), [grid], copied, (*x_tab, rest), 24, (2,))
    blocks = call(z_inverse_collect_kernel, [block] * parts, [held(1), tiles], (z_inv, *last), 16)
    rest, blocks = lax.optimization_barrier((rest, list(blocks)))
    rest = lax.all_to_all(rest, "gx", 0, 0, tiled=True)
    arrived = {late[0]: travel(late[0], blocks, False)}
    blocks = call(z_inverse_kernel, [block] * (size * parts), [held(size)], (z_inv, rest), 16)
    for slot, f in enumerate(early):
        arrived[f] = travel(f, blocks[slot * parts : (slot + 1) * parts], False)
    full = (6, sections, cells_x, cells_z)
    args = [a for f in range(FIELDS) for a in arrived[f]]
    return tuple(
        call(
            stress_kernel,
            [full, full],
            [held(FIELDS), pltpu.VMEM(full, F32), pltpu.VMEM(full, F32), pltpu.SemaphoreType.DMA((2 * sections,))],
            (moduli, mean_strain, labels, normals, *args),
            24,
            smem=2,
            hbm_out=(0, 1),
        )
    )


def orientation(normals, blk):
    tilt_angle = math.pi / ANGLES * normals.astype(jnp.float32)
    tilt_angle = jnp.repeat(jnp.repeat(tilt_angle, blk, axis=1), blk, axis=2)
    return (jnp.cos(tilt_angle), jnp.sin(tilt_angle))


def stress_law(strain_field, labels, cosine_tilt, sine_tilt, moduli):
    laminate = labels == 1
    lame_local = jnp.where(laminate, moduli[2], moduli[0])
    shear_local = jnp.where(laminate, moduli[3], moduli[1])
    trace_sum = strain_field[0] + strain_field[1] + strain_field[2]
    normal_part = (
        cosine_tilt * cosine_tilt * strain_field[0]
        + sine_tilt * sine_tilt * strain_field[2]
        + 2.0 * cosine_tilt * sine_tilt * strain_field[4]
    )
    laminate_term = moduli[4] * labels.astype(jnp.float32) * normal_part
    dyad = [
        cosine_tilt * cosine_tilt,
        None,
        sine_tilt * sine_tilt,
        None,
        cosine_tilt * sine_tilt,
        None,
    ]
    result = []
    for slot in range(6):
        value = 2.0 * shear_local * strain_field[slot]
        if slot < 3:
            value = value + lame_local * trace_sum
        if dyad[slot] is not None:
            value = value + laminate_term * dyad[slot]
        result.append(value)
    return jnp.stack(result)


def polarize(stresses, strain_field, lame_ref, shear_ref):
    trace_sum = strain_field[0] + strain_field[1] + strain_field[2]
    result = []
    for slot in range(6):
        value = stresses[slot] - 2.0 * shear_ref * strain_field[slot]
        if slot < 3:
            value = value - lame_ref * trace_sum
        result.append(value)
    return jnp.stack(result)


def green_apply(spectrum, unit_x, unit_z, lame_ref, shear_ref):
    coupling = (lame_ref + shear_ref) / (shear_ref * (lame_ref + 2.0 * shear_ref))
    traction_x = spectrum[0] * unit_x + spectrum[4] * unit_z
    traction_y = spectrum[5] * unit_x + spectrum[3] * unit_z
    traction_z = spectrum[4] * unit_x + spectrum[2] * unit_z
    normal_load = unit_x * traction_x + unit_z * traction_z
    half_inverse = 0.5 / shear_ref
    result = [
        2.0 * half_inverse * unit_x * traction_x - coupling * normal_load * unit_x * unit_x,
        jnp.zeros_like(traction_x),
        2.0 * half_inverse * unit_z * traction_z - coupling * normal_load * unit_z * unit_z,
        half_inverse * unit_z * traction_y,
        half_inverse * (unit_z * traction_x + unit_x * traction_z)
        - coupling * normal_load * unit_x * unit_z,
        half_inverse * unit_x * traction_y,
    ]
    return -jnp.stack(result)


def phases(left_ids, right_ids, length):
    product = left_ids[:, None] * right_ids[None, :] % length
    phase_angle = 2.0 * math.pi / length * product.astype(jnp.float32)
    return (jnp.cos(phase_angle), jnp.sin(phase_angle))


def contract(form, left_side, right_side):
    return jnp.einsum(
        form,
        left_side,
        right_side,
        precision=lax.Precision.HIGHEST,
        preferred_element_type=jnp.float32,
    )


def signed_value(counter, length):
    return jnp.where(counter < length // 2, counter, counter - length).astype(jnp.float32)


def shards_general(strain, labels, normals, moduli, mean_strain):
    z_devices = lax.axis_size("gz")
    x_devices = lax.axis_size("gx")
    z_index = lax.axis_index("gz")
    x_index = lax.axis_index("gx")
    sections = strain.shape[1]
    cells_x = strain.shape[2]
    cells_z = strain.shape[3]
    x_total = cells_x * x_devices
    z_total = cells_z * z_devices
    line_count = sections * cells_x
    kz_share = cells_z // x_devices
    cosine_tilt, sine_tilt = orientation(normals, strain.shape[2] // normals.shape[1])
    lame_ref = 0.5 * (moduli[0] + moduli[2])
    shear_ref = 0.5 * (moduli[1] + moduli[3])
    stresses = stress_law(strain, labels, cosine_tilt, sine_tilt, moduli)
    polarized = polarize(stresses, strain, lame_ref, shear_ref)
    flattened = polarized.reshape(6, line_count, cells_z)
    own_block = z_index * cells_z + jnp.arange(cells_z, dtype=jnp.int32)
    empty_sum = jnp.zeros((6, cells_z, line_count), jnp.float32)
    pieces = lax.all_gather(flattened, "gz", axis=2, tiled=True)
    z_ids = jnp.arange(pieces.shape[2], dtype=jnp.int32)
    cos_table, sin_table = phases(z_ids, own_block, z_total)
    real_part = contract("cmz,zk->ckm", pieces, cos_table)
    imag_part = (empty_sum, empty_sum)[1] - contract("cmz,zk->ckm", pieces, sin_table)
    real_rows, imag_rows = (
        lax.all_to_all(real_part, "gx", split_axis=1, concat_axis=2, tiled=True),
        lax.all_to_all(imag_part, "gx", split_axis=1, concat_axis=2, tiled=True),
    )
    grid_shape = (6, kz_share, x_devices, sections, cells_x)
    real_rows = real_rows.reshape(grid_shape)
    imag_rows = imag_rows.reshape(grid_shape)
    every_x = jnp.arange(x_total, dtype=jnp.int32)
    cos_x, sin_x = phases(every_x, every_x, x_total)
    cos_x = cos_x.reshape(x_devices, cells_x, x_total)
    sin_x = sin_x.reshape(x_devices, cells_x, x_total)
    spec_real = contract("ckgsx,gxq->cksq", real_rows, cos_x) + contract(
        "ckgsx,gxq->cksq", imag_rows, sin_x
    )
    spec_imag = contract("ckgsx,gxq->cksq", imag_rows, cos_x) - contract(
        "ckgsx,gxq->cksq", real_rows, sin_x
    )
    kz_ids = z_index * cells_z + x_index * kz_share + jnp.arange(kz_share, dtype=jnp.int32)
    freq_z = signed_value(kz_ids, z_total)[:, None, None]
    freq_x = signed_value(every_x, x_total)[None, None, :]
    radius_sq = freq_x * freq_x + freq_z * freq_z
    at_anchor = radius_sq == 0.0
    safe_radius = jnp.sqrt(jnp.where(at_anchor, 1.0, radius_sq))
    unit_x = freq_x / safe_radius
    unit_z = freq_z / safe_radius
    anchor_term = jnp.where(at_anchor, float(x_total * z_total), 0.0)
    new_real = green_apply(spec_real, unit_x, unit_z, lame_ref, shear_ref)
    new_real = new_real + mean_strain[:, None, None, None] * anchor_term[None]
    new_imag = green_apply(spec_imag, unit_x, unit_z, lame_ref, shear_ref)
    back_real = contract("cksq,gxq->ckgsx", new_real, cos_x) - contract(
        "cksq,gxq->ckgsx", new_imag, sin_x
    )
    back_imag = contract("cksq,gxq->ckgsx", new_real, sin_x) + contract(
        "cksq,gxq->ckgsx", new_imag, cos_x
    )
    back_real = back_real.reshape(6, kz_share, x_devices * line_count)
    back_imag = back_imag.reshape(6, kz_share, x_devices * line_count)
    real_part, imag_part = (
        lax.all_to_all(back_real, "gx", split_axis=2, concat_axis=1, tiled=True),
        lax.all_to_all(back_imag, "gx", split_axis=2, concat_axis=1, tiled=True),
    )
    z_ids = jnp.arange(lax.axis_size("gz") * cells_z, dtype=jnp.int32)
    cos_table, sin_table = phases(own_block, z_ids, z_total)
    summed = lax.psum_scatter(
        contract("ckm,kz->zcm", real_part, cos_table)
        - contract("ckm,kz->zcm", imag_part, sin_table),
        "gz",
        scatter_dimension=0,
        tiled=True,
    )
    field_lines = jnp.transpose(summed, (1, 2, 0))
    strain_next = (field_lines * (1.0 / (x_total * z_total))).reshape(6, sections, cells_x, cells_z)
    stress_next = stress_law(strain_next, labels, cosine_tilt, sine_tilt, moduli)
    return (strain_next, stress_next)


def solution(mesh):
    in_specs = (P(None, None, "gx", "gz"), P(None, "gx", "gz"), P(None, "gx", "gz"), P(), P())
    out_specs = (P(None, None, "gx", "gz"), P(None, None, "gx", "gz"))

    def run(strain, labels, normals, moduli, mean_strain):
        _, sections, x_total, z_total = strain.shape
        parts, x_devices = mesh.shape["gz"], mesh.shape["gx"]
        grouped = (
            sections == 2
            and parts == len(GROUPS)
            and x_devices == 8
            and z_total == 128 * x_devices
            and x_total % (128 * x_devices) == 0
        )
        body = shards if grouped else shards_general
        mapped = jax.shard_map(body, mesh=mesh, in_specs=in_specs, out_specs=out_specs, check_vma=False)
        return mapped(strain, labels, normals, moduli, mean_strain)

    return run
```

```python
import functools
import math

import jax
import jax.numpy as jnp
import numpy as np
from jax import lax
from jax.experimental import pallas as pl
from jax.experimental.pallas import tpu as pltpu
from jax.sharding import PartitionSpec as P

ANGLES = 8
XX, YY, ZZ, YZ, XZ, XY = range(6)
GROUPS = (
    ((XY, 0), (YZ, 0)),
    ((XX, 0), (ZZ, 0), (XZ, 0)),
    ((XX, 1), (ZZ, 1), (XZ, 1)),
    ((XY, 1), (YZ, 1)),
)
INPLANE = (1, 2)
FIELDS = 3
CHUNKS = ((0, 2), (1,))
F32, BF16 = jnp.float32, jnp.bfloat16
MIB = 1 << 20


def split_table(table):
    table = np.asarray(table, np.float32)
    high = table.astype(jnp.bfloat16)
    low = (table - high.astype(np.float32)).astype(jnp.bfloat16)
    return jnp.asarray(np.stack([high, low]))


def half_frequencies(length):
    quarter = length // 4
    return (
        4 * np.arange(quarter) + 1,
        4 * np.arange(quarter // 2),
        4 * np.arange(quarter // 2) + 2,
    )


def interleave(real, imag, slots):
    rows, count = real.shape
    both = np.stack([real.reshape(rows, -1, slots), imag.reshape(rows, -1, slots)], 2)
    return both.reshape(rows, 2 * count)


def z_tables(length, slots, scale):
    quarter = length // 4
    z = np.arange(quarter, dtype=np.int64)[:, None]
    ones, zeros, twos = half_frequencies(length)

    def angles(freqs):
        return 2.0 * math.pi / length * ((z * freqs[None, :]) % length)

    one, zero, two = angles(ones), angles(zeros), angles(twos)
    top = interleave(np.cos(one), -np.sin(one), slots)
    bottom = interleave(-np.sin(one), -np.cos(one), slots)
    forward_one = np.concatenate([top, bottom], 0)
    real, imag = np.cos(zero), -np.sin(zero)
    imag[:, 0] = np.where(np.arange(quarter) % 2 == 0, 1.0, -1.0)
    forward_zero = interleave(real, imag, slots)
    forward_two = interleave(np.cos(two), -np.sin(two), slots)
    weight = 2.0 * scale
    inverse_one = weight * np.concatenate(
        [interleave(np.cos(one), -np.sin(one), slots), interleave(np.sin(one), np.cos(one), slots)], 0
    ).T
    half = np.full(quarter // 2, weight)
    half[0] = scale
    inverse_zero = interleave(real * half, imag * half, slots).T
    inverse_two = weight * forward_two.T

    def pack(first, second, third):
        return split_table(np.concatenate([first, np.concatenate([second, third], 1)], 0))

    return pack(forward_one, forward_zero, forward_two), pack(inverse_one, inverse_zero, inverse_two)


def x_tables(length):
    quarter = length // 4
    k = np.arange(quarter, dtype=np.int64)
    angle = 2.0 * math.pi / quarter * ((k[:, None] * k[None, :]) % quarter)
    turn = 2.0 * math.pi / length * k
    columns = [f(residue * turn) for residue in (1, 2, 3) for f in (np.cos, np.sin)]
    twiddles = jnp.asarray(np.stack(columns + columns[:2], 1).astype(np.float32))
    return split_table(np.concatenate([np.cos(angle), np.sin(angle)], 0)), twiddles


def halves(value):
    high = value.astype(BF16)
    return high, (value - high.astype(F32)).astype(BF16)


def dot(left, right):
    return jnp.dot(left, right, preferred_element_type=F32)


def dot_right(value, table, part):
    big = table.shape[2]
    half = big // 2
    rows = slice(0, big) if part == 0 else slice(big, big + half)
    columns = slice(0, big) if part == 0 else slice((part - 1) * half, part * half)
    high_table, low_table = table[0, rows, columns], table[1, rows, columns]
    high, low = halves(value)
    return dot(high, high_table) + (dot(low, high_table) + dot(high, low_table))


def dot_left(table, value):
    high, low = halves(value)
    return dot(table[0], high) + (dot(table[0], low) + dot(table[1], high))


def tilt(normals, section, cells_z):
    blocks = normals[section].astype(F32)
    count = blocks.shape[1]
    size = cells_z // count
    owner = lax.broadcasted_iota(jnp.int32, (count, cells_z), 1) // size
    own = lax.broadcasted_iota(jnp.int32, (count, cells_z), 0)
    spread = jnp.where(owner == own, 1.0, 0.0).astype(F32)
    angle = (math.pi / ANGLES) * dot(blocks, spread)
    cosine, sine = jnp.cos(angle), jnp.sin(angle)
    return cosine * cosine, sine * sine, cosine * sine


def law(strain, label, squares, lame, shear, stiff):
    cc, ss, cs = squares
    laminate = label == 1
    lame_local = jnp.where(laminate, lame[1], lame[0])
    twice_shear = jnp.where(laminate, 2.0 * shear[1], 2.0 * shear[0])
    spherical = lame_local * (strain[XX] + strain[YY] + strain[ZZ])
    normal = cc * strain[XX] + ss * strain[ZZ] + 2.0 * cs * strain[XZ]
    normal = jnp.where(laminate, stiff, 0.0) * normal
    return {
        XX: twice_shear * strain[XX] + spherical + normal * cc,
        YY: twice_shear * strain[YY] + spherical,
        ZZ: twice_shear * strain[ZZ] + spherical + normal * ss,
        YZ: twice_shear * strain[YZ],
        XZ: twice_shear * strain[XZ] + normal * cs,
        XY: twice_shear * strain[XY],
    }


def row_of(squares, block, size):
    return [jnp.broadcast_to(s[block : block + 1], (size, s.shape[1])) for s in squares]


def polarize_kernel(moduli_h, strain_h, labels_h, normals_h, *rest):
    outs, (held, strain, labels, normals, moduli, sems) = rest[:-6], rest[-6:]
    sections, cells_x, cells_z = labels.shape
    copies = [
        pltpu.make_async_copy(moduli_h, moduli, sems.at[0]),
        pltpu.make_async_copy(normals_h, normals, sems.at[1]),
    ]
    for k in range(sections):
        copies.append(pltpu.make_async_copy(labels_h.at[k], labels.at[k], sems.at[2 + 2 * k]))
        copies.append(pltpu.make_async_copy(strain_h.at[:, k], strain.at[:, k], sems.at[3 + 2 * k]))
    for copy in copies:
        copy.start()
    for copy in copies[:2]:
        copy.wait()
    parts = len(GROUPS)
    place = lax.axis_index("gz")
    size = cells_x // normals.shape[1]
    lame_ref = 0.5 * (moduli[0] + moduli[2])
    shear_ref = 0.5 * (moduli[1] + moduli[3])
    lame = (moduli[0] - lame_ref, moduli[2] - lame_ref)
    shear = (moduli[1] - shear_ref, moduli[3] - shear_ref)
    for group, fields in enumerate(GROUPS):
        if len(fields) < 3:
            held[group, 2] = jnp.zeros((cells_x, cells_z), F32)
    for section in range(sections):
        copies[2 + 2 * section].wait()
        copies[3 + 2 * section].wait()
        squares = tilt(normals, section, cells_z)
        for block in range(cells_x // size):
            rows = pl.ds(block * size, size)
            local = [strain[c, section, rows, :] for c in range(6)]
            value = law(local, labels[section, rows, :], row_of(squares, block, size), lame, shear, moduli[4])
            for group, fields in enumerate(GROUPS):
                for slot, (component, of) in enumerate(fields):
                    if of == section:
                        held[group, slot, rows, :] = value[component]
    for step in range(parts):
        target = lax.rem(place + step, parts)
        for slot in range(FIELDS):
            outs[slot * parts + step][...] = held[target, slot]


def deal(blocks, own, swapped):
    mine = lax.axis_index("gx")
    chip, core = mine // 2, lax.rem(mine, 2)
    for step in range(own.shape[0]):
        there = 2 * lax.bitwise_xor(chip, step)
        own[step] = blocks[there + core, 0]
        swapped[step] = blocks[there + 1 - core, 0]


def collect(own, got, moved, blocks):
    mine = lax.axis_index("gx")
    chip, core = mine // 2, lax.rem(mine, 2)
    for step in range(own.shape[0]):
        there = 2 * lax.bitwise_xor(chip, step)
        blocks[there + core, 0] = own[0] if step == 0 else moved[step - 1][0]
        blocks[there + 1 - core, 0] = got[0] if step == 0 else moved[step - 1][1]


def merge_kernel(own, got, *outs):
    for k, out in enumerate(outs):
        out[0] = own[k + 1]
        out[1] = got[k + 1]


def z_forward_deal_kernel(table, *rest):
    arrived, (own, swapped, held, blocks) = rest[:-4], rest[-4:]
    z_forward_kernel(table, *arrived, blocks, held)
    deal(blocks, own, swapped)


def z_inverse_collect_kernel(table, own, got, *rest):
    chips = own.shape[0]
    moved, outs, (held, blocks) = rest[: chips - 1], rest[chips - 1 : -2], rest[-2:]
    collect(own, got, moved, blocks)
    z_inverse_kernel(table, blocks, *outs, held)


def z_forward_kernel(table, *rest):
    parts = len(GROUPS)
    arrived, (out, held) = rest[:-2], rest[-2:]
    place = lax.axis_index("gz")
    for step in range(parts):
        source = lax.rem(place + parts - step, parts)
        for slot in range(held.shape[1]):
            held[source, slot] = arrived[slot * parts + step][...]
    fields, rows, width = held.shape[1:]
    lanes = out.shape[3]
    z0, z1, z2, z3 = (held[k].reshape(fields * rows, width) for k in range(parts))
    first = jnp.concatenate([z0 - z2, z1 - z3], 1)
    even, odd = z0 + z2, z1 + z3
    spectra = (
        dot_right(first, table, 0),
        dot_right(even + odd, table, 1),
        dot_right(even - odd, table, 2),
    )
    target = 0
    for spectrum in spectra:
        for k in range(spectrum.shape[1] // lanes):
            out[target] = spectrum[:, k * lanes : (k + 1) * lanes].reshape(fields, rows, lanes)
            target += 1


def swap(value):
    lanes = value.shape[1]
    return jnp.concatenate([pltpu.roll(value[:, k : k + 128], 64, 1) for k in range(0, lanes, 128)], 1)


def turn_sign(width):
    lane = lax.broadcasted_iota(jnp.int32, (1, width), 1) % 128
    return jnp.where(lane < 64, 1.0, -1.0).astype(F32)


def twiddle(twiddles, residue, value, sign):
    if residue == 0:
        return value
    pick = 2 * (residue - 1)
    quarter = value.shape[0]
    cosine = jnp.broadcast_to(twiddles[:, pick : pick + 1], (quarter, 128))
    sine = jnp.broadcast_to(twiddles[:, pick + 1 : pick + 2], (quarter, 128)) * sign[:, :128]
    pieces = []
    for k in range(0, value.shape[1], 128):
        piece = value[:, k : k + 128]
        pieces.append(cosine * piece + sine * pltpu.roll(piece, 64, 1))
    return jnp.concatenate(pieces, 1)


def x_forward(data, table, twiddles):
    sources, fields, rows, lanes = data.shape
    quarter = sources * rows // 4
    per = sources // 4
    width = fields * lanes
    sign = turn_sign(width)
    block = [
        jnp.concatenate([data[a * per : (a + 1) * per, f].reshape(quarter, lanes) for f in range(fields)], 1)
        for a in range(4)
    ]
    even, odd = block[0] + block[2], block[1] + block[3]
    diff, turned = block[0] - block[2], sign * swap(block[1] - block[3])
    values = (even + odd, diff + turned, even - odd, diff - turned)
    values = [twiddle(twiddles, residue, value, sign) for residue, value in enumerate(values)]
    both = dot_left(table, jnp.concatenate(values, 1))
    for residue in range(4):
        columns = slice(residue * width, (residue + 1) * width)
        yield both[:quarter, columns] + sign * swap(both[quarter:, columns])


def x_inverse(spectra, table, twiddles, is_special, out):
    sources, fields, rows, lanes = out.shape
    quarter = sources * rows // 4
    per = sources // 4
    width = fields * lanes
    sign = turn_sign(spectra.shape[1])
    both = dot_left(table, spectra)
    both = both[:quarter] - sign * swap(both[quarter:])
    sign = sign[:, :width]

    def join(values):
        h0, h1, h2, h3 = [twiddle(twiddles, residue, value, -sign) for residue, value in enumerate(values)]
        even, odd = h0 + h2, h1 + h3
        diff, turned = h0 - h2, sign * swap(h1 - h3)
        return even + odd, diff - turned, even - odd, diff + turned

    packed = both[:, 4 * width :]
    unpacked = [packed]
    for residue in range(1, 4):
        pieces = [pltpu.roll(packed[:, k : k + lanes], lanes - residue, 1) for k in range(0, width, lanes)]
        unpacked.append(jnp.concatenate(pieces, 1))
    lane = lax.broadcasted_iota(jnp.int32, (1, width), 1) % lanes
    edge = jnp.logical_and(is_special, lane == lanes // 2)
    whole = join([both[:, residue * width : (residue + 1) * width] for residue in range(4)])
    for a, (value, other) in enumerate(zip(whole, join(unpacked))):
        final = jnp.where(edge, other, value)
        for f in range(fields):
            out[a * per : (a + 1) * per, f] = final[:, f * lanes : (f + 1) * lanes].reshape(per, rows, lanes)


def holds_edge(slots, z_cells):
    return lax.axis_index("gx") * slots == z_cells // 4


def x_forward_kernel(table, twiddles, data_h, out, data, sem):
    copy = pltpu.make_async_copy(data_h, data, sem)
    copy.start()
    copy.wait()
    fields, lanes = data.shape[1], data.shape[3]
    for residue, spectrum in enumerate(x_forward(data, table, twiddles)):
        for f in range(fields):
            out[residue, f] = spectrum[:, f * lanes : (f + 1) * lanes]


def x_inverse_kernel(z_cells, table, twiddles, data_h, out, data, sem):
    copy = pltpu.make_async_copy(data_h, data, sem)
    copy.start()
    copy.wait()
    special = holds_edge(out.shape[3] // 2, z_cells)
    x_inverse(data[...], table, twiddles, special, out)


def green_kernel(x_cells, z_cells, chunks, moduli, mean, table, twiddles, done, own_in, got, *rest):
    chips = own_in.shape[0]
    moved, rest = rest[: chips - 1], rest[chips - 1 :]
    own_out, swapped, rest_h, data, out, own, new, rest_out, sem = rest
    collect(own_in, got, moved, data)
    rest_chunk, own_chunk = chunks
    lanes = data.shape[3]
    slots = lanes // 2
    quarter = x_cells // 4
    place, mine = lax.axis_index("gz"), lax.axis_index("gx")
    inplane = functools.reduce(jnp.logical_or, [place == k for k in INPLANE])
    lame_ref = 0.5 * (moduli[0] + moduli[2])
    shear_ref = 0.5 * (moduli[1] + moduli[3])
    half_inverse = 0.5 / shear_ref
    coupling = (lame_ref + shear_ref) / (shear_ref * (lame_ref + 2.0 * shear_ref))
    c1 = jnp.where(inplane, coupling, 0.0)
    k1 = jnp.where(inplane, 2.0 * half_inverse, half_inverse)
    k2 = jnp.where(inplane, half_inverse, 0.0)
    ka = jnp.where(inplane, 0.0, half_inverse)
    total = float(x_cells * z_cells)
    means = (
        total * jnp.where(inplane, mean[XX], mean[XY]),
        total * jnp.where(inplane, mean[ZZ], mean[YZ]),
        total * mean[XZ],
    )

    for residue, spectrum in enumerate(x_forward(data, table, twiddles)):
        for slot in range(len(own_chunk)):
            own[residue, slot] = spectrum[:, slot * lanes : (slot + 1) * lanes]

    def load(field, residue, rows):
        if field in own_chunk:
            return own[residue, own_chunk.index(field), rows, :]
        return done[residue, rest_chunk.index(field), rows, :]

    def store(field, residue, rows, value):
        chunk, spectra = (own_chunk, new) if field in own_chunk else (rest_chunk, rest_out)
        block = residue * len(chunk) + chunk.index(field)
        spectra[rows, block * lanes : (block + 1) * lanes] = value

    def green(kx, kz, odd_kx, s, anchored=False):
        radius = kx * kx + kz * kz
        if anchored:
            radius = jnp.where(radius == 0.0, 1.0, radius)
        inverse = 1.0 / radius
        a, b = kx * kx * inverse, kz * kz * inverse
        d = odd_kx * kz * inverse
        ab = c1 * (a * b)
        ca, cb = c1 * a, c1 * b
        h02, h12 = d * (ca - k2), d * (cb - k2)
        m01 = ab - ka * d
        twice = 2.0 * s[2]
        return (
            a * (ca - k1) * s[0] + m01 * s[1] + h02 * twice,
            m01 * s[0] + b * (cb - k1) * s[1] + h12 * twice,
            h02 * s[0] + h12 * s[1] + (2.0 * ab - k2) * s[2],
        )

    lane = lax.broadcasted_iota(jnp.int32, (1, lanes), 1)
    slot_of = lane % slots
    order = mine * slots + slot_of
    zeros_at, twos_at = z_cells // 4, z_cells // 4 + z_cells // 8
    kz = jnp.where(
        order < zeros_at,
        4 * order + 1,
        jnp.where(order < twos_at, 4 * (order - zeros_at), 4 * (order - twos_at) + 2),
    )
    kz = jnp.where(kz < z_cells // 2, kz, kz - z_cells).astype(F32)
    special = order == zeros_at
    size = 32
    for start in range(0, quarter, size):
        rows = pl.ds(start, size)
        row = lax.broadcasted_iota(jnp.int32, (size, lanes), 0) + start
        full_kz = jnp.broadcast_to(kz, (size, lanes))
        first_kx = (4 * row - (x_cells if 2 * start >= quarter else 0)).astype(F32)
        mirror = 2 * start == quarter
        edge = [None] * FIELDS
        for residue in range(4):
            s = [load(f, residue, rows) for f in range(FIELDS)]
            for f in range(FIELDS):
                moved = s[f] if residue == 0 else pltpu.roll(s[f], residue, 1)
                edge[f] = moved if residue == 0 else jnp.where(slot_of == residue, moved, edge[f])
            kx = first_kx + float(residue)
            odd_kx = jnp.where(row == start, 0.0, kx) if mirror and residue == 0 else kx
            with_anchor = residue == 0 and start == 0
            fresh = list(green(kx, full_kz, odd_kx, s, with_anchor))
            if with_anchor:
                anchor = jnp.logical_and(row == 0, special)
                for f in range(FIELDS):
                    fresh[f] = jnp.where(anchor, jnp.where(lane < slots, means[f], 0.0), fresh[f])
            for f in range(FIELDS):
                store(f, residue, rows, fresh[f])
        kx = first_kx + slot_of.astype(F32)
        odd_kx = jnp.where(jnp.logical_and(row == start, slot_of == 0), kx, 0.0) if mirror else jnp.zeros_like(kx)
        fresh = green(kx, jnp.full((size, lanes), -0.5 * z_cells, F32), odd_kx, edge)
        for f in range(FIELDS):
            store(f, 4, rows, fresh[f])
    copy = pltpu.make_async_copy(rest_out, rest_h, sem)
    copy.start()
    x_inverse(new[...], table, twiddles, holds_edge(slots, z_cells), out)
    deal(out, own_out, swapped)
    copy.wait()


def z_inverse_kernel(table, data, *rest):
    outs, held = rest[:-1], rest[-1]
    parts = len(GROUPS)
    place = lax.axis_index("gz")
    sources, fields, rows, lanes = data.shape
    half = sources // 2
    fourth = sources // 4

    def columns(begin, end):
        return jnp.concatenate([data[k].reshape(fields * rows, lanes) for k in range(begin, end)], 1)

    first = dot_right(columns(0, half), table, 0)
    zero = dot_right(columns(half, half + fourth), table, 1)
    two = dot_right(columns(half + fourth, sources), table, 2)
    width = zero.shape[1]
    real, imag = first[:, :width], first[:, width:]
    plus, minus = zero + two, zero - two
    for k, value in enumerate((plus + real, minus - imag, plus - real, minus + imag)):
        held[k] = value.reshape(fields, rows, width)
    for step in range(parts):
        target = lax.rem(place + step, parts)
        for slot in range(fields):
            outs[slot * parts + step][...] = held[target, slot]


def stress_kernel(slots, strain_parts, stress_parts, moduli, mean, labels, normals, *rest):
    parts = len(GROUPS)
    arrived = rest[: len(slots) * parts]
    strain_to, stress_to, held, strain_out, stress_out, sems = rest[-6:]
    place = lax.axis_index("gz")
    sections, cells_x, cells_z = labels.shape
    size = cells_x // normals.shape[1]
    for step in range(parts):
        source = lax.rem(place + parts - step, parts)
        for k, slot in enumerate(slots):
            held[source, slot] = arrived[k * parts + step][...]
    copies = []
    for section in range(sections):
        squares = tilt(normals, section, cells_z)
        for block in range(cells_x // size):
            rows = pl.ds(block * size, size)
            local = {c: jnp.zeros((size, cells_z), F32) for c in range(6)}
            local[YY] = jnp.full((size, cells_z), mean[YY], F32)
            for group, fields in enumerate(GROUPS):
                for slot, (component, of) in enumerate(fields):
                    if of == section and slot in slots:
                        local[component] = held[group, slot, rows, :]
            value = law(
                local,
                labels[section, rows, :],
                row_of(squares, block, size),
                (moduli[0], moduli[2]),
                (moduli[1], moduli[3]),
                moduli[4],
            )
            for component in strain_parts:
                strain_out[component, section, rows, :] = local[component]
            for component in stress_parts:
                stress_out[component, section, rows, :] = value[component]
        for here, there, chosen in ((strain_out, strain_to, strain_parts), (stress_out, stress_to, stress_parts)):
            for c in chosen:
                copy = pltpu.make_async_copy(here.at[c, section], there.at[c, section], sems.at[len(copies)])
                copy.start()
                copies.append(copy)
    for copy in copies:
        copy.wait()


def call(kernel, outs, scratch, args, limit, hbm=(), smem=0, hbm_out=(), aliases={}):
    def space(k):
        return pltpu.HBM if k in hbm else pltpu.SMEM if k < smem else pltpu.VMEM

    args = [pltpu.with_memory_space_constraint(a, pltpu.HBM) if k in hbm else a for k, a in enumerate(args)]
    moved = sum(a.size * a.dtype.itemsize for a in args) + sum(math.prod(o) * 4 for o in outs)
    return pl.pallas_call(
        kernel,
        out_shape=[
            pltpu.HBM(o, F32) if k in hbm_out else jax.ShapeDtypeStruct(o, F32) for k, o in enumerate(outs)
        ],
        in_specs=[pl.BlockSpec(memory_space=space(k)) for k in range(len(args))],
        out_specs=[
            pl.BlockSpec(memory_space=pltpu.HBM if k in hbm_out else pltpu.VMEM) for k in range(len(outs))
        ],
        scratch_shapes=scratch,
        input_output_aliases=aliases,
        compiler_params=pltpu.CompilerParams(vmem_limit_bytes=limit * MIB),
        cost_estimate=pl.CostEstimate(flops=0, bytes_accessed=moved, transcendentals=0),
    )(*args)


def shards(strain, labels, normals, moduli, mean_strain):
    parts = lax.axis_size("gz")
    x_devices = lax.axis_size("gx")
    _, sections, cells_x, cells_z = strain.shape
    x_total, z_total = cells_x * x_devices, cells_z * parts
    slots = z_total // 2 // x_devices
    lanes = 2 * slots
    z_fwd, z_inv = z_tables(z_total, slots, 1.0 / (x_total * z_total))
    x_tab = x_tables(x_total)
    block = (cells_x, cells_z)
    everyone = range(parts)

    def travel(field, blocks, gather):
        ends = INPLANE if field == 2 else everyone
        moved = [blocks[0]]
        for step in range(1, parts):
            way = [(k, (k + step) % parts) for k in range(parts)]
            way = [(a, b) for a, b in way if (b if gather else a) in ends]
            moved.append(lax.ppermute(blocks[step], "gz", way))
        return moved

    def held(fields):
        return pltpu.VMEM((parts, fields, cells_x, cells_z), F32)

    blocks = call(
        polarize_kernel,
        [block] * (FIELDS * parts),
        [
            held(FIELDS),
            pltpu.VMEM(strain.shape, F32),
            pltpu.VMEM(labels.shape, jnp.int32),
            pltpu.VMEM(normals.shape, jnp.int32),
            pltpu.SMEM(moduli.shape, F32),
            pltpu.SemaphoreType.DMA((2 + 2 * sections,)),
        ],
        (moduli, strain, labels, normals),
        16,
        range(4),
    )
    blocks = {f: list(blocks[f * parts : (f + 1) * parts]) for f in range(FIELDS)}
    quarter = x_total // 4
    chips = x_devices // 2
    early, late = CHUNKS
    size = len(early)
    grid = (x_devices, size, cells_x, lanes)
    tile = (chips, cells_x, lanes)
    tiles = pltpu.VMEM((x_devices, 1, cells_x, lanes), F32)

    def exchange(own, swapped, after):
        got = lax.ppermute(swapped, "gx", [(k, k ^ 1) for k in range(x_devices)])
        merged = call(merge_kernel, [(2, cells_x, lanes)] * (chips - 1), [], (own, got), 8)
        merged, after = lax.optimization_barrier((merged, after))
        moved = [
            lax.ppermute(block, "gx", [(k, k ^ (2 * step)) for k in range(x_devices)])
            for step, block in enumerate(merged, 1)
        ]
        return (own, got, *moved), after

    args = [a for f in early for a in travel(f, blocks[f], True)]
    args, blocks = lax.optimization_barrier((args, blocks))
    (rows,) = call(z_forward_kernel, [grid], [held(size)], (z_fwd, *args), 16)
    rows = lax.all_to_all(rows, "gx", 0, 0, tiled=True)
    args = travel(late[0], blocks[late[0]], True)
    args, rows = lax.optimization_barrier((args, rows))
    own, swapped = call(z_forward_deal_kernel, [tile] * 2, [held(1), tiles], (z_fwd, *args), 16)
    last, rows = exchange(own, swapped, rows)
    copied = [pltpu.VMEM(grid, F32), pltpu.SemaphoreType.DMA]
    (spectrum,) = call(x_forward_kernel, [(4, size, quarter, lanes)], copied, (*x_tab, rows), 24, (2,))
    own, swapped, rest = call(
        functools.partial(green_kernel, x_total, z_total, CHUNKS),
        [tile, tile, (quarter, 5 * size * lanes)],
        [
            tiles,
            tiles,
            pltpu.VMEM((4, 1, quarter, lanes), F32),
            pltpu.VMEM((quarter, 5 * lanes), F32),
            pltpu.VMEM((quarter, 5 * size * lanes), F32),
            pltpu.SemaphoreType.DMA,
        ],
        (moduli, mean_strain, *x_tab, spectrum, *last),
        32,
        smem=2,
        hbm_out=(2,),
    )
    last, rest = exchange(own, swapped, rest)
    copied = [pltpu.VMEM(rest.shape, F32), pltpu.SemaphoreType.DMA]
    (rest,) = call(functools.partial(x_inverse_kernel, z_total), [grid], copied, (*x_tab, rest), 24, (2,))
    blocks = call(z_inverse_collect_kernel, [block] * parts, [held(1), tiles], (z_inv, *last), 16)
    rest, blocks = lax.optimization_barrier((rest, list(blocks)))
    rest = lax.all_to_all(rest, "gx", 0, 0, tiled=True)
    arrived = {late[0]: travel(late[0], blocks, False)}
    blocks = call(z_inverse_kernel, [block] * (size * parts), [held(size)], (z_inv, rest), 16)
    for slot, f in enumerate(early):
        arrived[f] = travel(f, blocks[slot * parts : (slot + 1) * parts], False)
    full = (6, sections, cells_x, cells_z)
    results = ()
    for slots, strains, stresses in (((0, 1), (XX, YY, ZZ, YZ, XY), (YY, YZ, XY)), ((0, 1, 2), (XZ,), (XX, ZZ, XZ))):
        args = (moduli, mean_strain, labels, normals, *[a for f in slots for a in arrived[f]], *results)
        hbm = range(len(args) - len(results), len(args))
        count = sections * (len(strains) + len(stresses))
        results = call(
            functools.partial(stress_kernel, slots, strains, stresses),
            [full, full],
            [held(FIELDS), pltpu.VMEM(full, F32), pltpu.VMEM(full, F32), pltpu.SemaphoreType.DMA((count,))],
            args,
            16,
            hbm,
            smem=2,
            hbm_out=(0, 1),
            aliases={k: out for out, k in enumerate(hbm)},
        )
    return tuple(results)


def orientation(normals, blk):
    tilt_angle = math.pi / ANGLES * normals.astype(jnp.float32)
    tilt_angle = jnp.repeat(jnp.repeat(tilt_angle, blk, axis=1), blk, axis=2)
    return (jnp.cos(tilt_angle), jnp.sin(tilt_angle))


def stress_law(strain_field, labels, cosine_tilt, sine_tilt, moduli):
    laminate = labels == 1
    lame_local = jnp.where(laminate, moduli[2], moduli[0])
    shear_local = jnp.where(laminate, moduli[3], moduli[1])
    trace_sum = strain_field[0] + strain_field[1] + strain_field[2]
    normal_part = (
        cosine_tilt * cosine_tilt * strain_field[0]
        + sine_tilt * sine_tilt * strain_field[2]
        + 2.0 * cosine_tilt * sine_tilt * strain_field[4]
    )
    laminate_term = moduli[4] * labels.astype(jnp.float32) * normal_part
    dyad = [
        cosine_tilt * cosine_tilt,
        None,
        sine_tilt * sine_tilt,
        None,
        cosine_tilt * sine_tilt,
        None,
    ]
    result = []
    for slot in range(6):
        value = 2.0 * shear_local * strain_field[slot]
        if slot < 3:
            value = value + lame_local * trace_sum
        if dyad[slot] is not None:
            value = value + laminate_term * dyad[slot]
        result.append(value)
    return jnp.stack(result)


def polarize(stresses, strain_field, lame_ref, shear_ref):
    trace_sum = strain_field[0] + strain_field[1] + strain_field[2]
    result = []
    for slot in range(6):
        value = stresses[slot] - 2.0 * shear_ref * strain_field[slot]
        if slot < 3:
            value = value - lame_ref * trace_sum
        result.append(value)
    return jnp.stack(result)


def green_apply(spectrum, unit_x, unit_z, lame_ref, shear_ref):
    coupling = (lame_ref + shear_ref) / (shear_ref * (lame_ref + 2.0 * shear_ref))
    traction_x = spectrum[0] * unit_x + spectrum[4] * unit_z
    traction_y = spectrum[5] * unit_x + spectrum[3] * unit_z
    traction_z = spectrum[4] * unit_x + spectrum[2] * unit_z
    normal_load = unit_x * traction_x + unit_z * traction_z
    half_inverse = 0.5 / shear_ref
    result = [
        2.0 * half_inverse * unit_x * traction_x - coupling * normal_load * unit_x * unit_x,
        jnp.zeros_like(traction_x),
        2.0 * half_inverse * unit_z * traction_z - coupling * normal_load * unit_z * unit_z,
        half_inverse * unit_z * traction_y,
        half_inverse * (unit_z * traction_x + unit_x * traction_z)
        - coupling * normal_load * unit_x * unit_z,
        half_inverse * unit_x * traction_y,
    ]
    return -jnp.stack(result)


def phases(left_ids, right_ids, length):
    product = left_ids[:, None] * right_ids[None, :] % length
    phase_angle = 2.0 * math.pi / length * product.astype(jnp.float32)
    return (jnp.cos(phase_angle), jnp.sin(phase_angle))


def contract(form, left_side, right_side):
    return jnp.einsum(
        form,
        left_side,
        right_side,
        precision=lax.Precision.HIGHEST,
        preferred_element_type=jnp.float32,
    )


def signed_value(counter, length):
    return jnp.where(counter < length // 2, counter, counter - length).astype(jnp.float32)


def shards_general(strain, labels, normals, moduli, mean_strain):
    z_devices = lax.axis_size("gz")
    x_devices = lax.axis_size("gx")
    z_index = lax.axis_index("gz")
    x_index = lax.axis_index("gx")
    sections = strain.shape[1]
    cells_x = strain.shape[2]
    cells_z = strain.shape[3]
    x_total = cells_x * x_devices
    z_total = cells_z * z_devices
    line_count = sections * cells_x
    kz_share = cells_z // x_devices
    cosine_tilt, sine_tilt = orientation(normals, strain.shape[2] // normals.shape[1])
    lame_ref = 0.5 * (moduli[0] + moduli[2])
    shear_ref = 0.5 * (moduli[1] + moduli[3])
    stresses = stress_law(strain, labels, cosine_tilt, sine_tilt, moduli)
    polarized = polarize(stresses, strain, lame_ref, shear_ref)
    flattened = polarized.reshape(6, line_count, cells_z)
    own_block = z_index * cells_z + jnp.arange(cells_z, dtype=jnp.int32)
    empty_sum = jnp.zeros((6, cells_z, line_count), jnp.float32)
    pieces = lax.all_gather(flattened, "gz", axis=2, tiled=True)
    z_ids = jnp.arange(pieces.shape[2], dtype=jnp.int32)
    cos_table, sin_table = phases(z_ids, own_block, z_total)
    real_part = contract("cmz,zk->ckm", pieces, cos_table)
    imag_part = (empty_sum, empty_sum)[1] - contract("cmz,zk->ckm", pieces, sin_table)
    real_rows, imag_rows = (
        lax.all_to_all(real_part, "gx", split_axis=1, concat_axis=2, tiled=True),
        lax.all_to_all(imag_part, "gx", split_axis=1, concat_axis=2, tiled=True),
    )
    grid_shape = (6, kz_share, x_devices, sections, cells_x)
    real_rows = real_rows.reshape(grid_shape)
    imag_rows = imag_rows.reshape(grid_shape)
    every_x = jnp.arange(x_total, dtype=jnp.int32)
    cos_x, sin_x = phases(every_x, every_x, x_total)
    cos_x = cos_x.reshape(x_devices, cells_x, x_total)
    sin_x = sin_x.reshape(x_devices, cells_x, x_total)
    spec_real = contract("ckgsx,gxq->cksq", real_rows, cos_x) + contract(
        "ckgsx,gxq->cksq", imag_rows, sin_x
    )
    spec_imag = contract("ckgsx,gxq->cksq", imag_rows, cos_x) - contract(
        "ckgsx,gxq->cksq", real_rows, sin_x
    )
    kz_ids = z_index * cells_z + x_index * kz_share + jnp.arange(kz_share, dtype=jnp.int32)
    freq_z = signed_value(kz_ids, z_total)[:, None, None]
    freq_x = signed_value(every_x, x_total)[None, None, :]
    radius_sq = freq_x * freq_x + freq_z * freq_z
    at_anchor = radius_sq == 0.0
    safe_radius = jnp.sqrt(jnp.where(at_anchor, 1.0, radius_sq))
    unit_x = freq_x / safe_radius
    unit_z = freq_z / safe_radius
    anchor_term = jnp.where(at_anchor, float(x_total * z_total), 0.0)
    new_real = green_apply(spec_real, unit_x, unit_z, lame_ref, shear_ref)
    new_real = new_real + mean_strain[:, None, None, None] * anchor_term[None]
    new_imag = green_apply(spec_imag, unit_x, unit_z, lame_ref, shear_ref)
    back_real = contract("cksq,gxq->ckgsx", new_real, cos_x) - contract(
        "cksq,gxq->ckgsx", new_imag, sin_x
    )
    back_imag = contract("cksq,gxq->ckgsx", new_real, sin_x) + contract(
        "cksq,gxq->ckgsx", new_imag, cos_x
    )
    back_real = back_real.reshape(6, kz_share, x_devices * line_count)
    back_imag = back_imag.reshape(6, kz_share, x_devices * line_count)
    real_part, imag_part = (
        lax.all_to_all(back_real, "gx", split_axis=2, concat_axis=1, tiled=True),
        lax.all_to_all(back_imag, "gx", split_axis=2, concat_axis=1, tiled=True),
    )
    z_ids = jnp.arange(lax.axis_size("gz") * cells_z, dtype=jnp.int32)
    cos_table, sin_table = phases(own_block, z_ids, z_total)
    summed = lax.psum_scatter(
        contract("ckm,kz->zcm", real_part, cos_table)
        - contract("ckm,kz->zcm", imag_part, sin_table),
        "gz",
        scatter_dimension=0,
        tiled=True,
    )
    field_lines = jnp.transpose(summed, (1, 2, 0))
    strain_next = (field_lines * (1.0 / (x_total * z_total))).reshape(6, sections, cells_x, cells_z)
    stress_next = stress_law(strain_next, labels, cosine_tilt, sine_tilt, moduli)
    return (strain_next, stress_next)


def solution(mesh):
    in_specs = (P(None, None, "gx", "gz"), P(None, "gx", "gz"), P(None, "gx", "gz"), P(), P())
    out_specs = (P(None, None, "gx", "gz"), P(None, None, "gx", "gz"))

    def run(strain, labels, normals, moduli, mean_strain):
        _, sections, x_total, z_total = strain.shape
        parts, x_devices = mesh.shape["gz"], mesh.shape["gx"]
        grouped = (
            sections == 2
            and parts == len(GROUPS)
            and x_devices == 8
            and z_total == 128 * x_devices
            and x_total % (128 * x_devices) == 0
        )
        body = shards if grouped else shards_general
        mapped = jax.shard_map(body, mesh=mesh, in_specs=in_specs, out_specs=out_specs, check_vma=False)
        return mapped(strain, labels, normals, moduli, mean_strain)

    return run
```

```python
import functools
import math

import jax
import jax.numpy as jnp
import numpy as np
from jax import lax
from jax.experimental import pallas as pl
from jax.experimental.pallas import tpu as pltpu
from jax.sharding import PartitionSpec as P

ANGLES = 8
XX, YY, ZZ, YZ, XZ, XY = range(6)
GROUPS = (
    ((XY, 0), (YZ, 0)),
    ((XX, 0), (ZZ, 0), (XZ, 0)),
    ((XX, 1), (ZZ, 1), (XZ, 1)),
    ((XY, 1), (YZ, 1)),
)
INPLANE = (1, 2)
FIELDS = 3
CHUNKS = ((0, 2), (1,))
F32, BF16 = jnp.float32, jnp.bfloat16
MIB = 1 << 20


def split_table(table):
    table = np.asarray(table, np.float32)
    high = table.astype(jnp.bfloat16)
    low = (table - high.astype(np.float32)).astype(jnp.bfloat16)
    return jnp.asarray(np.stack([high, low]))


def half_frequencies(length):
    quarter = length // 4
    return (
        4 * np.arange(quarter) + 1,
        4 * np.arange(quarter // 2),
        4 * np.arange(quarter // 2) + 2,
    )


def interleave(real, imag, slots):
    rows, count = real.shape
    both = np.stack([real.reshape(rows, -1, slots), imag.reshape(rows, -1, slots)], 2)
    return both.reshape(rows, 2 * count)


def z_tables(length, slots, scale):
    quarter = length // 4
    z = np.arange(quarter, dtype=np.int64)[:, None]
    ones, zeros, twos = half_frequencies(length)

    def angles(freqs):
        return 2.0 * math.pi / length * ((z * freqs[None, :]) % length)

    one, zero, two = angles(ones), angles(zeros), angles(twos)
    top = interleave(np.cos(one), -np.sin(one), slots)
    bottom = interleave(-np.sin(one), -np.cos(one), slots)
    forward_one = np.concatenate([top, bottom], 0)
    real, imag = np.cos(zero), -np.sin(zero)
    imag[:, 0] = np.where(np.arange(quarter) % 2 == 0, 1.0, -1.0)
    forward_zero = interleave(real, imag, slots)
    forward_two = interleave(np.cos(two), -np.sin(two), slots)
    weight = 2.0 * scale
    inverse_one = weight * np.concatenate(
        [interleave(np.cos(one), -np.sin(one), slots), interleave(np.sin(one), np.cos(one), slots)], 0
    ).T
    half = np.full(quarter // 2, weight)
    half[0] = scale
    inverse_zero = interleave(real * half, imag * half, slots).T
    inverse_two = weight * forward_two.T

    def pack(first, second, third):
        return split_table(np.concatenate([first, np.concatenate([second, third], 1)], 0))

    return pack(forward_one, forward_zero, forward_two), pack(inverse_one, inverse_zero, inverse_two)


def x_tables(length):
    quarter = length // 4
    k = np.arange(quarter, dtype=np.int64)
    angle = 2.0 * math.pi / quarter * ((k[:, None] * k[None, :]) % quarter)
    turn = 2.0 * math.pi / length * k
    columns = [f(residue * turn) for residue in (1, 2, 3) for f in (np.cos, np.sin)]
    twiddles = jnp.asarray(np.stack(columns + columns[:2], 1).astype(np.float32))
    return split_table(np.concatenate([np.cos(angle), np.sin(angle)], 0)), twiddles


def halves(value):
    high = value.astype(BF16)
    return high, (value - high.astype(F32)).astype(BF16)


def dot(left, right):
    return jnp.dot(left, right, preferred_element_type=F32)


def dot_right(value, table, part):
    big = table.shape[2]
    half = big // 2
    rows = slice(0, big) if part == 0 else slice(big, big + half)
    columns = slice(0, big) if part == 0 else slice((part - 1) * half, part * half)
    high_table, low_table = table[0, rows, columns], table[1, rows, columns]
    high, low = halves(value)
    return dot(high, high_table) + (dot(low, high_table) + dot(high, low_table))


def dot_left(table, value):
    high, low = halves(value)
    return dot(table[0], high) + (dot(table[0], low) + dot(table[1], high))


def tilt(normals, section, cells_z):
    blocks = normals[section].astype(F32)
    count = blocks.shape[1]
    size = cells_z // count
    owner = lax.broadcasted_iota(jnp.int32, (count, cells_z), 1) // size
    own = lax.broadcasted_iota(jnp.int32, (count, cells_z), 0)
    spread = jnp.where(owner == own, 1.0, 0.0).astype(F32)
    angle = (math.pi / ANGLES) * dot(blocks, spread)
    cosine, sine = jnp.cos(angle), jnp.sin(angle)
    return cosine * cosine, sine * sine, cosine * sine


def law(strain, label, squares, lame, shear, stiff):
    cc, ss, cs = squares
    laminate = label == 1
    lame_local = jnp.where(laminate, lame[1], lame[0])
    twice_shear = jnp.where(laminate, 2.0 * shear[1], 2.0 * shear[0])
    spherical = lame_local * (strain[XX] + strain[YY] + strain[ZZ])
    normal = cc * strain[XX] + ss * strain[ZZ] + 2.0 * cs * strain[XZ]
    normal = jnp.where(laminate, stiff, 0.0) * normal
    return {
        XX: twice_shear * strain[XX] + spherical + normal * cc,
        YY: twice_shear * strain[YY] + spherical,
        ZZ: twice_shear * strain[ZZ] + spherical + normal * ss,
        YZ: twice_shear * strain[YZ],
        XZ: twice_shear * strain[XZ] + normal * cs,
        XY: twice_shear * strain[XY],
    }


def row_of(squares, block, size):
    return [jnp.broadcast_to(s[block : block + 1], (size, s.shape[1])) for s in squares]


def polarize_kernel(moduli_h, strain_h, labels_h, normals_h, *rest):
    outs, (held, strain, labels, normals, moduli, sems) = rest[:-6], rest[-6:]
    sections, cells_x, cells_z = labels.shape
    copies = [
        pltpu.make_async_copy(moduli_h, moduli, sems.at[0]),
        pltpu.make_async_copy(normals_h, normals, sems.at[1]),
    ]
    for k in range(sections):
        copies.append(pltpu.make_async_copy(labels_h.at[k], labels.at[k], sems.at[2 + 2 * k]))
        copies.append(pltpu.make_async_copy(strain_h.at[:, k], strain.at[:, k], sems.at[3 + 2 * k]))
    for copy in copies:
        copy.start()
    for copy in copies[:2]:
        copy.wait()
    parts = len(GROUPS)
    place = lax.axis_index("gz")
    size = cells_x // normals.shape[1]
    lame_ref = 0.5 * (moduli[0] + moduli[2])
    shear_ref = 0.5 * (moduli[1] + moduli[3])
    lame = (moduli[0] - lame_ref, moduli[2] - lame_ref)
    shear = (moduli[1] - shear_ref, moduli[3] - shear_ref)
    for group, fields in enumerate(GROUPS):
        if len(fields) < 3:
            held[group, 2] = jnp.zeros((cells_x, cells_z), F32)
    for section in range(sections):
        copies[2 + 2 * section].wait()
        copies[3 + 2 * section].wait()
        squares = tilt(normals, section, cells_z)
        for block in range(cells_x // size):
            rows = pl.ds(block * size, size)
            local = [strain[c, section, rows, :] for c in range(6)]
            value = law(local, labels[section, rows, :], row_of(squares, block, size), lame, shear, moduli[4])
            for group, fields in enumerate(GROUPS):
                for slot, (component, of) in enumerate(fields):
                    if of == section:
                        held[group, slot, rows, :] = value[component]
    for step in range(parts):
        target = lax.rem(place + step, parts)
        for slot in range(FIELDS):
            outs[slot * parts + step][...] = held[target, slot]


def deal(blocks, own, swapped):
    mine = lax.axis_index("gx")
    chip, core = mine // 2, lax.rem(mine, 2)
    for step in range(own.shape[0]):
        there = 2 * lax.bitwise_xor(chip, step)
        own[step] = blocks[there + core, 0]
        swapped[step] = blocks[there + 1 - core, 0]


def collect(own, got, moved, blocks):
    mine = lax.axis_index("gx")
    chip, core = mine // 2, lax.rem(mine, 2)
    for step in range(own.shape[0]):
        there = 2 * lax.bitwise_xor(chip, step)
        blocks[there + core, 0] = own[0] if step == 0 else moved[step - 1][0]
        blocks[there + 1 - core, 0] = got[0] if step == 0 else moved[step - 1][1]


def merge_kernel(own, got, *outs):
    for k, out in enumerate(outs):
        out[0] = own[k + 1]
        out[1] = got[k + 1]


def z_forward_deal_kernel(table, *rest):
    arrived, (own, swapped, held, blocks) = rest[:-4], rest[-4:]
    z_forward_kernel(table, *arrived, blocks, held)
    deal(blocks, own, swapped)


def z_inverse_collect_kernel(table, own, got, *rest):
    chips = own.shape[0]
    moved, outs, (held, blocks) = rest[: chips - 1], rest[chips - 1 : -2], rest[-2:]
    collect(own, got, moved, blocks)
    z_inverse_kernel(table, blocks, *outs, held)


def z_forward_kernel(table, *rest):
    parts = len(GROUPS)
    arrived, (out, held) = rest[:-2], rest[-2:]
    place = lax.axis_index("gz")
    for step in range(parts):
        source = lax.rem(place + parts - step, parts)
        for slot in range(held.shape[1]):
            held[source, slot] = arrived[slot * parts + step][...]
    fields, rows, width = held.shape[1:]
    lanes = out.shape[3]
    z0, z1, z2, z3 = (held[k].reshape(fields * rows, width) for k in range(parts))
    first = jnp.concatenate([z0 - z2, z1 - z3], 1)
    even, odd = z0 + z2, z1 + z3
    spectra = (
        dot_right(first, table, 0),
        dot_right(even + odd, table, 1),
        dot_right(even - odd, table, 2),
    )
    target = 0
    for spectrum in spectra:
        for k in range(spectrum.shape[1] // lanes):
            out[target] = spectrum[:, k * lanes : (k + 1) * lanes].reshape(fields, rows, lanes)
            target += 1


def swap(value):
    lanes = value.shape[1]
    return jnp.concatenate([pltpu.roll(value[:, k : k + 128], 64, 1) for k in range(0, lanes, 128)], 1)


def turn_sign(width):
    lane = lax.broadcasted_iota(jnp.int32, (1, width), 1) % 128
    return jnp.where(lane < 64, 1.0, -1.0).astype(F32)


def twiddle(twiddles, residue, value, sign):
    if residue == 0:
        return value
    pick = 2 * (residue - 1)
    quarter = value.shape[0]
    cosine = jnp.broadcast_to(twiddles[:, pick : pick + 1], (quarter, 128))
    sine = jnp.broadcast_to(twiddles[:, pick + 1 : pick + 2], (quarter, 128)) * sign[:, :128]
    pieces = []
    for k in range(0, value.shape[1], 128):
        piece = value[:, k : k + 128]
        pieces.append(cosine * piece + sine * pltpu.roll(piece, 64, 1))
    return jnp.concatenate(pieces, 1)


def x_forward(data, table, twiddles):
    sources, fields, rows, lanes = data.shape
    quarter = sources * rows // 4
    per = sources // 4
    width = fields * lanes
    sign = turn_sign(width)
    block = [
        jnp.concatenate([data[a * per : (a + 1) * per, f].reshape(quarter, lanes) for f in range(fields)], 1)
        for a in range(4)
    ]
    even, odd = block[0] + block[2], block[1] + block[3]
    diff, turned = block[0] - block[2], sign * swap(block[1] - block[3])
    values = (even + odd, diff + turned, even - odd, diff - turned)
    values = [twiddle(twiddles, residue, value, sign) for residue, value in enumerate(values)]
    both = dot_left(table, jnp.concatenate(values, 1))
    for residue in range(4):
        columns = slice(residue * width, (residue + 1) * width)
        yield both[:quarter, columns] + sign * swap(both[quarter:, columns])


def x_inverse(spectra, table, twiddles, is_special, out):
    sources, fields, rows, lanes = out.shape
    quarter = sources * rows // 4
    per = sources // 4
    width = fields * lanes
    sign = turn_sign(spectra.shape[1])
    both = dot_left(table, spectra)
    both = both[:quarter] - sign * swap(both[quarter:])
    sign = sign[:, :width]

    def join(values):
        h0, h1, h2, h3 = [twiddle(twiddles, residue, value, -sign) for residue, value in enumerate(values)]
        even, odd = h0 + h2, h1 + h3
        diff, turned = h0 - h2, sign * swap(h1 - h3)
        return even + odd, diff - turned, even - odd, diff + turned

    packed = both[:, 4 * width :]
    unpacked = [packed]
    for residue in range(1, 4):
        pieces = [pltpu.roll(packed[:, k : k + lanes], lanes - residue, 1) for k in range(0, width, lanes)]
        unpacked.append(jnp.concatenate(pieces, 1))
    lane = lax.broadcasted_iota(jnp.int32, (1, width), 1) % lanes
    edge = jnp.logical_and(is_special, lane == lanes // 2)
    whole = join([both[:, residue * width : (residue + 1) * width] for residue in range(4)])
    for a, (value, other) in enumerate(zip(whole, join(unpacked))):
        final = jnp.where(edge, other, value)
        for f in range(fields):
            out[a * per : (a + 1) * per, f] = final[:, f * lanes : (f + 1) * lanes].reshape(per, rows, lanes)


def holds_edge(slots, z_cells):
    return lax.axis_index("gx") * slots == z_cells // 4


def x_forward_kernel(table, twiddles, data_h, out, data, sem):
    copy = pltpu.make_async_copy(data_h, data, sem)
    copy.start()
    copy.wait()
    fields, lanes = data.shape[1], data.shape[3]
    for residue, spectrum in enumerate(x_forward(data, table, twiddles)):
        for f in range(fields):
            out[residue, f] = spectrum[:, f * lanes : (f + 1) * lanes]


def green_rows(x_cells, z_cells, chunk, moduli, mean, load, new):
    quarter, lanes = new.shape[0], new.shape[1] // (5 * len(chunk))
    slots = lanes // 2
    place, mine = lax.axis_index("gz"), lax.axis_index("gx")
    inplane = functools.reduce(jnp.logical_or, [place == k for k in INPLANE])
    lame_ref = 0.5 * (moduli[0] + moduli[2])
    shear_ref = 0.5 * (moduli[1] + moduli[3])
    half_inverse = 0.5 / shear_ref
    coupling = (lame_ref + shear_ref) / (shear_ref * (lame_ref + 2.0 * shear_ref))
    c1 = jnp.where(inplane, coupling, 0.0)
    k1 = jnp.where(inplane, 2.0 * half_inverse, half_inverse)
    k2 = jnp.where(inplane, half_inverse, 0.0)
    ka = jnp.where(inplane, 0.0, half_inverse)
    total = float(x_cells * z_cells)
    means = (
        total * jnp.where(inplane, mean[XX], mean[XY]),
        total * jnp.where(inplane, mean[ZZ], mean[YZ]),
        total * mean[XZ],
    )

    def store(field, residue, rows, value):
        block = residue * len(chunk) + chunk.index(field)
        new[rows, block * lanes : (block + 1) * lanes] = value

    def green(kx, kz, odd_kx, s, anchored=False):
        radius = kx * kx + kz * kz
        if anchored:
            radius = jnp.where(radius == 0.0, 1.0, radius)
        inverse = 1.0 / radius
        a, b = kx * kx * inverse, kz * kz * inverse
        d = odd_kx * kz * inverse
        ab = c1 * (a * b)
        ca, cb = c1 * a, c1 * b
        h02, h12 = d * (ca - k2), d * (cb - k2)
        m01 = ab - ka * d
        twice = 2.0 * s[2]
        rows = (
            lambda: a * (ca - k1) * s[0] + m01 * s[1] + h02 * twice,
            lambda: m01 * s[0] + b * (cb - k1) * s[1] + h12 * twice,
            lambda: h02 * s[0] + h12 * s[1] + (2.0 * ab - k2) * s[2],
        )
        return {f: rows[f]() for f in chunk}

    lane = lax.broadcasted_iota(jnp.int32, (1, lanes), 1)
    slot_of = lane % slots
    order = mine * slots + slot_of
    zeros_at, twos_at = z_cells // 4, z_cells // 4 + z_cells // 8
    kz = jnp.where(
        order < zeros_at,
        4 * order + 1,
        jnp.where(order < twos_at, 4 * (order - zeros_at), 4 * (order - twos_at) + 2),
    )
    kz = jnp.where(kz < z_cells // 2, kz, kz - z_cells).astype(F32)
    special = order == zeros_at
    size = 32
    for start in range(0, quarter, size):
        rows = pl.ds(start, size)
        row = lax.broadcasted_iota(jnp.int32, (size, lanes), 0) + start
        full_kz = jnp.broadcast_to(kz, (size, lanes))
        first_kx = (4 * row - (x_cells if 2 * start >= quarter else 0)).astype(F32)
        mirror = 2 * start == quarter
        edge = [None] * FIELDS
        for residue in range(4):
            s = [load(f, residue, rows) for f in range(FIELDS)]
            for f in range(FIELDS):
                moved = s[f] if residue == 0 else pltpu.roll(s[f], residue, 1)
                edge[f] = moved if residue == 0 else jnp.where(slot_of == residue, moved, edge[f])
            kx = first_kx + float(residue)
            odd_kx = jnp.where(row == start, 0.0, kx) if mirror and residue == 0 else kx
            with_anchor = residue == 0 and start == 0
            fresh = green(kx, full_kz, odd_kx, s, with_anchor)
            if with_anchor:
                anchor = jnp.logical_and(row == 0, special)
                for f in chunk:
                    fresh[f] = jnp.where(anchor, jnp.where(lane < slots, means[f], 0.0), fresh[f])
            for f in chunk:
                store(f, residue, rows, fresh[f])
        kx = first_kx + slot_of.astype(F32)
        odd_kx = jnp.where(jnp.logical_and(row == start, slot_of == 0), kx, 0.0) if mirror else jnp.zeros_like(kx)
        fresh = green(kx, jnp.full((size, lanes), -0.5 * z_cells, F32), odd_kx, edge)
        for f in chunk:
            store(f, 4, rows, fresh[f])


def loader(chunks, early, late):
    def load(field, residue, rows):
        spectra, chunk = (early, chunks[0]) if field in chunks[0] else (late, chunks[1])
        return spectra[residue, chunk.index(field), rows, :]

    return load


def early_inverse_kernel(x_cells, z_cells, chunks, moduli, mean, table, twiddles, early, late, out, new):
    green_rows(x_cells, z_cells, chunks[0], moduli, mean, loader(chunks, early, late), new)
    x_inverse(new[...], table, twiddles, holds_edge(out.shape[3] // 2, z_cells), out)


def late_kernel(x_cells, z_cells, chunks, moduli, mean, table, twiddles, early, own_in, got, *rest):
    chips = own_in.shape[0]
    moved, rest = rest[: chips - 1], rest[chips - 1 :]
    own_out, swapped, late, data, out, new = rest
    collect(own_in, got, moved, data)
    lanes = data.shape[3]
    for residue, spectrum in enumerate(x_forward(data, table, twiddles)):
        for slot in range(data.shape[1]):
            late[residue, slot] = spectrum[:, slot * lanes : (slot + 1) * lanes]
    green_rows(x_cells, z_cells, chunks[1], moduli, mean, loader(chunks, early, late), new)
    x_inverse(new[...], table, twiddles, holds_edge(lanes // 2, z_cells), out)
    deal(out, own_out, swapped)


def z_inverse_kernel(table, data, *rest):
    outs, held = rest[:-1], rest[-1]
    parts = len(GROUPS)
    place = lax.axis_index("gz")
    sources, fields, rows, lanes = data.shape
    half = sources // 2
    fourth = sources // 4

    def columns(begin, end):
        return jnp.concatenate([data[k].reshape(fields * rows, lanes) for k in range(begin, end)], 1)

    first = dot_right(columns(0, half), table, 0)
    zero = dot_right(columns(half, half + fourth), table, 1)
    two = dot_right(columns(half + fourth, sources), table, 2)
    width = zero.shape[1]
    real, imag = first[:, :width], first[:, width:]
    plus, minus = zero + two, zero - two
    for k, value in enumerate((plus + real, minus - imag, plus - real, minus + imag)):
        held[k] = value.reshape(fields, rows, width)
    for step in range(parts):
        target = lax.rem(place + step, parts)
        for slot in range(fields):
            outs[slot * parts + step][...] = held[target, slot]


def stress_kernel(slots, strain_parts, stress_parts, moduli, mean, labels, normals, *rest):
    parts = len(GROUPS)
    arrived = rest[: len(slots) * parts]
    strain_to, stress_to, held, strain_out, stress_out, sems = rest[-6:]
    place = lax.axis_index("gz")
    sections, cells_x, cells_z = labels.shape
    size = cells_x // normals.shape[1]
    for step in range(parts):
        source = lax.rem(place + parts - step, parts)
        for k, slot in enumerate(slots):
            held[source, slot] = arrived[k * parts + step][...]
    copies = []
    for section in range(sections):
        squares = tilt(normals, section, cells_z)
        for block in range(cells_x // size):
            rows = pl.ds(block * size, size)
            local = {c: jnp.zeros((size, cells_z), F32) for c in range(6)}
            local[YY] = jnp.full((size, cells_z), mean[YY], F32)
            for group, fields in enumerate(GROUPS):
                for slot, (component, of) in enumerate(fields):
                    if of == section and slot in slots:
                        local[component] = held[group, slot, rows, :]
            value = law(
                local,
                labels[section, rows, :],
                row_of(squares, block, size),
                (moduli[0], moduli[2]),
                (moduli[1], moduli[3]),
                moduli[4],
            )
            for component in strain_parts:
                strain_out[component, section, rows, :] = local[component]
            for component in stress_parts:
                stress_out[component, section, rows, :] = value[component]
        for here, there, chosen in ((strain_out, strain_to, strain_parts), (stress_out, stress_to, stress_parts)):
            for c in chosen:
                copy = pltpu.make_async_copy(here.at[c, section], there.at[c, section], sems.at[len(copies)])
                copy.start()
                copies.append(copy)
    for copy in copies:
        copy.wait()


def call(kernel, outs, scratch, args, limit, hbm=(), smem=0, hbm_out=(), aliases={}):
    def space(k):
        return pltpu.HBM if k in hbm else pltpu.SMEM if k < smem else pltpu.VMEM

    args = [pltpu.with_memory_space_constraint(a, pltpu.HBM) if k in hbm else a for k, a in enumerate(args)]
    moved = sum(a.size * a.dtype.itemsize for a in args) + sum(math.prod(o) * 4 for o in outs)
    return pl.pallas_call(
        kernel,
        out_shape=[
            pltpu.HBM(o, F32) if k in hbm_out else jax.ShapeDtypeStruct(o, F32) for k, o in enumerate(outs)
        ],
        in_specs=[pl.BlockSpec(memory_space=space(k)) for k in range(len(args))],
        out_specs=[
            pl.BlockSpec(memory_space=pltpu.HBM if k in hbm_out else pltpu.VMEM) for k in range(len(outs))
        ],
        scratch_shapes=scratch,
        input_output_aliases=aliases,
        compiler_params=pltpu.CompilerParams(vmem_limit_bytes=limit * MIB),
        cost_estimate=pl.CostEstimate(flops=0, bytes_accessed=moved, transcendentals=0),
    )(*args)


def shards(strain, labels, normals, moduli, mean_strain):
    parts = lax.axis_size("gz")
    x_devices = lax.axis_size("gx")
    _, sections, cells_x, cells_z = strain.shape
    x_total, z_total = cells_x * x_devices, cells_z * parts
    slots = z_total // 2 // x_devices
    lanes = 2 * slots
    z_fwd, z_inv = z_tables(z_total, slots, 1.0 / (x_total * z_total))
    x_tab = x_tables(x_total)
    block = (cells_x, cells_z)
    everyone = range(parts)

    def travel(field, blocks, gather):
        ends = INPLANE if field == 2 else everyone
        moved = [blocks[0]]
        for step in range(1, parts):
            way = [(k, (k + step) % parts) for k in range(parts)]
            way = [(a, b) for a, b in way if (b if gather else a) in ends]
            moved.append(lax.ppermute(blocks[step], "gz", way))
        return moved

    def held(fields):
        return pltpu.VMEM((parts, fields, cells_x, cells_z), F32)

    blocks = call(
        polarize_kernel,
        [block] * (FIELDS * parts),
        [
            held(FIELDS),
            pltpu.VMEM(strain.shape, F32),
            pltpu.VMEM(labels.shape, jnp.int32),
            pltpu.VMEM(normals.shape, jnp.int32),
            pltpu.SMEM(moduli.shape, F32),
            pltpu.SemaphoreType.DMA((2 + 2 * sections,)),
        ],
        (moduli, strain, labels, normals),
        16,
        range(4),
    )
    blocks = {f: list(blocks[f * parts : (f + 1) * parts]) for f in range(FIELDS)}
    quarter = x_total // 4
    chips = x_devices // 2
    early, late = CHUNKS
    size = len(early)
    grid = (x_devices, size, cells_x, lanes)
    tile = (chips, cells_x, lanes)
    tiles = pltpu.VMEM((x_devices, 1, cells_x, lanes), F32)

    def exchange(own, swapped, after):
        got = lax.ppermute(swapped, "gx", [(k, k ^ 1) for k in range(x_devices)])
        merged = call(merge_kernel, [(2, cells_x, lanes)] * (chips - 1), [], (own, got), 8)
        merged, after = lax.optimization_barrier((merged, after))
        moved = [
            lax.ppermute(block, "gx", [(k, k ^ (2 * step)) for k in range(x_devices)])
            for step, block in enumerate(merged, 1)
        ]
        return (own, got, *moved), after

    args = [a for f in early for a in travel(f, blocks[f], True)]
    args, blocks = lax.optimization_barrier((args, blocks))
    (rows,) = call(z_forward_kernel, [grid], [held(size)], (z_fwd, *args), 16)
    rows = lax.all_to_all(rows, "gx", 0, 0, tiled=True)
    args = travel(late[0], blocks[late[0]], True)
    args, rows = lax.optimization_barrier((args, rows))
    own, swapped = call(z_forward_deal_kernel, [tile] * 2, [held(1), tiles], (z_fwd, *args), 16)
    last, rows = exchange(own, swapped, rows)
    copied = [pltpu.VMEM(grid, F32), pltpu.SemaphoreType.DMA]
    (spectrum,) = call(x_forward_kernel, [(4, size, quarter, lanes)], copied, (*x_tab, rows), 24, (2,))
    own, swapped, late_spectrum = call(
        functools.partial(late_kernel, x_total, z_total, CHUNKS),
        [tile, tile, (4, 1, quarter, lanes)],
        [tiles, tiles, pltpu.VMEM((quarter, 5 * lanes), F32)],
        (moduli, mean_strain, *x_tab, spectrum, *last),
        24,
        smem=2,
    )
    last, late_spectrum = exchange(own, swapped, late_spectrum)
    (rest,) = call(
        functools.partial(early_inverse_kernel, x_total, z_total, CHUNKS),
        [grid],
        [pltpu.VMEM((quarter, 5 * size * lanes), F32)],
        (moduli, mean_strain, *x_tab, spectrum, late_spectrum),
        24,
        smem=2,
    )
    blocks = call(z_inverse_collect_kernel, [block] * parts, [held(1), tiles], (z_inv, *last), 16)
    rest, blocks = lax.optimization_barrier((rest, list(blocks)))
    rest = lax.all_to_all(rest, "gx", 0, 0, tiled=True)
    arrived = {late[0]: travel(late[0], blocks, False)}
    blocks = call(z_inverse_kernel, [block] * (size * parts), [held(size)], (z_inv, rest), 16)
    for slot, f in enumerate(early):
        arrived[f] = travel(f, blocks[slot * parts : (slot + 1) * parts], False)
    full = (6, sections, cells_x, cells_z)
    results = ()
    for slots, strains, stresses in (((0, 1), (XX, YY, ZZ, YZ, XY), (YY, YZ, XY)), ((0, 1, 2), (XZ,), (XX, ZZ, XZ))):
        args = (moduli, mean_strain, labels, normals, *[a for f in slots for a in arrived[f]], *results)
        hbm = range(len(args) - len(results), len(args))
        count = sections * (len(strains) + len(stresses))
        results = call(
            functools.partial(stress_kernel, slots, strains, stresses),
            [full, full],
            [held(FIELDS), pltpu.VMEM(full, F32), pltpu.VMEM(full, F32), pltpu.SemaphoreType.DMA((count,))],
            args,
            16,
            hbm,
            smem=2,
            hbm_out=(0, 1),
            aliases={k: out for out, k in enumerate(hbm)},
        )
    return tuple(results)


def orientation(normals, blk):
    tilt_angle = math.pi / ANGLES * normals.astype(jnp.float32)
    tilt_angle = jnp.repeat(jnp.repeat(tilt_angle, blk, axis=1), blk, axis=2)
    return (jnp.cos(tilt_angle), jnp.sin(tilt_angle))


def stress_law(strain_field, labels, cosine_tilt, sine_tilt, moduli):
    laminate = labels == 1
    lame_local = jnp.where(laminate, moduli[2], moduli[0])
    shear_local = jnp.where(laminate, moduli[3], moduli[1])
    trace_sum = strain_field[0] + strain_field[1] + strain_field[2]
    normal_part = (
        cosine_tilt * cosine_tilt * strain_field[0]
        + sine_tilt * sine_tilt * strain_field[2]
        + 2.0 * cosine_tilt * sine_tilt * strain_field[4]
    )
    laminate_term = moduli[4] * labels.astype(jnp.float32) * normal_part
    dyad = [
        cosine_tilt * cosine_tilt,
        None,
        sine_tilt * sine_tilt,
        None,
        cosine_tilt * sine_tilt,
        None,
    ]
    result = []
    for slot in range(6):
        value = 2.0 * shear_local * strain_field[slot]
        if slot < 3:
            value = value + lame_local * trace_sum
        if dyad[slot] is not None:
            value = value + laminate_term * dyad[slot]
        result.append(value)
    return jnp.stack(result)


def polarize(stresses, strain_field, lame_ref, shear_ref):
    trace_sum = strain_field[0] + strain_field[1] + strain_field[2]
    result = []
    for slot in range(6):
        value = stresses[slot] - 2.0 * shear_ref * strain_field[slot]
        if slot < 3:
            value = value - lame_ref * trace_sum
        result.append(value)
    return jnp.stack(result)


def green_apply(spectrum, unit_x, unit_z, lame_ref, shear_ref):
    coupling = (lame_ref + shear_ref) / (shear_ref * (lame_ref + 2.0 * shear_ref))
    traction_x = spectrum[0] * unit_x + spectrum[4] * unit_z
    traction_y = spectrum[5] * unit_x + spectrum[3] * unit_z
    traction_z = spectrum[4] * unit_x + spectrum[2] * unit_z
    normal_load = unit_x * traction_x + unit_z * traction_z
    half_inverse = 0.5 / shear_ref
    result = [
        2.0 * half_inverse * unit_x * traction_x - coupling * normal_load * unit_x * unit_x,
        jnp.zeros_like(traction_x),
        2.0 * half_inverse * unit_z * traction_z - coupling * normal_load * unit_z * unit_z,
        half_inverse * unit_z * traction_y,
        half_inverse * (unit_z * traction_x + unit_x * traction_z)
        - coupling * normal_load * unit_x * unit_z,
        half_inverse * unit_x * traction_y,
    ]
    return -jnp.stack(result)


def phases(left_ids, right_ids, length):
    product = left_ids[:, None] * right_ids[None, :] % length
    phase_angle = 2.0 * math.pi / length * product.astype(jnp.float32)
    return (jnp.cos(phase_angle), jnp.sin(phase_angle))


def contract(form, left_side, right_side):
    return jnp.einsum(
        form,
        left_side,
        right_side,
        precision=lax.Precision.HIGHEST,
        preferred_element_type=jnp.float32,
    )


def signed_value(counter, length):
    return jnp.where(counter < length // 2, counter, counter - length).astype(jnp.float32)


def shards_general(strain, labels, normals, moduli, mean_strain):
    z_devices = lax.axis_size("gz")
    x_devices = lax.axis_size("gx")
    z_index = lax.axis_index("gz")
    x_index = lax.axis_index("gx")
    sections = strain.shape[1]
    cells_x = strain.shape[2]
    cells_z = strain.shape[3]
    x_total = cells_x * x_devices
    z_total = cells_z * z_devices
    line_count = sections * cells_x
    kz_share = cells_z // x_devices
    cosine_tilt, sine_tilt = orientation(normals, strain.shape[2] // normals.shape[1])
    lame_ref = 0.5 * (moduli[0] + moduli[2])
    shear_ref = 0.5 * (moduli[1] + moduli[3])
    stresses = stress_law(strain, labels, cosine_tilt, sine_tilt, moduli)
    polarized = polarize(stresses, strain, lame_ref, shear_ref)
    flattened = polarized.reshape(6, line_count, cells_z)
    own_block = z_index * cells_z + jnp.arange(cells_z, dtype=jnp.int32)
    empty_sum = jnp.zeros((6, cells_z, line_count), jnp.float32)
    pieces = lax.all_gather(flattened, "gz", axis=2, tiled=True)
    z_ids = jnp.arange(pieces.shape[2], dtype=jnp.int32)
    cos_table, sin_table = phases(z_ids, own_block, z_total)
    real_part = contract("cmz,zk->ckm", pieces, cos_table)
    imag_part = (empty_sum, empty_sum)[1] - contract("cmz,zk->ckm", pieces, sin_table)
    real_rows, imag_rows = (
        lax.all_to_all(real_part, "gx", split_axis=1, concat_axis=2, tiled=True),
        lax.all_to_all(imag_part, "gx", split_axis=1, concat_axis=2, tiled=True),
    )
    grid_shape = (6, kz_share, x_devices, sections, cells_x)
    real_rows = real_rows.reshape(grid_shape)
    imag_rows = imag_rows.reshape(grid_shape)
    every_x = jnp.arange(x_total, dtype=jnp.int32)
    cos_x, sin_x = phases(every_x, every_x, x_total)
    cos_x = cos_x.reshape(x_devices, cells_x, x_total)
    sin_x = sin_x.reshape(x_devices, cells_x, x_total)
    spec_real = contract("ckgsx,gxq->cksq", real_rows, cos_x) + contract(
        "ckgsx,gxq->cksq", imag_rows, sin_x
    )
    spec_imag = contract("ckgsx,gxq->cksq", imag_rows, cos_x) - contract(
        "ckgsx,gxq->cksq", real_rows, sin_x
    )
    kz_ids = z_index * cells_z + x_index * kz_share + jnp.arange(kz_share, dtype=jnp.int32)
    freq_z = signed_value(kz_ids, z_total)[:, None, None]
    freq_x = signed_value(every_x, x_total)[None, None, :]
    radius_sq = freq_x * freq_x + freq_z * freq_z
    at_anchor = radius_sq == 0.0
    safe_radius = jnp.sqrt(jnp.where(at_anchor, 1.0, radius_sq))
    unit_x = freq_x / safe_radius
    unit_z = freq_z / safe_radius
    anchor_term = jnp.where(at_anchor, float(x_total * z_total), 0.0)
    new_real = green_apply(spec_real, unit_x, unit_z, lame_ref, shear_ref)
    new_real = new_real + mean_strain[:, None, None, None] * anchor_term[None]
    new_imag = green_apply(spec_imag, unit_x, unit_z, lame_ref, shear_ref)
    back_real = contract("cksq,gxq->ckgsx", new_real, cos_x) - contract(
        "cksq,gxq->ckgsx", new_imag, sin_x
    )
    back_imag = contract("cksq,gxq->ckgsx", new_real, sin_x) + contract(
        "cksq,gxq->ckgsx", new_imag, cos_x
    )
    back_real = back_real.reshape(6, kz_share, x_devices * line_count)
    back_imag = back_imag.reshape(6, kz_share, x_devices * line_count)
    real_part, imag_part = (
        lax.all_to_all(back_real, "gx", split_axis=2, concat_axis=1, tiled=True),
        lax.all_to_all(back_imag, "gx", split_axis=2, concat_axis=1, tiled=True),
    )
    z_ids = jnp.arange(lax.axis_size("gz") * cells_z, dtype=jnp.int32)
    cos_table, sin_table = phases(own_block, z_ids, z_total)
    summed = lax.psum_scatter(
        contract("ckm,kz->zcm", real_part, cos_table)
        - contract("ckm,kz->zcm", imag_part, sin_table),
        "gz",
        scatter_dimension=0,
        tiled=True,
    )
    field_lines = jnp.transpose(summed, (1, 2, 0))
    strain_next = (field_lines * (1.0 / (x_total * z_total))).reshape(6, sections, cells_x, cells_z)
    stress_next = stress_law(strain_next, labels, cosine_tilt, sine_tilt, moduli)
    return (strain_next, stress_next)


def solution(mesh):
    in_specs = (P(None, None, "gx", "gz"), P(None, "gx", "gz"), P(None, "gx", "gz"), P(), P())
    out_specs = (P(None, None, "gx", "gz"), P(None, None, "gx", "gz"))

    def run(strain, labels, normals, moduli, mean_strain):
        _, sections, x_total, z_total = strain.shape
        parts, x_devices = mesh.shape["gz"], mesh.shape["gx"]
        grouped = (
            sections == 2
            and parts == len(GROUPS)
            and x_devices == 8
            and z_total == 128 * x_devices
            and x_total % (128 * x_devices) == 0
        )
        body = shards if grouped else shards_general
        mapped = jax.shard_map(body, mesh=mesh, in_specs=in_specs, out_specs=out_specs, check_vma=False)
        return mapped(strain, labels, normals, moduli, mean_strain)

    return run
```

```python
import functools
import math

import jax
import jax.numpy as jnp
import numpy as np
from jax import lax
from jax.experimental import pallas as pl
from jax.experimental.pallas import tpu as pltpu
from jax.sharding import PartitionSpec as P

ANGLES = 8
XX, YY, ZZ, YZ, XZ, XY = range(6)
GROUPS = (
    ((XY, 0), (YZ, 0)),
    ((XX, 0), (ZZ, 0), (XZ, 0)),
    ((XX, 1), (ZZ, 1), (XZ, 1)),
    ((XY, 1), (YZ, 1)),
)
INPLANE = (1, 2)
FIELDS = 3
CHUNKS = ((0, 2), (1,))
F32, BF16 = jnp.float32, jnp.bfloat16
MIB = 1 << 20


def split_table(table):
    table = np.asarray(table, np.float32)
    high = table.astype(jnp.bfloat16)
    low = (table - high.astype(np.float32)).astype(jnp.bfloat16)
    return jnp.asarray(np.stack([high, low]))


def half_frequencies(length):
    quarter = length // 4
    return (
        4 * np.arange(quarter) + 1,
        4 * np.arange(quarter // 2),
        4 * np.arange(quarter // 2) + 2,
    )


def interleave(real, imag, slots):
    rows, count = real.shape
    both = np.stack([real.reshape(rows, -1, slots), imag.reshape(rows, -1, slots)], 2)
    return both.reshape(rows, 2 * count)


def z_tables(length, slots, scale):
    quarter = length // 4
    z = np.arange(quarter, dtype=np.int64)[:, None]
    ones, zeros, twos = half_frequencies(length)

    def angles(freqs):
        return 2.0 * math.pi / length * ((z * freqs[None, :]) % length)

    one, zero, two = angles(ones), angles(zeros), angles(twos)
    top = interleave(np.cos(one), -np.sin(one), slots)
    bottom = interleave(-np.sin(one), -np.cos(one), slots)
    forward_one = np.concatenate([top, bottom], 0)
    real, imag = np.cos(zero), -np.sin(zero)
    imag[:, 0] = np.where(np.arange(quarter) % 2 == 0, 1.0, -1.0)
    forward_zero = interleave(real, imag, slots)
    forward_two = interleave(np.cos(two), -np.sin(two), slots)
    weight = 2.0 * scale
    inverse_one = weight * np.concatenate(
        [interleave(np.cos(one), -np.sin(one), slots), interleave(np.sin(one), np.cos(one), slots)], 0
    ).T
    half = np.full(quarter // 2, weight)
    half[0] = scale
    inverse_zero = interleave(real * half, imag * half, slots).T
    inverse_two = weight * forward_two.T

    def pack(first, second, third):
        return split_table(np.concatenate([first, np.concatenate([second, third], 1)], 0))

    return pack(forward_one, forward_zero, forward_two), pack(inverse_one, inverse_zero, inverse_two)


def x_tables(length):
    quarter = length // 4
    k = np.arange(quarter, dtype=np.int64)
    angle = 2.0 * math.pi / quarter * ((k[:, None] * k[None, :]) % quarter)
    turn = 2.0 * math.pi / length * k
    columns = [f(residue * turn) for residue in (1, 2, 3) for f in (np.cos, np.sin)]
    twiddles = jnp.asarray(np.stack(columns + columns[:2], 1).astype(np.float32))
    return split_table(np.concatenate([np.cos(angle), np.sin(angle)], 0)), twiddles


def halves(value):
    high = value.astype(BF16)
    return high, (value - high.astype(F32)).astype(BF16)


def dot(left, right):
    return jnp.dot(left, right, preferred_element_type=F32)


def dot_right(value, table, part):
    big = table.shape[2]
    half = big // 2
    rows = slice(0, big) if part == 0 else slice(big, big + half)
    columns = slice(0, big) if part == 0 else slice((part - 1) * half, part * half)
    high_table, low_table = table[0, rows, columns], table[1, rows, columns]
    high, low = halves(value)
    return dot(high, high_table) + (dot(low, high_table) + dot(high, low_table))


def dot_left(table, value):
    high, low = halves(value)
    return dot(table[0], high) + (dot(table[0], low) + dot(table[1], high))


def tilt(normals, section, cells_z):
    blocks = normals[section].astype(F32)
    count = blocks.shape[1]
    size = cells_z // count
    owner = lax.broadcasted_iota(jnp.int32, (count, cells_z), 1) // size
    own = lax.broadcasted_iota(jnp.int32, (count, cells_z), 0)
    spread = jnp.where(owner == own, 1.0, 0.0).astype(F32)
    angle = (math.pi / ANGLES) * dot(blocks, spread)
    cosine, sine = jnp.cos(angle), jnp.sin(angle)
    return cosine * cosine, sine * sine, cosine * sine


def law(strain, label, squares, lame, shear, stiff):
    cc, ss, cs = squares
    laminate = label == 1
    lame_local = jnp.where(laminate, lame[1], lame[0])
    twice_shear = jnp.where(laminate, 2.0 * shear[1], 2.0 * shear[0])
    spherical = lame_local * (strain[XX] + strain[YY] + strain[ZZ])
    normal = cc * strain[XX] + ss * strain[ZZ] + 2.0 * cs * strain[XZ]
    normal = jnp.where(laminate, stiff, 0.0) * normal
    return {
        XX: twice_shear * strain[XX] + spherical + normal * cc,
        YY: twice_shear * strain[YY] + spherical,
        ZZ: twice_shear * strain[ZZ] + spherical + normal * ss,
        YZ: twice_shear * strain[YZ],
        XZ: twice_shear * strain[XZ] + normal * cs,
        XY: twice_shear * strain[XY],
    }


def row_of(squares, block, size):
    return [jnp.broadcast_to(s[block : block + 1], (size, s.shape[1])) for s in squares]


def polarize_kernel(moduli_h, strain_h, labels_h, normals_h, *rest):
    outs, (held, strain, labels, normals, moduli, sems) = rest[:-6], rest[-6:]
    sections, cells_x, cells_z = labels.shape
    copies = [
        pltpu.make_async_copy(moduli_h, moduli, sems.at[0]),
        pltpu.make_async_copy(normals_h, normals, sems.at[1]),
    ]
    for k in range(sections):
        copies.append(pltpu.make_async_copy(labels_h.at[k], labels.at[k], sems.at[2 + 2 * k]))
        copies.append(pltpu.make_async_copy(strain_h.at[:, k], strain.at[:, k], sems.at[3 + 2 * k]))
    for copy in copies:
        copy.start()
    for copy in copies[:2]:
        copy.wait()
    parts = len(GROUPS)
    place = lax.axis_index("gz")
    size = cells_x // normals.shape[1]
    lame_ref = 0.5 * (moduli[0] + moduli[2])
    shear_ref = 0.5 * (moduli[1] + moduli[3])
    lame = (moduli[0] - lame_ref, moduli[2] - lame_ref)
    shear = (moduli[1] - shear_ref, moduli[3] - shear_ref)
    for group, fields in enumerate(GROUPS):
        if len(fields) < 3:
            held[group, 2] = jnp.zeros((cells_x, cells_z), F32)
    for section in range(sections):
        copies[2 + 2 * section].wait()
        copies[3 + 2 * section].wait()
        squares = tilt(normals, section, cells_z)
        for block in range(cells_x // size):
            rows = pl.ds(block * size, size)
            local = [strain[c, section, rows, :] for c in range(6)]
            value = law(local, labels[section, rows, :], row_of(squares, block, size), lame, shear, moduli[4])
            for group, fields in enumerate(GROUPS):
                for slot, (component, of) in enumerate(fields):
                    if of == section:
                        held[group, slot, rows, :] = value[component]
    for step in range(parts):
        target = lax.rem(place + step, parts)
        for slot in range(FIELDS):
            outs[slot * parts + step][...] = held[target, slot]


def deal(blocks, own, swapped):
    mine = lax.axis_index("gx")
    chip, core = mine // 2, lax.rem(mine, 2)
    for step in range(own.shape[0]):
        there = 2 * lax.bitwise_xor(chip, step)
        own[step] = blocks[there + core]
        swapped[step] = blocks[there + 1 - core]


def collect(own, got, moved, blocks):
    mine = lax.axis_index("gx")
    chip, core = mine // 2, lax.rem(mine, 2)
    for step in range(own.shape[0]):
        there = 2 * lax.bitwise_xor(chip, step)
        blocks[there + core] = own[0] if step == 0 else moved[step - 1][0]
        blocks[there + 1 - core] = got[0] if step == 0 else moved[step - 1][1]


def merge_kernel(own, got, *outs):
    for k, out in enumerate(outs):
        out[0] = own[k + 1]
        out[1] = got[k + 1]


def z_forward_deal_kernel(table, *rest):
    arrived, (own, swapped, held, blocks) = rest[:-4], rest[-4:]
    z_forward_kernel(table, *arrived, blocks, held)
    deal(blocks, own, swapped)


def z_inverse_collect_kernel(table, own, got, *rest):
    chips = own.shape[0]
    moved, outs, (held, blocks) = rest[: chips - 1], rest[chips - 1 : -2], rest[-2:]
    collect(own, got, moved, blocks)
    z_inverse_kernel(table, blocks, *outs, held)


def z_forward_kernel(table, *rest):
    parts = len(GROUPS)
    arrived, (out, held) = rest[:-2], rest[-2:]
    place = lax.axis_index("gz")
    for step in range(parts):
        source = lax.rem(place + parts - step, parts)
        for slot in range(held.shape[1]):
            held[source, slot] = arrived[slot * parts + step][...]
    fields, rows, width = held.shape[1:]
    lanes = out.shape[3]
    z0, z1, z2, z3 = (held[k].reshape(fields * rows, width) for k in range(parts))
    first = jnp.concatenate([z0 - z2, z1 - z3], 1)
    even, odd = z0 + z2, z1 + z3
    spectra = (
        dot_right(first, table, 0),
        dot_right(even + odd, table, 1),
        dot_right(even - odd, table, 2),
    )
    target = 0
    for spectrum in spectra:
        for k in range(spectrum.shape[1] // lanes):
            out[target] = spectrum[:, k * lanes : (k + 1) * lanes].reshape(fields, rows, lanes)
            target += 1


def swap(value):
    lanes = value.shape[1]
    return jnp.concatenate([pltpu.roll(value[:, k : k + 128], 64, 1) for k in range(0, lanes, 128)], 1)


def turn_sign(width):
    lane = lax.broadcasted_iota(jnp.int32, (1, width), 1) % 128
    return jnp.where(lane < 64, 1.0, -1.0).astype(F32)


def twiddle(twiddles, residue, value, sign):
    if residue == 0:
        return value
    pick = 2 * (residue - 1)
    quarter = value.shape[0]
    cosine = jnp.broadcast_to(twiddles[:, pick : pick + 1], (quarter, 128))
    sine = jnp.broadcast_to(twiddles[:, pick + 1 : pick + 2], (quarter, 128)) * sign[:, :128]
    pieces = []
    for k in range(0, value.shape[1], 128):
        piece = value[:, k : k + 128]
        pieces.append(cosine * piece + sine * pltpu.roll(piece, 64, 1))
    return jnp.concatenate(pieces, 1)


def x_forward(data, table, twiddles):
    sources, fields, rows, lanes = data.shape
    quarter = sources * rows // 4
    per = sources // 4
    width = fields * lanes
    sign = turn_sign(width)
    block = [
        jnp.concatenate([data[a * per : (a + 1) * per, f].reshape(quarter, lanes) for f in range(fields)], 1)
        for a in range(4)
    ]
    even, odd = block[0] + block[2], block[1] + block[3]
    diff, turned = block[0] - block[2], sign * swap(block[1] - block[3])
    values = (even + odd, diff + turned, even - odd, diff - turned)
    values = [twiddle(twiddles, residue, value, sign) for residue, value in enumerate(values)]
    both = dot_left(table, jnp.concatenate(values, 1))
    for residue in range(4):
        columns = slice(residue * width, (residue + 1) * width)
        yield both[:quarter, columns] + sign * swap(both[quarter:, columns])


def x_inverse(spectra, table, twiddles, is_special, out):
    sources, fields, rows, lanes = out.shape
    quarter = sources * rows // 4
    per = sources // 4
    width = fields * lanes
    sign = turn_sign(spectra.shape[1])
    both = dot_left(table, spectra)
    both = both[:quarter] - sign * swap(both[quarter:])
    sign = sign[:, :width]

    def join(values):
        h0, h1, h2, h3 = [twiddle(twiddles, residue, value, -sign) for residue, value in enumerate(values)]
        even, odd = h0 + h2, h1 + h3
        diff, turned = h0 - h2, sign * swap(h1 - h3)
        return even + odd, diff - turned, even - odd, diff + turned

    packed = both[:, 4 * width :]
    unpacked = [packed]
    for residue in range(1, 4):
        pieces = [pltpu.roll(packed[:, k : k + lanes], lanes - residue, 1) for k in range(0, width, lanes)]
        unpacked.append(jnp.concatenate(pieces, 1))
    lane = lax.broadcasted_iota(jnp.int32, (1, width), 1) % lanes
    edge = jnp.logical_and(is_special, lane == lanes // 2)
    whole = join([both[:, residue * width : (residue + 1) * width] for residue in range(4)])
    for a, (value, other) in enumerate(zip(whole, join(unpacked))):
        final = jnp.where(edge, other, value)
        for f in range(fields):
            out[a * per : (a + 1) * per, f] = final[:, f * lanes : (f + 1) * lanes].reshape(per, rows, lanes)


def holds_edge(slots, z_cells):
    return lax.axis_index("gx") * slots == z_cells // 4


def x_forward_kernel(table, twiddles, data_h, out, data, sem):
    copy = pltpu.make_async_copy(data_h, data, sem)
    copy.start()
    copy.wait()
    fields, lanes = data.shape[1], data.shape[3]
    for residue, spectrum in enumerate(x_forward(data, table, twiddles)):
        for f in range(fields):
            out[residue, f] = spectrum[:, f * lanes : (f + 1) * lanes]


def green_rows(x_cells, z_cells, chunk, moduli, mean, load, new):
    quarter, lanes = new.shape[0], new.shape[1] // (5 * len(chunk))
    slots = lanes // 2
    place, mine = lax.axis_index("gz"), lax.axis_index("gx")
    inplane = functools.reduce(jnp.logical_or, [place == k for k in INPLANE])
    lame_ref = 0.5 * (moduli[0] + moduli[2])
    shear_ref = 0.5 * (moduli[1] + moduli[3])
    half_inverse = 0.5 / shear_ref
    coupling = (lame_ref + shear_ref) / (shear_ref * (lame_ref + 2.0 * shear_ref))
    c1 = jnp.where(inplane, coupling, 0.0)
    k1 = jnp.where(inplane, 2.0 * half_inverse, half_inverse)
    k2 = jnp.where(inplane, half_inverse, 0.0)
    ka = jnp.where(inplane, 0.0, half_inverse)
    total = float(x_cells * z_cells)
    means = (
        total * jnp.where(inplane, mean[XX], mean[XY]),
        total * jnp.where(inplane, mean[ZZ], mean[YZ]),
        total * mean[XZ],
    )

    def store(field, residue, rows, value):
        block = residue * len(chunk) + chunk.index(field)
        new[rows, block * lanes : (block + 1) * lanes] = value

    def green(kx, kz, odd_kx, s, anchored=False):
        radius = kx * kx + kz * kz
        if anchored:
            radius = jnp.where(radius == 0.0, 1.0, radius)
        inverse = 1.0 / radius
        a, b = kx * kx * inverse, kz * kz * inverse
        d = odd_kx * kz * inverse
        ab = c1 * (a * b)
        ca, cb = c1 * a, c1 * b
        h02, h12 = d * (ca - k2), d * (cb - k2)
        m01 = ab - ka * d
        twice = 2.0 * s[2]
        rows = (
            lambda: a * (ca - k1) * s[0] + m01 * s[1] + h02 * twice,
            lambda: m01 * s[0] + b * (cb - k1) * s[1] + h12 * twice,
            lambda: h02 * s[0] + h12 * s[1] + (2.0 * ab - k2) * s[2],
        )
        return {f: rows[f]() for f in chunk}

    lane = lax.broadcasted_iota(jnp.int32, (1, lanes), 1)
    slot_of = lane % slots
    order = mine * slots + slot_of
    zeros_at, twos_at = z_cells // 4, z_cells // 4 + z_cells // 8
    kz = jnp.where(
        order < zeros_at,
        4 * order + 1,
        jnp.where(order < twos_at, 4 * (order - zeros_at), 4 * (order - twos_at) + 2),
    )
    kz = jnp.where(kz < z_cells // 2, kz, kz - z_cells).astype(F32)
    special = order == zeros_at
    size = 32
    for start in range(0, quarter, size):
        rows = pl.ds(start, size)
        row = lax.broadcasted_iota(jnp.int32, (size, lanes), 0) + start
        full_kz = jnp.broadcast_to(kz, (size, lanes))
        first_kx = (4 * row - (x_cells if 2 * start >= quarter else 0)).astype(F32)
        mirror = 2 * start == quarter
        edge = [None] * FIELDS
        for residue in range(4):
            s = [load(f, residue, rows) for f in range(FIELDS)]
            for f in range(FIELDS):
                moved = s[f] if residue == 0 else pltpu.roll(s[f], residue, 1)
                edge[f] = moved if residue == 0 else jnp.where(slot_of == residue, moved, edge[f])
            kx = first_kx + float(residue)
            odd_kx = jnp.where(row == start, 0.0, kx) if mirror and residue == 0 else kx
            with_anchor = residue == 0 and start == 0
            fresh = green(kx, full_kz, odd_kx, s, with_anchor)
            if with_anchor:
                anchor = jnp.logical_and(row == 0, special)
                for f in chunk:
                    fresh[f] = jnp.where(anchor, jnp.where(lane < slots, means[f], 0.0), fresh[f])
            for f in chunk:
                store(f, residue, rows, fresh[f])
        kx = first_kx + slot_of.astype(F32)
        odd_kx = jnp.where(jnp.logical_and(row == start, slot_of == 0), kx, 0.0) if mirror else jnp.zeros_like(kx)
        fresh = green(kx, jnp.full((size, lanes), -0.5 * z_cells, F32), odd_kx, edge)
        for f in chunk:
            store(f, 4, rows, fresh[f])


def loader(chunks, early, late):
    def load(field, residue, rows):
        spectra, chunk = (early, chunks[0]) if field in chunks[0] else (late, chunks[1])
        return spectra[residue, chunk.index(field), rows, :]

    return load


def early_inverse_kernel(x_cells, z_cells, chunks, moduli, mean, table, twiddles, early, late, own, swapped, out, new):
    green_rows(x_cells, z_cells, chunks[0], moduli, mean, loader(chunks, early, late), new)
    x_inverse(new[...], table, twiddles, holds_edge(out.shape[3] // 2, z_cells), out)
    deal(out, own, swapped)


def late_kernel(x_cells, z_cells, chunks, moduli, mean, table, twiddles, early, own_in, got, *rest):
    chips = own_in.shape[0]
    moved, rest = rest[: chips - 1], rest[chips - 1 :]
    own_out, swapped, late, data, out, new = rest
    collect(own_in, got, moved, data)
    lanes = data.shape[3]
    for residue, spectrum in enumerate(x_forward(data, table, twiddles)):
        for slot in range(data.shape[1]):
            late[residue, slot] = spectrum[:, slot * lanes : (slot + 1) * lanes]
    green_rows(x_cells, z_cells, chunks[1], moduli, mean, loader(chunks, early, late), new)
    x_inverse(new[...], table, twiddles, holds_edge(lanes // 2, z_cells), out)
    deal(out, own_out, swapped)


def z_inverse_kernel(table, data, *rest):
    outs, held = rest[:-1], rest[-1]
    parts = len(GROUPS)
    place = lax.axis_index("gz")
    sources, fields, rows, lanes = data.shape
    half = sources // 2
    fourth = sources // 4

    def columns(begin, end):
        return jnp.concatenate([data[k].reshape(fields * rows, lanes) for k in range(begin, end)], 1)

    first = dot_right(columns(0, half), table, 0)
    zero = dot_right(columns(half, half + fourth), table, 1)
    two = dot_right(columns(half + fourth, sources), table, 2)
    width = zero.shape[1]
    real, imag = first[:, :width], first[:, width:]
    plus, minus = zero + two, zero - two
    for k, value in enumerate((plus + real, minus - imag, plus - real, minus + imag)):
        held[k] = value.reshape(fields, rows, width)
    for step in range(parts):
        target = lax.rem(place + step, parts)
        for slot in range(fields):
            outs[slot * parts + step][...] = held[target, slot]


def stress_kernel(slots, strain_parts, stress_parts, moduli, mean, labels, normals, *rest):
    parts = len(GROUPS)
    arrived = rest[: len(slots) * parts]
    strain_to, stress_to, held, strain_out, stress_out, sems = rest[-6:]
    place = lax.axis_index("gz")
    sections, cells_x, cells_z = labels.shape
    size = cells_x // normals.shape[1]
    for step in range(parts):
        source = lax.rem(place + parts - step, parts)
        for k, slot in enumerate(slots):
            held[source, slot] = arrived[k * parts + step][...]
    copies = []
    for section in range(sections):
        squares = tilt(normals, section, cells_z)
        for block in range(cells_x // size):
            rows = pl.ds(block * size, size)
            local = {c: jnp.zeros((size, cells_z), F32) for c in range(6)}
            local[YY] = jnp.full((size, cells_z), mean[YY], F32)
            for group, fields in enumerate(GROUPS):
                for slot, (component, of) in enumerate(fields):
                    if of == section and slot in slots:
                        local[component] = held[group, slot, rows, :]
            value = law(
                local,
                labels[section, rows, :],
                row_of(squares, block, size),
                (moduli[0], moduli[2]),
                (moduli[1], moduli[3]),
                moduli[4],
            )
            for component in strain_parts:
                strain_out[component, section, rows, :] = local[component]
            for component in stress_parts:
                stress_out[component, section, rows, :] = value[component]
        for here, there, chosen in ((strain_out, strain_to, strain_parts), (stress_out, stress_to, stress_parts)):
            for c in chosen:
                copy = pltpu.make_async_copy(here.at[c, section], there.at[c, section], sems.at[len(copies)])
                copy.start()
                copies.append(copy)
    for copy in copies:
        copy.wait()


def call(kernel, outs, scratch, args, limit, hbm=(), smem=0, hbm_out=(), aliases={}):
    def space(k):
        return pltpu.HBM if k in hbm else pltpu.SMEM if k < smem else pltpu.VMEM

    args = [pltpu.with_memory_space_constraint(a, pltpu.HBM) if k in hbm else a for k, a in enumerate(args)]
    moved = sum(a.size * a.dtype.itemsize for a in args) + sum(math.prod(o) * 4 for o in outs)
    return pl.pallas_call(
        kernel,
        out_shape=[
            pltpu.HBM(o, F32) if k in hbm_out else jax.ShapeDtypeStruct(o, F32) for k, o in enumerate(outs)
        ],
        in_specs=[pl.BlockSpec(memory_space=space(k)) for k in range(len(args))],
        out_specs=[
            pl.BlockSpec(memory_space=pltpu.HBM if k in hbm_out else pltpu.VMEM) for k in range(len(outs))
        ],
        scratch_shapes=scratch,
        input_output_aliases=aliases,
        compiler_params=pltpu.CompilerParams(vmem_limit_bytes=limit * MIB),
        cost_estimate=pl.CostEstimate(flops=0, bytes_accessed=moved, transcendentals=0),
    )(*args)


def shards(strain, labels, normals, moduli, mean_strain):
    parts = lax.axis_size("gz")
    x_devices = lax.axis_size("gx")
    _, sections, cells_x, cells_z = strain.shape
    x_total, z_total = cells_x * x_devices, cells_z * parts
    slots = z_total // 2 // x_devices
    lanes = 2 * slots
    z_fwd, z_inv = z_tables(z_total, slots, 1.0 / (x_total * z_total))
    x_tab = x_tables(x_total)
    block = (cells_x, cells_z)
    everyone = range(parts)

    def travel(field, blocks, gather):
        ends = INPLANE if field == 2 else everyone
        moved = [blocks[0]]
        for step in range(1, parts):
            way = [(k, (k + step) % parts) for k in range(parts)]
            way = [(a, b) for a, b in way if (b if gather else a) in ends]
            moved.append(lax.ppermute(blocks[step], "gz", way))
        return moved

    def held(fields):
        return pltpu.VMEM((parts, fields, cells_x, cells_z), F32)

    blocks = call(
        polarize_kernel,
        [block] * (FIELDS * parts),
        [
            held(FIELDS),
            pltpu.VMEM(strain.shape, F32),
            pltpu.VMEM(labels.shape, jnp.int32),
            pltpu.VMEM(normals.shape, jnp.int32),
            pltpu.SMEM(moduli.shape, F32),
            pltpu.SemaphoreType.DMA((2 + 2 * sections,)),
        ],
        (moduli, strain, labels, normals),
        16,
        range(4),
    )
    blocks = {f: list(blocks[f * parts : (f + 1) * parts]) for f in range(FIELDS)}
    quarter = x_total // 4
    chips = x_devices // 2
    early, late = CHUNKS
    size = len(early)
    grid = (x_devices, size, cells_x, lanes)
    tile = (chips, 1, cells_x, lanes)
    tile_early = (chips, size, cells_x, lanes)
    tiles = pltpu.VMEM((x_devices, 1, cells_x, lanes), F32)

    def exchange(own, swapped, after):
        got = lax.ppermute(swapped, "gx", [(k, k ^ 1) for k in range(x_devices)])
        merged = call(merge_kernel, [(2, *own.shape[1:])] * (chips - 1), [], (own, got), 8)
        merged, after = lax.optimization_barrier((merged, after))
        moved = [
            lax.ppermute(block, "gx", [(k, k ^ (2 * step)) for k in range(x_devices)])
            for step, block in enumerate(merged, 1)
        ]
        return (own, got, *moved), after

    args = [a for f in early for a in travel(f, blocks[f], True)]
    args, blocks = lax.optimization_barrier((args, blocks))
    (rows,) = call(z_forward_kernel, [grid], [held(size)], (z_fwd, *args), 16)
    rows = lax.all_to_all(rows, "gx", 0, 0, tiled=True)
    args = travel(late[0], blocks[late[0]], True)
    args, rows = lax.optimization_barrier((args, rows))
    own, swapped = call(z_forward_deal_kernel, [tile] * 2, [held(1), tiles], (z_fwd, *args), 16)
    last, rows = exchange(own, swapped, rows)
    copied = [pltpu.VMEM(grid, F32), pltpu.SemaphoreType.DMA]
    (spectrum,) = call(x_forward_kernel, [(4, size, quarter, lanes)], copied, (*x_tab, rows), 24, (2,))
    own, swapped, late_spectrum = call(
        functools.partial(late_kernel, x_total, z_total, CHUNKS),
        [tile, tile, (4, 1, quarter, lanes)],
        [tiles, tiles, pltpu.VMEM((quarter, 5 * lanes), F32)],
        (moduli, mean_strain, *x_tab, spectrum, *last),
        24,
        smem=2,
    )
    last, late_spectrum = exchange(own, swapped, late_spectrum)
    rest = call(
        functools.partial(early_inverse_kernel, x_total, z_total, CHUNKS),
        [tile_early] * 2,
        [pltpu.VMEM(grid, F32), pltpu.VMEM((quarter, 5 * size * lanes), F32)],
        (moduli, mean_strain, *x_tab, spectrum, late_spectrum),
        24,
        smem=2,
    )
    rest, last = lax.optimization_barrier((rest, last))
    blocks = call(z_inverse_collect_kernel, [block] * parts, [held(1), tiles], (z_inv, *last), 16)
    rest, blocks = exchange(*rest, list(blocks))
    arrived = {late[0]: travel(late[0], blocks, False)}
    scratch = [held(size), pltpu.VMEM(grid, F32)]
    blocks = call(z_inverse_collect_kernel, [block] * (size * parts), scratch, (z_inv, *rest), 16)
    for slot, f in enumerate(early):
        arrived[f] = travel(f, blocks[slot * parts : (slot + 1) * parts], False)
    full = (6, sections, cells_x, cells_z)
    results = ()
    for slots, strains, stresses in (((0, 1), (XX, YY, ZZ, YZ, XY), (YY, YZ, XY)), ((0, 1, 2), (XZ,), (XX, ZZ, XZ))):
        args = (moduli, mean_strain, labels, normals, *[a for f in slots for a in arrived[f]], *results)
        hbm = range(len(args) - len(results), len(args))
        count = sections * (len(strains) + len(stresses))
        results = call(
            functools.partial(stress_kernel, slots, strains, stresses),
            [full, full],
            [held(FIELDS), pltpu.VMEM(full, F32), pltpu.VMEM(full, F32), pltpu.SemaphoreType.DMA((count,))],
            args,
            16,
            hbm,
            smem=2,
            hbm_out=(0, 1),
            aliases={k: out for out, k in enumerate(hbm)},
        )
    return tuple(results)


def orientation(normals, blk):
    tilt_angle = math.pi / ANGLES * normals.astype(jnp.float32)
    tilt_angle = jnp.repeat(jnp.repeat(tilt_angle, blk, axis=1), blk, axis=2)
    return (jnp.cos(tilt_angle), jnp.sin(tilt_angle))


def stress_law(strain_field, labels, cosine_tilt, sine_tilt, moduli):
    laminate = labels == 1
    lame_local = jnp.where(laminate, moduli[2], moduli[0])
    shear_local = jnp.where(laminate, moduli[3], moduli[1])
    trace_sum = strain_field[0] + strain_field[1] + strain_field[2]
    normal_part = (
        cosine_tilt * cosine_tilt * strain_field[0]
        + sine_tilt * sine_tilt * strain_field[2]
        + 2.0 * cosine_tilt * sine_tilt * strain_field[4]
    )
    laminate_term = moduli[4] * labels.astype(jnp.float32) * normal_part
    dyad = [
        cosine_tilt * cosine_tilt,
        None,
        sine_tilt * sine_tilt,
        None,
        cosine_tilt * sine_tilt,
        None,
    ]
    result = []
    for slot in range(6):
        value = 2.0 * shear_local * strain_field[slot]
        if slot < 3:
            value = value + lame_local * trace_sum
        if dyad[slot] is not None:
            value = value + laminate_term * dyad[slot]
        result.append(value)
    return jnp.stack(result)


def polarize(stresses, strain_field, lame_ref, shear_ref):
    trace_sum = strain_field[0] + strain_field[1] + strain_field[2]
    result = []
    for slot in range(6):
        value = stresses[slot] - 2.0 * shear_ref * strain_field[slot]
        if slot < 3:
            value = value - lame_ref * trace_sum
        result.append(value)
    return jnp.stack(result)


def green_apply(spectrum, unit_x, unit_z, lame_ref, shear_ref):
    coupling = (lame_ref + shear_ref) / (shear_ref * (lame_ref + 2.0 * shear_ref))
    traction_x = spectrum[0] * unit_x + spectrum[4] * unit_z
    traction_y = spectrum[5] * unit_x + spectrum[3] * unit_z
    traction_z = spectrum[4] * unit_x + spectrum[2] * unit_z
    normal_load = unit_x * traction_x + unit_z * traction_z
    half_inverse = 0.5 / shear_ref
    result = [
        2.0 * half_inverse * unit_x * traction_x - coupling * normal_load * unit_x * unit_x,
        jnp.zeros_like(traction_x),
        2.0 * half_inverse * unit_z * traction_z - coupling * normal_load * unit_z * unit_z,
        half_inverse * unit_z * traction_y,
        half_inverse * (unit_z * traction_x + unit_x * traction_z)
        - coupling * normal_load * unit_x * unit_z,
        half_inverse * unit_x * traction_y,
    ]
    return -jnp.stack(result)


def phases(left_ids, right_ids, length):
    product = left_ids[:, None] * right_ids[None, :] % length
    phase_angle = 2.0 * math.pi / length * product.astype(jnp.float32)
    return (jnp.cos(phase_angle), jnp.sin(phase_angle))


def contract(form, left_side, right_side):
    return jnp.einsum(
        form,
        left_side,
        right_side,
        precision=lax.Precision.HIGHEST,
        preferred_element_type=jnp.float32,
    )


def signed_value(counter, length):
    return jnp.where(counter < length // 2, counter, counter - length).astype(jnp.float32)


def shards_general(strain, labels, normals, moduli, mean_strain):
    z_devices = lax.axis_size("gz")
    x_devices = lax.axis_size("gx")
    z_index = lax.axis_index("gz")
    x_index = lax.axis_index("gx")
    sections = strain.shape[1]
    cells_x = strain.shape[2]
    cells_z = strain.shape[3]
    x_total = cells_x * x_devices
    z_total = cells_z * z_devices
    line_count = sections * cells_x
    kz_share = cells_z // x_devices
    cosine_tilt, sine_tilt = orientation(normals, strain.shape[2] // normals.shape[1])
    lame_ref = 0.5 * (moduli[0] + moduli[2])
    shear_ref = 0.5 * (moduli[1] + moduli[3])
    stresses = stress_law(strain, labels, cosine_tilt, sine_tilt, moduli)
    polarized = polarize(stresses, strain, lame_ref, shear_ref)
    flattened = polarized.reshape(6, line_count, cells_z)
    own_block = z_index * cells_z + jnp.arange(cells_z, dtype=jnp.int32)
    empty_sum = jnp.zeros((6, cells_z, line_count), jnp.float32)
    pieces = lax.all_gather(flattened, "gz", axis=2, tiled=True)
    z_ids = jnp.arange(pieces.shape[2], dtype=jnp.int32)
    cos_table, sin_table = phases(z_ids, own_block, z_total)
    real_part = contract("cmz,zk->ckm", pieces, cos_table)
    imag_part = (empty_sum, empty_sum)[1] - contract("cmz,zk->ckm", pieces, sin_table)
    real_rows, imag_rows = (
        lax.all_to_all(real_part, "gx", split_axis=1, concat_axis=2, tiled=True),
        lax.all_to_all(imag_part, "gx", split_axis=1, concat_axis=2, tiled=True),
    )
    grid_shape = (6, kz_share, x_devices, sections, cells_x)
    real_rows = real_rows.reshape(grid_shape)
    imag_rows = imag_rows.reshape(grid_shape)
    every_x = jnp.arange(x_total, dtype=jnp.int32)
    cos_x, sin_x = phases(every_x, every_x, x_total)
    cos_x = cos_x.reshape(x_devices, cells_x, x_total)
    sin_x = sin_x.reshape(x_devices, cells_x, x_total)
    spec_real = contract("ckgsx,gxq->cksq", real_rows, cos_x) + contract(
        "ckgsx,gxq->cksq", imag_rows, sin_x
    )
    spec_imag = contract("ckgsx,gxq->cksq", imag_rows, cos_x) - contract(
        "ckgsx,gxq->cksq", real_rows, sin_x
    )
    kz_ids = z_index * cells_z + x_index * kz_share + jnp.arange(kz_share, dtype=jnp.int32)
    freq_z = signed_value(kz_ids, z_total)[:, None, None]
    freq_x = signed_value(every_x, x_total)[None, None, :]
    radius_sq = freq_x * freq_x + freq_z * freq_z
    at_anchor = radius_sq == 0.0
    safe_radius = jnp.sqrt(jnp.where(at_anchor, 1.0, radius_sq))
    unit_x = freq_x / safe_radius
    unit_z = freq_z / safe_radius
    anchor_term = jnp.where(at_anchor, float(x_total * z_total), 0.0)
    new_real = green_apply(spec_real, unit_x, unit_z, lame_ref, shear_ref)
    new_real = new_real + mean_strain[:, None, None, None] * anchor_term[None]
    new_imag = green_apply(spec_imag, unit_x, unit_z, lame_ref, shear_ref)
    back_real = contract("cksq,gxq->ckgsx", new_real, cos_x) - contract(
        "cksq,gxq->ckgsx", new_imag, sin_x
    )
    back_imag = contract("cksq,gxq->ckgsx", new_real, sin_x) + contract(
        "cksq,gxq->ckgsx", new_imag, cos_x
    )
    back_real = back_real.reshape(6, kz_share, x_devices * line_count)
    back_imag = back_imag.reshape(6, kz_share, x_devices * line_count)
    real_part, imag_part = (
        lax.all_to_all(back_real, "gx", split_axis=2, concat_axis=1, tiled=True),
        lax.all_to_all(back_imag, "gx", split_axis=2, concat_axis=1, tiled=True),
    )
    z_ids = jnp.arange(lax.axis_size("gz") * cells_z, dtype=jnp.int32)
    cos_table, sin_table = phases(own_block, z_ids, z_total)
    summed = lax.psum_scatter(
        contract("ckm,kz->zcm", real_part, cos_table)
        - contract("ckm,kz->zcm", imag_part, sin_table),
        "gz",
        scatter_dimension=0,
        tiled=True,
    )
    field_lines = jnp.transpose(summed, (1, 2, 0))
    strain_next = (field_lines * (1.0 / (x_total * z_total))).reshape(6, sections, cells_x, cells_z)
    stress_next = stress_law(strain_next, labels, cosine_tilt, sine_tilt, moduli)
    return (strain_next, stress_next)


def solution(mesh):
    in_specs = (P(None, None, "gx", "gz"), P(None, "gx", "gz"), P(None, "gx", "gz"), P(), P())
    out_specs = (P(None, None, "gx", "gz"), P(None, None, "gx", "gz"))

    def run(strain, labels, normals, moduli, mean_strain):
        _, sections, x_total, z_total = strain.shape
        parts, x_devices = mesh.shape["gz"], mesh.shape["gx"]
        grouped = (
            sections == 2
            and parts == len(GROUPS)
            and x_devices == 8
            and z_total == 128 * x_devices
            and x_total % (128 * x_devices) == 0
        )
        body = shards if grouped else shards_general
        mapped = jax.shard_map(body, mesh=mesh, in_specs=in_specs, out_specs=out_specs, check_vma=False)
        return mapped(strain, labels, normals, moduli, mean_strain)

    return run
```

```python
import functools
import math

import jax
import jax.numpy as jnp
import numpy as np
from jax import lax
from jax.experimental import pallas as pl
from jax.experimental.pallas import tpu as pltpu
from jax.sharding import PartitionSpec as P

ANGLES = 8
XX, YY, ZZ, YZ, XZ, XY = range(6)
GROUPS = (
    ((XY, 0), (YZ, 0)),
    ((XX, 0), (ZZ, 0), (XZ, 0)),
    ((XX, 1), (ZZ, 1), (XZ, 1)),
    ((XY, 1), (YZ, 1)),
)
INPLANE = (1, 2)
FIELDS = 3
CHUNKS = ((0, 2), (1,))
F32, BF16 = jnp.float32, jnp.bfloat16
MIB = 1 << 20


def split_table(table):
    table = np.asarray(table, np.float32)
    high = table.astype(jnp.bfloat16)
    low = (table - high.astype(np.float32)).astype(jnp.bfloat16)
    return jnp.asarray(np.stack([high, low]))


def half_frequencies(length):
    quarter = length // 4
    return (
        4 * np.arange(quarter) + 1,
        4 * np.arange(quarter // 2),
        4 * np.arange(quarter // 2) + 2,
    )


def interleave(real, imag, slots):
    rows, count = real.shape
    both = np.stack([real.reshape(rows, -1, slots), imag.reshape(rows, -1, slots)], 2)
    return both.reshape(rows, 2 * count)


def z_tables(length, slots, scale):
    quarter = length // 4
    z = np.arange(quarter, dtype=np.int64)[:, None]
    ones, zeros, twos = half_frequencies(length)

    def angles(freqs):
        return 2.0 * math.pi / length * ((z * freqs[None, :]) % length)

    one, zero, two = angles(ones), angles(zeros), angles(twos)
    top = interleave(np.cos(one), -np.sin(one), slots)
    bottom = interleave(-np.sin(one), -np.cos(one), slots)
    forward_one = np.concatenate([top, bottom], 0)
    real, imag = np.cos(zero), -np.sin(zero)
    imag[:, 0] = np.where(np.arange(quarter) % 2 == 0, 1.0, -1.0)
    forward_zero = interleave(real, imag, slots)
    forward_two = interleave(np.cos(two), -np.sin(two), slots)
    weight = 2.0 * scale
    inverse_one = weight * np.concatenate(
        [interleave(np.cos(one), -np.sin(one), slots), interleave(np.sin(one), np.cos(one), slots)], 0
    ).T
    half = np.full(quarter // 2, weight)
    half[0] = scale
    inverse_zero = interleave(real * half, imag * half, slots).T
    inverse_two = weight * forward_two.T

    def pack(first, second, third):
        return split_table(np.concatenate([first, np.concatenate([second, third], 1)], 0))

    return pack(forward_one, forward_zero, forward_two), pack(inverse_one, inverse_zero, inverse_two)


def x_tables(length):
    quarter = length // 4
    k = np.arange(quarter, dtype=np.int64)
    angle = 2.0 * math.pi / quarter * ((k[:, None] * k[None, :]) % quarter)
    turn = 2.0 * math.pi / length * k
    columns = [f(residue * turn) for residue in (1, 2, 3) for f in (np.cos, np.sin)]
    twiddles = jnp.asarray(np.stack(columns + columns[:2], 1).astype(np.float32))
    return split_table(np.concatenate([np.cos(angle), np.sin(angle)], 0)), twiddles


def halves(value):
    high = value.astype(BF16)
    return high, (value - high.astype(F32)).astype(BF16)


def dot(left, right):
    return jnp.dot(left, right, preferred_element_type=F32)


def dot_right(value, table, part):
    big = table.shape[2]
    half = big // 2
    rows = slice(0, big) if part == 0 else slice(big, big + half)
    columns = slice(0, big) if part == 0 else slice((part - 1) * half, part * half)
    high_table, low_table = table[0, rows, columns], table[1, rows, columns]
    high, low = halves(value)
    return dot(high, high_table) + (dot(low, high_table) + dot(high, low_table))


def dot_left(table, value):
    high, low = halves(value)
    return dot(table[0], high) + (dot(table[0], low) + dot(table[1], high))


def tilt(normals, section, cells_z):
    blocks = normals[section].astype(F32)
    count = blocks.shape[1]
    size = cells_z // count
    owner = lax.broadcasted_iota(jnp.int32, (count, cells_z), 1) // size
    own = lax.broadcasted_iota(jnp.int32, (count, cells_z), 0)
    spread = jnp.where(owner == own, 1.0, 0.0).astype(F32)
    angle = (math.pi / ANGLES) * dot(blocks, spread)
    cosine, sine = jnp.cos(angle), jnp.sin(angle)
    return cosine * cosine, sine * sine, cosine * sine


def law(strain, label, squares, lame, shear, stiff):
    cc, ss, cs = squares
    laminate = label == 1
    lame_local = jnp.where(laminate, lame[1], lame[0])
    twice_shear = jnp.where(laminate, 2.0 * shear[1], 2.0 * shear[0])
    spherical = lame_local * (strain[XX] + strain[YY] + strain[ZZ])
    normal = cc * strain[XX] + ss * strain[ZZ] + 2.0 * cs * strain[XZ]
    normal = jnp.where(laminate, stiff, 0.0) * normal
    return {
        XX: twice_shear * strain[XX] + spherical + normal * cc,
        YY: twice_shear * strain[YY] + spherical,
        ZZ: twice_shear * strain[ZZ] + spherical + normal * ss,
        YZ: twice_shear * strain[YZ],
        XZ: twice_shear * strain[XZ] + normal * cs,
        XY: twice_shear * strain[XY],
    }


def row_of(squares, block, size):
    return [jnp.broadcast_to(s[block : block + 1], (size, s.shape[1])) for s in squares]


def polarize_kernel(moduli_h, strain_h, labels_h, normals_h, *rest):
    outs, (held, strain, labels, normals, moduli, sems) = rest[:-6], rest[-6:]
    sections, cells_x, cells_z = labels.shape
    copies = [
        pltpu.make_async_copy(moduli_h, moduli, sems.at[0]),
        pltpu.make_async_copy(normals_h, normals, sems.at[1]),
    ]
    for k in range(sections):
        copies.append(pltpu.make_async_copy(labels_h.at[k], labels.at[k], sems.at[2 + 2 * k]))
        copies.append(pltpu.make_async_copy(strain_h.at[:, k], strain.at[:, k], sems.at[3 + 2 * k]))
    for copy in copies:
        copy.start()
    for copy in copies[:2]:
        copy.wait()
    parts = len(GROUPS)
    place = lax.axis_index("gz")
    size = cells_x // normals.shape[1]
    lame_ref = 0.5 * (moduli[0] + moduli[2])
    shear_ref = 0.5 * (moduli[1] + moduli[3])
    lame = (moduli[0] - lame_ref, moduli[2] - lame_ref)
    shear = (moduli[1] - shear_ref, moduli[3] - shear_ref)
    for group, fields in enumerate(GROUPS):
        if len(fields) < 3:
            held[group, 2] = jnp.zeros((cells_x, cells_z), F32)
    for section in range(sections):
        copies[2 + 2 * section].wait()
        copies[3 + 2 * section].wait()
        squares = tilt(normals, section, cells_z)
        for block in range(cells_x // size):
            rows = pl.ds(block * size, size)
            local = [strain[c, section, rows, :] for c in range(6)]
            value = law(local, labels[section, rows, :], row_of(squares, block, size), lame, shear, moduli[4])
            for group, fields in enumerate(GROUPS):
                for slot, (component, of) in enumerate(fields):
                    if of == section:
                        held[group, slot, rows, :] = value[component]
    for step in range(parts):
        target = lax.rem(place + step, parts)
        for slot in range(FIELDS):
            outs[slot * parts + step][...] = held[target, slot]


def deal(blocks, own, swapped):
    mine = lax.axis_index("gx")
    chip, core = mine // 2, lax.rem(mine, 2)
    for step in range(own.shape[0]):
        there = 2 * lax.bitwise_xor(chip, step)
        own[step] = blocks[there + core]
        swapped[step] = blocks[there + 1 - core]


def collect(own, got, moved, blocks):
    mine = lax.axis_index("gx")
    chip, core = mine // 2, lax.rem(mine, 2)
    for step in range(own.shape[0]):
        there = 2 * lax.bitwise_xor(chip, step)
        blocks[there + core] = own[0] if step == 0 else moved[step - 1][0]
        blocks[there + 1 - core] = got[0] if step == 0 else moved[step - 1][1]


def merge_kernel(own, got, *outs):
    for k, out in enumerate(outs):
        out[0] = own[k + 1]
        out[1] = got[k + 1]


def z_forward_deal_kernel(table, *rest):
    arrived, (own, swapped, held, blocks) = rest[:-4], rest[-4:]
    z_forward_kernel(table, *arrived, blocks, held)
    deal(blocks, own, swapped)


def z_inverse_collect_kernel(table, own, got, *rest):
    chips = own.shape[0]
    moved, outs, (held, blocks) = rest[: chips - 1], rest[chips - 1 : -2], rest[-2:]
    collect(own, got, moved, blocks)
    z_inverse_kernel(table, blocks, *outs, held)


def z_forward_kernel(table, *rest):
    parts = len(GROUPS)
    arrived, (out, held) = rest[:-2], rest[-2:]
    place = lax.axis_index("gz")
    for step in range(parts):
        source = lax.rem(place + parts - step, parts)
        for slot in range(held.shape[1]):
            held[source, slot] = arrived[slot * parts + step][...]
    fields, rows, width = held.shape[1:]
    lanes = out.shape[3]
    z0, z1, z2, z3 = (held[k].reshape(fields * rows, width) for k in range(parts))
    first = jnp.concatenate([z0 - z2, z1 - z3], 1)
    even, odd = z0 + z2, z1 + z3
    spectra = (
        dot_right(first, table, 0),
        dot_right(even + odd, table, 1),
        dot_right(even - odd, table, 2),
    )
    target = 0
    for spectrum in spectra:
        for k in range(spectrum.shape[1] // lanes):
            out[target] = spectrum[:, k * lanes : (k + 1) * lanes].reshape(fields, rows, lanes)
            target += 1


def swap(value):
    lanes = value.shape[1]
    return jnp.concatenate([pltpu.roll(value[:, k : k + 128], 64, 1) for k in range(0, lanes, 128)], 1)


def turn_sign(width):
    lane = lax.broadcasted_iota(jnp.int32, (1, width), 1) % 128
    return jnp.where(lane < 64, 1.0, -1.0).astype(F32)


def twiddle(twiddles, residue, value, sign):
    if residue == 0:
        return value
    pick = 2 * (residue - 1)
    quarter = value.shape[0]
    cosine = jnp.broadcast_to(twiddles[:, pick : pick + 1], (quarter, 128))
    sine = jnp.broadcast_to(twiddles[:, pick + 1 : pick + 2], (quarter, 128)) * sign[:, :128]
    pieces = []
    for k in range(0, value.shape[1], 128):
        piece = value[:, k : k + 128]
        pieces.append(cosine * piece + sine * pltpu.roll(piece, 64, 1))
    return jnp.concatenate(pieces, 1)


def x_forward(data, table, twiddles):
    sources, fields, rows, lanes = data.shape
    quarter = sources * rows // 4
    per = sources // 4
    width = fields * lanes
    sign = turn_sign(width)
    block = [
        jnp.concatenate([data[a * per : (a + 1) * per, f].reshape(quarter, lanes) for f in range(fields)], 1)
        for a in range(4)
    ]
    even, odd = block[0] + block[2], block[1] + block[3]
    diff, turned = block[0] - block[2], sign * swap(block[1] - block[3])
    values = (even + odd, diff + turned, even - odd, diff - turned)
    values = [twiddle(twiddles, residue, value, sign) for residue, value in enumerate(values)]
    both = dot_left(table, jnp.concatenate(values, 1))
    for residue in range(4):
        columns = slice(residue * width, (residue + 1) * width)
        yield both[:quarter, columns] + sign * swap(both[quarter:, columns])


def x_inverse(spectra, table, twiddles, is_special, out):
    sources, fields, rows, lanes = out.shape
    quarter = sources * rows // 4
    per = sources // 4
    width = fields * lanes
    sign = turn_sign(spectra.shape[1])
    both = dot_left(table, spectra)
    both = both[:quarter] - sign * swap(both[quarter:])
    sign = sign[:, :width]

    def join(values):
        h0, h1, h2, h3 = [twiddle(twiddles, residue, value, -sign) for residue, value in enumerate(values)]
        even, odd = h0 + h2, h1 + h3
        diff, turned = h0 - h2, sign * swap(h1 - h3)
        return even + odd, diff - turned, even - odd, diff + turned

    packed = both[:, 4 * width :]
    unpacked = [packed]
    for residue in range(1, 4):
        pieces = [pltpu.roll(packed[:, k : k + lanes], lanes - residue, 1) for k in range(0, width, lanes)]
        unpacked.append(jnp.concatenate(pieces, 1))
    lane = lax.broadcasted_iota(jnp.int32, (1, width), 1) % lanes
    edge = jnp.logical_and(is_special, lane == lanes // 2)
    whole = join([both[:, residue * width : (residue + 1) * width] for residue in range(4)])
    for a, (value, other) in enumerate(zip(whole, join(unpacked))):
        final = jnp.where(edge, other, value)
        for f in range(fields):
            out[a * per : (a + 1) * per, f] = final[:, f * lanes : (f + 1) * lanes].reshape(per, rows, lanes)


def holds_edge(slots, z_cells):
    return lax.axis_index("gx") * slots == z_cells // 4


def x_forward_kernel(table, twiddles, own, got, *rest):
    moved, (out, data) = rest[:-2], rest[-2:]
    collect(own, got, moved, data)
    fields, lanes = data.shape[1], data.shape[3]
    for residue, spectrum in enumerate(x_forward(data, table, twiddles)):
        for f in range(fields):
            out[residue, f] = spectrum[:, f * lanes : (f + 1) * lanes]


def green_rows(x_cells, z_cells, chunk, moduli, mean, load, new):
    quarter, lanes = new.shape[0], new.shape[1] // (5 * len(chunk))
    slots = lanes // 2
    place, mine = lax.axis_index("gz"), lax.axis_index("gx")
    inplane = functools.reduce(jnp.logical_or, [place == k for k in INPLANE])
    lame_ref = 0.5 * (moduli[0] + moduli[2])
    shear_ref = 0.5 * (moduli[1] + moduli[3])
    half_inverse = 0.5 / shear_ref
    coupling = (lame_ref + shear_ref) / (shear_ref * (lame_ref + 2.0 * shear_ref))
    c1 = jnp.where(inplane, coupling, 0.0)
    k1 = jnp.where(inplane, 2.0 * half_inverse, half_inverse)
    k2 = jnp.where(inplane, half_inverse, 0.0)
    ka = jnp.where(inplane, 0.0, half_inverse)
    total = float(x_cells * z_cells)
    means = (
        total * jnp.where(inplane, mean[XX], mean[XY]),
        total * jnp.where(inplane, mean[ZZ], mean[YZ]),
        total * mean[XZ],
    )

    def store(field, residue, rows, value):
        block = residue * len(chunk) + chunk.index(field)
        new[rows, block * lanes : (block + 1) * lanes] = value

    def green(kx, kz, odd_kx, s, anchored=False):
        radius = kx * kx + kz * kz
        if anchored:
            radius = jnp.where(radius == 0.0, 1.0, radius)
        inverse = 1.0 / radius
        a, b = kx * kx * inverse, kz * kz * inverse
        d = odd_kx * kz * inverse
        ab = c1 * (a * b)
        ca, cb = c1 * a, c1 * b
        h02, h12 = d * (ca - k2), d * (cb - k2)
        m01 = ab - ka * d
        twice = 2.0 * s[2]
        rows = (
            lambda: a * (ca - k1) * s[0] + m01 * s[1] + h02 * twice,
            lambda: m01 * s[0] + b * (cb - k1) * s[1] + h12 * twice,
            lambda: h02 * s[0] + h12 * s[1] + (2.0 * ab - k2) * s[2],
        )
        return {f: rows[f]() for f in chunk}

    lane = lax.broadcasted_iota(jnp.int32, (1, lanes), 1)
    slot_of = lane % slots
    order = mine * slots + slot_of
    zeros_at, twos_at = z_cells // 4, z_cells // 4 + z_cells // 8
    kz = jnp.where(
        order < zeros_at,
        4 * order + 1,
        jnp.where(order < twos_at, 4 * (order - zeros_at), 4 * (order - twos_at) + 2),
    )
    kz = jnp.where(kz < z_cells // 2, kz, kz - z_cells).astype(F32)
    special = order == zeros_at
    size = 32
    for start in range(0, quarter, size):
        rows = pl.ds(start, size)
        row = lax.broadcasted_iota(jnp.int32, (size, lanes), 0) + start
        full_kz = jnp.broadcast_to(kz, (size, lanes))
        first_kx = (4 * row - (x_cells if 2 * start >= quarter else 0)).astype(F32)
        mirror = 2 * start == quarter
        edge = [None] * FIELDS
        for residue in range(4):
            s = [load(f, residue, rows) for f in range(FIELDS)]
            for f in range(FIELDS):
                moved = s[f] if residue == 0 else pltpu.roll(s[f], residue, 1)
                edge[f] = moved if residue == 0 else jnp.where(slot_of == residue, moved, edge[f])
            kx = first_kx + float(residue)
            odd_kx = jnp.where(row == start, 0.0, kx) if mirror and residue == 0 else kx
            with_anchor = residue == 0 and start == 0
            fresh = green(kx, full_kz, odd_kx, s, with_anchor)
            if with_anchor:
                anchor = jnp.logical_and(row == 0, special)
                for f in chunk:
                    fresh[f] = jnp.where(anchor, jnp.where(lane < slots, means[f], 0.0), fresh[f])
            for f in chunk:
                store(f, residue, rows, fresh[f])
        kx = first_kx + slot_of.astype(F32)
        odd_kx = jnp.where(jnp.logical_and(row == start, slot_of == 0), kx, 0.0) if mirror else jnp.zeros_like(kx)
        fresh = green(kx, jnp.full((size, lanes), -0.5 * z_cells, F32), odd_kx, edge)
        for f in chunk:
            store(f, 4, rows, fresh[f])


def loader(chunks, early, late):
    def load(field, residue, rows):
        spectra, chunk = (early, chunks[0]) if field in chunks[0] else (late, chunks[1])
        return spectra[residue, chunk.index(field), rows, :]

    return load


def early_inverse_kernel(x_cells, z_cells, chunks, moduli, mean, table, twiddles, early, late, own, swapped, out, new):
    green_rows(x_cells, z_cells, chunks[0], moduli, mean, loader(chunks, early, late), new)
    x_inverse(new[...], table, twiddles, holds_edge(out.shape[3] // 2, z_cells), out)
    deal(out, own, swapped)


def late_kernel(x_cells, z_cells, chunks, moduli, mean, table, twiddles, early, own_in, got, *rest):
    chips = own_in.shape[0]
    moved, rest = rest[: chips - 1], rest[chips - 1 :]
    own_out, swapped, late, data, out, new = rest
    collect(own_in, got, moved, data)
    lanes = data.shape[3]
    for residue, spectrum in enumerate(x_forward(data, table, twiddles)):
        for slot in range(data.shape[1]):
            late[residue, slot] = spectrum[:, slot * lanes : (slot + 1) * lanes]
    green_rows(x_cells, z_cells, chunks[1], moduli, mean, loader(chunks, early, late), new)
    x_inverse(new[...], table, twiddles, holds_edge(lanes // 2, z_cells), out)
    deal(out, own_out, swapped)


def z_inverse_kernel(table, data, *rest):
    outs, held = rest[:-1], rest[-1]
    parts = len(GROUPS)
    place = lax.axis_index("gz")
    sources, fields, rows, lanes = data.shape
    half = sources // 2
    fourth = sources // 4

    def columns(begin, end):
        return jnp.concatenate([data[k].reshape(fields * rows, lanes) for k in range(begin, end)], 1)

    first = dot_right(columns(0, half), table, 0)
    zero = dot_right(columns(half, half + fourth), table, 1)
    two = dot_right(columns(half + fourth, sources), table, 2)
    width = zero.shape[1]
    real, imag = first[:, :width], first[:, width:]
    plus, minus = zero + two, zero - two
    for k, value in enumerate((plus + real, minus - imag, plus - real, minus + imag)):
        held[k] = value.reshape(fields, rows, width)
    for step in range(parts):
        target = lax.rem(place + step, parts)
        for slot in range(fields):
            outs[slot * parts + step][...] = held[target, slot]


def stress_kernel(slots, strain_parts, stress_parts, moduli, mean, labels, normals, *rest):
    parts = len(GROUPS)
    arrived = rest[: len(slots) * parts]
    strain_to, stress_to, held, strain_out, stress_out, sems = rest[-6:]
    place = lax.axis_index("gz")
    sections, cells_x, cells_z = labels.shape
    size = cells_x // normals.shape[1]
    for step in range(parts):
        source = lax.rem(place + parts - step, parts)
        for k, slot in enumerate(slots):
            held[source, slot] = arrived[k * parts + step][...]
    copies = []
    for section in range(sections):
        squares = tilt(normals, section, cells_z)
        for block in range(cells_x // size):
            rows = pl.ds(block * size, size)
            local = {c: jnp.zeros((size, cells_z), F32) for c in range(6)}
            local[YY] = jnp.full((size, cells_z), mean[YY], F32)
            for group, fields in enumerate(GROUPS):
                for slot, (component, of) in enumerate(fields):
                    if of == section and slot in slots:
                        local[component] = held[group, slot, rows, :]
            value = law(
                local,
                labels[section, rows, :],
                row_of(squares, block, size),
                (moduli[0], moduli[2]),
                (moduli[1], moduli[3]),
                moduli[4],
            )
            for component in strain_parts:
                strain_out[component, section, rows, :] = local[component]
            for component in stress_parts:
                stress_out[component, section, rows, :] = value[component]
        for here, there, chosen in ((strain_out, strain_to, strain_parts), (stress_out, stress_to, stress_parts)):
            for c in chosen:
                copy = pltpu.make_async_copy(here.at[c, section], there.at[c, section], sems.at[len(copies)])
                copy.start()
                copies.append(copy)
    for copy in copies:
        copy.wait()


def call(kernel, outs, scratch, args, limit, hbm=(), smem=0, hbm_out=(), aliases={}):
    def space(k):
        return pltpu.HBM if k in hbm else pltpu.SMEM if k < smem else pltpu.VMEM

    args = [pltpu.with_memory_space_constraint(a, pltpu.HBM) if k in hbm else a for k, a in enumerate(args)]
    moved = sum(a.size * a.dtype.itemsize for a in args) + sum(math.prod(o) * 4 for o in outs)
    return pl.pallas_call(
        kernel,
        out_shape=[
            pltpu.HBM(o, F32) if k in hbm_out else jax.ShapeDtypeStruct(o, F32) for k, o in enumerate(outs)
        ],
        in_specs=[pl.BlockSpec(memory_space=space(k)) for k in range(len(args))],
        out_specs=[
            pl.BlockSpec(memory_space=pltpu.HBM if k in hbm_out else pltpu.VMEM) for k in range(len(outs))
        ],
        scratch_shapes=scratch,
        input_output_aliases=aliases,
        compiler_params=pltpu.CompilerParams(vmem_limit_bytes=limit * MIB),
        cost_estimate=pl.CostEstimate(flops=0, bytes_accessed=moved, transcendentals=0),
    )(*args)


def shards(strain, labels, normals, moduli, mean_strain):
    parts = lax.axis_size("gz")
    x_devices = lax.axis_size("gx")
    _, sections, cells_x, cells_z = strain.shape
    x_total, z_total = cells_x * x_devices, cells_z * parts
    slots = z_total // 2 // x_devices
    lanes = 2 * slots
    z_fwd, z_inv = z_tables(z_total, slots, 1.0 / (x_total * z_total))
    x_tab = x_tables(x_total)
    block = (cells_x, cells_z)
    everyone = range(parts)

    def travel(field, blocks, gather):
        ends = INPLANE if field == 2 else everyone
        moved = [blocks[0]]
        for step in range(1, parts):
            way = [(k, (k + step) % parts) for k in range(parts)]
            way = [(a, b) for a, b in way if (b if gather else a) in ends]
            moved.append(lax.ppermute(blocks[step], "gz", way))
        return moved

    def held(fields):
        return pltpu.VMEM((parts, fields, cells_x, cells_z), F32)

    blocks = call(
        polarize_kernel,
        [block] * (FIELDS * parts),
        [
            held(FIELDS),
            pltpu.VMEM(strain.shape, F32),
            pltpu.VMEM(labels.shape, jnp.int32),
            pltpu.VMEM(normals.shape, jnp.int32),
            pltpu.SMEM(moduli.shape, F32),
            pltpu.SemaphoreType.DMA((2 + 2 * sections,)),
        ],
        (moduli, strain, labels, normals),
        16,
        range(4),
    )
    blocks = {f: list(blocks[f * parts : (f + 1) * parts]) for f in range(FIELDS)}
    quarter = x_total // 4
    chips = x_devices // 2
    early, late = CHUNKS
    size = len(early)
    grid = (x_devices, size, cells_x, lanes)
    tile = (chips, 1, cells_x, lanes)
    tile_early = (chips, size, cells_x, lanes)
    tiles = pltpu.VMEM((x_devices, 1, cells_x, lanes), F32)

    def exchange(own, swapped, after):
        got = lax.ppermute(swapped, "gx", [(k, k ^ 1) for k in range(x_devices)])
        merged = call(merge_kernel, [(2, *own.shape[1:])] * (chips - 1), [], (own, got), 8)
        merged, after = lax.optimization_barrier((merged, after))
        moved = [
            lax.ppermute(block, "gx", [(k, k ^ (2 * step)) for k in range(x_devices)])
            for step, block in enumerate(merged, 1)
        ]
        return (own, got, *moved), after

    args = [a for f in early for a in travel(f, blocks[f], True)]
    args, blocks = lax.optimization_barrier((args, blocks))
    scratch = [held(size), pltpu.VMEM(grid, F32)]
    dealt = call(z_forward_deal_kernel, [tile_early] * 2, scratch, (z_fwd, *args), 16)
    rows, blocks = exchange(*dealt, blocks)
    args = travel(late[0], blocks[late[0]], True)
    args, rows = lax.optimization_barrier((args, rows))
    own, swapped = call(z_forward_deal_kernel, [tile] * 2, [held(1), tiles], (z_fwd, *args), 16)
    last, rows = exchange(own, swapped, rows)
    (spectrum,) = call(
        x_forward_kernel, [(4, size, quarter, lanes)], [pltpu.VMEM(grid, F32)], (*x_tab, *rows), 24
    )
    own, swapped, late_spectrum = call(
        functools.partial(late_kernel, x_total, z_total, CHUNKS),
        [tile, tile, (4, 1, quarter, lanes)],
        [tiles, tiles, pltpu.VMEM((quarter, 5 * lanes), F32)],
        (moduli, mean_strain, *x_tab, spectrum, *last),
        24,
        smem=2,
    )
    last, late_spectrum = exchange(own, swapped, late_spectrum)
    rest = call(
        functools.partial(early_inverse_kernel, x_total, z_total, CHUNKS),
        [tile_early] * 2,
        [pltpu.VMEM(grid, F32), pltpu.VMEM((quarter, 5 * size * lanes), F32)],
        (moduli, mean_strain, *x_tab, spectrum, late_spectrum),
        24,
        smem=2,
    )
    rest, last = lax.optimization_barrier((rest, last))
    blocks = call(z_inverse_collect_kernel, [block] * parts, [held(1), tiles], (z_inv, *last), 16)
    rest, blocks = exchange(*rest, list(blocks))
    arrived = {late[0]: travel(late[0], blocks, False)}
    scratch = [held(size), pltpu.VMEM(grid, F32)]
    blocks = call(z_inverse_collect_kernel, [block] * (size * parts), scratch, (z_inv, *rest), 16)
    for slot, f in enumerate(early):
        arrived[f] = travel(f, blocks[slot * parts : (slot + 1) * parts], False)
    full = (6, sections, cells_x, cells_z)
    results = ()
    for slots, strains, stresses in (((0, 1), (XX, YY, ZZ, YZ, XY), (YY, YZ, XY)), ((0, 1, 2), (XZ,), (XX, ZZ, XZ))):
        args = (moduli, mean_strain, labels, normals, *[a for f in slots for a in arrived[f]], *results)
        hbm = range(len(args) - len(results), len(args))
        count = sections * (len(strains) + len(stresses))
        results = call(
            functools.partial(stress_kernel, slots, strains, stresses),
            [full, full],
            [held(FIELDS), pltpu.VMEM(full, F32), pltpu.VMEM(full, F32), pltpu.SemaphoreType.DMA((count,))],
            args,
            16,
            hbm,
            smem=2,
            hbm_out=(0, 1),
            aliases={k: out for out, k in enumerate(hbm)},
        )
    return tuple(results)


def orientation(normals, blk):
    tilt_angle = math.pi / ANGLES * normals.astype(jnp.float32)
    tilt_angle = jnp.repeat(jnp.repeat(tilt_angle, blk, axis=1), blk, axis=2)
    return (jnp.cos(tilt_angle), jnp.sin(tilt_angle))


def stress_law(strain_field, labels, cosine_tilt, sine_tilt, moduli):
    laminate = labels == 1
    lame_local = jnp.where(laminate, moduli[2], moduli[0])
    shear_local = jnp.where(laminate, moduli[3], moduli[1])
    trace_sum = strain_field[0] + strain_field[1] + strain_field[2]
    normal_part = (
        cosine_tilt * cosine_tilt * strain_field[0]
        + sine_tilt * sine_tilt * strain_field[2]
        + 2.0 * cosine_tilt * sine_tilt * strain_field[4]
    )
    laminate_term = moduli[4] * labels.astype(jnp.float32) * normal_part
    dyad = [
        cosine_tilt * cosine_tilt,
        None,
        sine_tilt * sine_tilt,
        None,
        cosine_tilt * sine_tilt,
        None,
    ]
    result = []
    for slot in range(6):
        value = 2.0 * shear_local * strain_field[slot]
        if slot < 3:
            value = value + lame_local * trace_sum
        if dyad[slot] is not None:
            value = value + laminate_term * dyad[slot]
        result.append(value)
    return jnp.stack(result)


def polarize(stresses, strain_field, lame_ref, shear_ref):
    trace_sum = strain_field[0] + strain_field[1] + strain_field[2]
    result = []
    for slot in range(6):
        value = stresses[slot] - 2.0 * shear_ref * strain_field[slot]
        if slot < 3:
            value = value - lame_ref * trace_sum
        result.append(value)
    return jnp.stack(result)


def green_apply(spectrum, unit_x, unit_z, lame_ref, shear_ref):
    coupling = (lame_ref + shear_ref) / (shear_ref * (lame_ref + 2.0 * shear_ref))
    traction_x = spectrum[0] * unit_x + spectrum[4] * unit_z
    traction_y = spectrum[5] * unit_x + spectrum[3] * unit_z
    traction_z = spectrum[4] * unit_x + spectrum[2] * unit_z
    normal_load = unit_x * traction_x + unit_z * traction_z
    half_inverse = 0.5 / shear_ref
    result = [
        2.0 * half_inverse * unit_x * traction_x - coupling * normal_load * unit_x * unit_x,
        jnp.zeros_like(traction_x),
        2.0 * half_inverse * unit_z * traction_z - coupling * normal_load * unit_z * unit_z,
        half_inverse * unit_z * traction_y,
        half_inverse * (unit_z * traction_x + unit_x * traction_z)
        - coupling * normal_load * unit_x * unit_z,
        half_inverse * unit_x * traction_y,
    ]
    return -jnp.stack(result)


def phases(left_ids, right_ids, length):
    product = left_ids[:, None] * right_ids[None, :] % length
    phase_angle = 2.0 * math.pi / length * product.astype(jnp.float32)
    return (jnp.cos(phase_angle), jnp.sin(phase_angle))


def contract(form, left_side, right_side):
    return jnp.einsum(
        form,
        left_side,
        right_side,
        precision=lax.Precision.HIGHEST,
        preferred_element_type=jnp.float32,
    )


def signed_value(counter, length):
    return jnp.where(counter < length // 2, counter, counter - length).astype(jnp.float32)


def shards_general(strain, labels, normals, moduli, mean_strain):
    z_devices = lax.axis_size("gz")
    x_devices = lax.axis_size("gx")
    z_index = lax.axis_index("gz")
    x_index = lax.axis_index("gx")
    sections = strain.shape[1]
    cells_x = strain.shape[2]
    cells_z = strain.shape[3]
    x_total = cells_x * x_devices
    z_total = cells_z * z_devices
    line_count = sections * cells_x
    kz_share = cells_z // x_devices
    cosine_tilt, sine_tilt = orientation(normals, strain.shape[2] // normals.shape[1])
    lame_ref = 0.5 * (moduli[0] + moduli[2])
    shear_ref = 0.5 * (moduli[1] + moduli[3])
    stresses = stress_law(strain, labels, cosine_tilt, sine_tilt, moduli)
    polarized = polarize(stresses, strain, lame_ref, shear_ref)
    flattened = polarized.reshape(6, line_count, cells_z)
    own_block = z_index * cells_z + jnp.arange(cells_z, dtype=jnp.int32)
    empty_sum = jnp.zeros((6, cells_z, line_count), jnp.float32)
    pieces = lax.all_gather(flattened, "gz", axis=2, tiled=True)
    z_ids = jnp.arange(pieces.shape[2], dtype=jnp.int32)
    cos_table, sin_table = phases(z_ids, own_block, z_total)
    real_part = contract("cmz,zk->ckm", pieces, cos_table)
    imag_part = (empty_sum, empty_sum)[1] - contract("cmz,zk->ckm", pieces, sin_table)
    real_rows, imag_rows = (
        lax.all_to_all(real_part, "gx", split_axis=1, concat_axis=2, tiled=True),
        lax.all_to_all(imag_part, "gx", split_axis=1, concat_axis=2, tiled=True),
    )
    grid_shape = (6, kz_share, x_devices, sections, cells_x)
    real_rows = real_rows.reshape(grid_shape)
    imag_rows = imag_rows.reshape(grid_shape)
    every_x = jnp.arange(x_total, dtype=jnp.int32)
    cos_x, sin_x = phases(every_x, every_x, x_total)
    cos_x = cos_x.reshape(x_devices, cells_x, x_total)
    sin_x = sin_x.reshape(x_devices, cells_x, x_total)
    spec_real = contract("ckgsx,gxq->cksq", real_rows, cos_x) + contract(
        "ckgsx,gxq->cksq", imag_rows, sin_x
    )
    spec_imag = contract("ckgsx,gxq->cksq", imag_rows, cos_x) - contract(
        "ckgsx,gxq->cksq", real_rows, sin_x
    )
    kz_ids = z_index * cells_z + x_index * kz_share + jnp.arange(kz_share, dtype=jnp.int32)
    freq_z = signed_value(kz_ids, z_total)[:, None, None]
    freq_x = signed_value(every_x, x_total)[None, None, :]
    radius_sq = freq_x * freq_x + freq_z * freq_z
    at_anchor = radius_sq == 0.0
    safe_radius = jnp.sqrt(jnp.where(at_anchor, 1.0, radius_sq))
    unit_x = freq_x / safe_radius
    unit_z = freq_z / safe_radius
    anchor_term = jnp.where(at_anchor, float(x_total * z_total), 0.0)
    new_real = green_apply(spec_real, unit_x, unit_z, lame_ref, shear_ref)
    new_real = new_real + mean_strain[:, None, None, None] * anchor_term[None]
    new_imag = green_apply(spec_imag, unit_x, unit_z, lame_ref, shear_ref)
    back_real = contract("cksq,gxq->ckgsx", new_real, cos_x) - contract(
        "cksq,gxq->ckgsx", new_imag, sin_x
    )
    back_imag = contract("cksq,gxq->ckgsx", new_real, sin_x) + contract(
        "cksq,gxq->ckgsx", new_imag, cos_x
    )
    back_real = back_real.reshape(6, kz_share, x_devices * line_count)
    back_imag = back_imag.reshape(6, kz_share, x_devices * line_count)
    real_part, imag_part = (
        lax.all_to_all(back_real, "gx", split_axis=2, concat_axis=1, tiled=True),
        lax.all_to_all(back_imag, "gx", split_axis=2, concat_axis=1, tiled=True),
    )
    z_ids = jnp.arange(lax.axis_size("gz") * cells_z, dtype=jnp.int32)
    cos_table, sin_table = phases(own_block, z_ids, z_total)
    summed = lax.psum_scatter(
        contract("ckm,kz->zcm", real_part, cos_table)
        - contract("ckm,kz->zcm", imag_part, sin_table),
        "gz",
        scatter_dimension=0,
        tiled=True,
    )
    field_lines = jnp.transpose(summed, (1, 2, 0))
    strain_next = (field_lines * (1.0 / (x_total * z_total))).reshape(6, sections, cells_x, cells_z)
    stress_next = stress_law(strain_next, labels, cosine_tilt, sine_tilt, moduli)
    return (strain_next, stress_next)


def solution(mesh):
    in_specs = (P(None, None, "gx", "gz"), P(None, "gx", "gz"), P(None, "gx", "gz"), P(), P())
    out_specs = (P(None, None, "gx", "gz"), P(None, None, "gx", "gz"))

    def run(strain, labels, normals, moduli, mean_strain):
        _, sections, x_total, z_total = strain.shape
        parts, x_devices = mesh.shape["gz"], mesh.shape["gx"]
        grouped = (
            sections == 2
            and parts == len(GROUPS)
            and x_devices == 8
            and z_total == 128 * x_devices
            and x_total % (128 * x_devices) == 0
        )
        body = shards if grouped else shards_general
        mapped = jax.shard_map(body, mesh=mesh, in_specs=in_specs, out_specs=out_specs, check_vma=False)
        return mapped(strain, labels, normals, moduli, mean_strain)

    return run
```

```python
import functools
import math

import jax
import jax.numpy as jnp
import numpy as np
from jax import lax
from jax.experimental import pallas as pl
from jax.experimental.pallas import tpu as pltpu
from jax.sharding import PartitionSpec as P

ANGLES = 8
XX, YY, ZZ, YZ, XZ, XY = range(6)
GROUPS = (
    ((XY, 0), (YZ, 0)),
    ((XX, 0), (ZZ, 0), (XZ, 0)),
    ((XX, 1), (ZZ, 1), (XZ, 1)),
    ((XY, 1), (YZ, 1)),
)
INPLANE = (1, 2)
FIELDS = 3
CHUNKS = ((0, 2), (1,))
F32, BF16 = jnp.float32, jnp.bfloat16
MIB = 1 << 20


def split_table(table):
    table = np.asarray(table, np.float32)
    high = table.astype(jnp.bfloat16)
    low = (table - high.astype(np.float32)).astype(jnp.bfloat16)
    return jnp.asarray(np.stack([high, low]))


def half_frequencies(length):
    quarter = length // 4
    return (
        4 * np.arange(quarter) + 1,
        4 * np.arange(quarter // 2),
        4 * np.arange(quarter // 2) + 2,
    )


def interleave(real, imag, slots):
    rows, count = real.shape
    both = np.stack([real.reshape(rows, -1, slots), imag.reshape(rows, -1, slots)], 2)
    return both.reshape(rows, 2 * count)


def z_tables(length, slots, scale):
    quarter = length // 4
    z = np.arange(quarter, dtype=np.int64)[:, None]
    ones, zeros, twos = half_frequencies(length)

    def angles(freqs):
        return 2.0 * math.pi / length * ((z * freqs[None, :]) % length)

    one, zero, two = angles(ones), angles(zeros), angles(twos)
    top = interleave(np.cos(one), -np.sin(one), slots)
    bottom = interleave(-np.sin(one), -np.cos(one), slots)
    forward_one = np.concatenate([top, bottom], 0)
    real, imag = np.cos(zero), -np.sin(zero)
    imag[:, 0] = np.where(np.arange(quarter) % 2 == 0, 1.0, -1.0)
    forward_zero = interleave(real, imag, slots)
    forward_two = interleave(np.cos(two), -np.sin(two), slots)
    weight = 2.0 * scale
    inverse_one = weight * np.concatenate(
        [interleave(np.cos(one), -np.sin(one), slots), interleave(np.sin(one), np.cos(one), slots)], 0
    ).T
    half = np.full(quarter // 2, weight)
    half[0] = scale
    inverse_zero = interleave(real * half, imag * half, slots).T
    inverse_two = weight * forward_two.T

    def pack(first, second, third):
        return split_table(np.concatenate([first, np.concatenate([second, third], 1)], 0))

    return pack(forward_one, forward_zero, forward_two), pack(inverse_one, inverse_zero, inverse_two)


def x_tables(length):
    quarter = length // 4
    k = np.arange(quarter, dtype=np.int64)
    angle = 2.0 * math.pi / quarter * ((k[:, None] * k[None, :]) % quarter)
    turn = 2.0 * math.pi / length * k
    columns = [f(residue * turn) for residue in (1, 2, 3) for f in (np.cos, np.sin)]
    twiddles = jnp.asarray(np.stack(columns + columns[:2], 1).astype(np.float32))
    return split_table(np.concatenate([np.cos(angle), np.sin(angle)], 0)), twiddles


def halves(value):
    high = value.astype(BF16)
    return high, (value - high.astype(F32)).astype(BF16)


def dot(left, right):
    return jnp.dot(left, right, preferred_element_type=F32)


def dot_right(value, table, part):
    big = table.shape[2]
    half = big // 2
    rows = slice(0, big) if part == 0 else slice(big, big + half)
    columns = slice(0, big) if part == 0 else slice((part - 1) * half, part * half)
    high_table, low_table = table[0, rows, columns], table[1, rows, columns]
    high, low = halves(value)
    return dot(high, high_table) + (dot(low, high_table) + dot(high, low_table))


def dot_left(table, value):
    high, low = halves(value)
    return dot(table[0], high) + (dot(table[0], low) + dot(table[1], high))


def tilt(normals, section, cells_z):
    blocks = normals[section].astype(F32)
    count = blocks.shape[1]
    size = cells_z // count
    owner = lax.broadcasted_iota(jnp.int32, (count, cells_z), 1) // size
    own = lax.broadcasted_iota(jnp.int32, (count, cells_z), 0)
    spread = jnp.where(owner == own, 1.0, 0.0).astype(F32)
    angle = (math.pi / ANGLES) * dot(blocks, spread)
    cosine, sine = jnp.cos(angle), jnp.sin(angle)
    return cosine * cosine, sine * sine, cosine * sine


def law(strain, label, squares, lame, shear, stiff):
    cc, ss, cs = squares
    laminate = label == 1
    lame_local = jnp.where(laminate, lame[1], lame[0])
    twice_shear = jnp.where(laminate, 2.0 * shear[1], 2.0 * shear[0])
    spherical = lame_local * (strain[XX] + strain[YY] + strain[ZZ])
    normal = cc * strain[XX] + ss * strain[ZZ] + 2.0 * cs * strain[XZ]
    normal = jnp.where(laminate, stiff, 0.0) * normal
    return {
        XX: twice_shear * strain[XX] + spherical + normal * cc,
        YY: twice_shear * strain[YY] + spherical,
        ZZ: twice_shear * strain[ZZ] + spherical + normal * ss,
        YZ: twice_shear * strain[YZ],
        XZ: twice_shear * strain[XZ] + normal * cs,
        XY: twice_shear * strain[XY],
    }


def row_of(squares, block, size):
    return [jnp.broadcast_to(s[block : block + 1], (size, s.shape[1])) for s in squares]


def polarize_kernel(moduli_h, strain_h, labels_h, normals_h, *rest):
    outs, (held, strain, labels, normals, moduli, sems) = rest[:-6], rest[-6:]
    sections, cells_x, cells_z = labels.shape
    copies = [
        pltpu.make_async_copy(moduli_h, moduli, sems.at[0]),
        pltpu.make_async_copy(normals_h, normals, sems.at[1]),
    ]
    for k in range(sections):
        copies.append(pltpu.make_async_copy(labels_h.at[k], labels.at[k], sems.at[2 + 2 * k]))
        copies.append(pltpu.make_async_copy(strain_h.at[:, k], strain.at[:, k], sems.at[3 + 2 * k]))
    for copy in copies:
        copy.start()
    for copy in copies[:2]:
        copy.wait()
    parts = len(GROUPS)
    place = lax.axis_index("gz")
    size = cells_x // normals.shape[1]
    lame_ref = 0.5 * (moduli[0] + moduli[2])
    shear_ref = 0.5 * (moduli[1] + moduli[3])
    lame = (moduli[0] - lame_ref, moduli[2] - lame_ref)
    shear = (moduli[1] - shear_ref, moduli[3] - shear_ref)
    for group, fields in enumerate(GROUPS):
        if len(fields) < 3:
            held[group, 2] = jnp.zeros((cells_x, cells_z), F32)
    for section in range(sections):
        copies[2 + 2 * section].wait()
        copies[3 + 2 * section].wait()
        squares = tilt(normals, section, cells_z)
        for block in range(cells_x // size):
            rows = pl.ds(block * size, size)
            local = [strain[c, section, rows, :] for c in range(6)]
            value = law(local, labels[section, rows, :], row_of(squares, block, size), lame, shear, moduli[4])
            for group, fields in enumerate(GROUPS):
                for slot, (component, of) in enumerate(fields):
                    if of == section:
                        held[group, slot, rows, :] = value[component]
    for step in range(parts):
        target = lax.rem(place + step, parts)
        for slot in range(FIELDS):
            outs[slot * parts + step][...] = held[target, slot]


def deal(blocks, own, swapped):
    mine = lax.axis_index("gx")
    chip, core = mine // 2, lax.rem(mine, 2)
    for step in range(own.shape[0]):
        there = 2 * lax.bitwise_xor(chip, step)
        own[step] = blocks[there + core]
        swapped[step] = blocks[there + 1 - core]


def collect(own, got, moved, blocks):
    mine = lax.axis_index("gx")
    chip, core = mine // 2, lax.rem(mine, 2)
    for step in range(own.shape[0]):
        there = 2 * lax.bitwise_xor(chip, step)
        blocks[there + core] = own[0] if step == 0 else moved[step - 1][0]
        blocks[there + 1 - core] = got[0] if step == 0 else moved[step - 1][1]


def merge_kernel(own, got, *outs):
    for k, out in enumerate(outs):
        out[0] = own[k + 1]
        out[1] = got[k + 1]


def z_forward_deal_kernel(table, *rest):
    arrived, (own, swapped, held, blocks) = rest[:-4], rest[-4:]
    z_forward_kernel(table, *arrived, blocks, held)
    deal(blocks, own, swapped)


def z_inverse_collect_kernel(table, own, got, *rest):
    chips = own.shape[0]
    moved, outs, (held, blocks) = rest[: chips - 1], rest[chips - 1 : -2], rest[-2:]
    collect(own, got, moved, blocks)
    z_inverse_kernel(table, blocks, *outs, held)


def z_forward_kernel(table, *rest):
    parts = len(GROUPS)
    arrived, (out, held) = rest[:-2], rest[-2:]
    place = lax.axis_index("gz")
    for step in range(parts):
        source = lax.rem(place + parts - step, parts)
        for slot in range(held.shape[1]):
            held[source, slot] = arrived[slot * parts + step][...]
    fields, rows, width = held.shape[1:]
    lanes = out.shape[3]
    z0, z1, z2, z3 = (held[k].reshape(fields * rows, width) for k in range(parts))
    first = jnp.concatenate([z0 - z2, z1 - z3], 1)
    even, odd = z0 + z2, z1 + z3
    spectra = (
        dot_right(first, table, 0),
        dot_right(even + odd, table, 1),
        dot_right(even - odd, table, 2),
    )
    target = 0
    for spectrum in spectra:
        for k in range(spectrum.shape[1] // lanes):
            out[target] = spectrum[:, k * lanes : (k + 1) * lanes].reshape(fields, rows, lanes)
            target += 1


def swap(value):
    lanes = value.shape[1]
    return jnp.concatenate([pltpu.roll(value[:, k : k + 128], 64, 1) for k in range(0, lanes, 128)], 1)


def turn_sign(width):
    lane = lax.broadcasted_iota(jnp.int32, (1, width), 1) % 128
    return jnp.where(lane < 64, 1.0, -1.0).astype(F32)


def twiddle(twiddles, residue, value, sign):
    if residue == 0:
        return value
    pick = 2 * (residue - 1)
    quarter = value.shape[0]
    cosine = jnp.broadcast_to(twiddles[:, pick : pick + 1], (quarter, 128))
    sine = jnp.broadcast_to(twiddles[:, pick + 1 : pick + 2], (quarter, 128)) * sign[:, :128]
    pieces = []
    for k in range(0, value.shape[1], 128):
        piece = value[:, k : k + 128]
        pieces.append(cosine * piece + sine * pltpu.roll(piece, 64, 1))
    return jnp.concatenate(pieces, 1)


def x_forward(data, table, twiddles):
    sources, fields, rows, lanes = data.shape
    quarter = sources * rows // 4
    per = sources // 4
    width = fields * lanes
    sign = turn_sign(width)
    block = [
        jnp.concatenate([data[a * per : (a + 1) * per, f].reshape(quarter, lanes) for f in range(fields)], 1)
        for a in range(4)
    ]
    even, odd = block[0] + block[2], block[1] + block[3]
    diff, turned = block[0] - block[2], sign * swap(block[1] - block[3])
    values = (even + odd, diff + turned, even - odd, diff - turned)
    values = [twiddle(twiddles, residue, value, sign) for residue, value in enumerate(values)]
    both = dot_left(table, jnp.concatenate(values, 1))
    for residue in range(4):
        columns = slice(residue * width, (residue + 1) * width)
        yield both[:quarter, columns] + sign * swap(both[quarter:, columns])


def x_inverse(spectra, table, twiddles, is_special, out):
    sources, fields, rows, lanes = out.shape
    quarter = sources * rows // 4
    per = sources // 4
    width = fields * lanes
    sign = turn_sign(spectra.shape[1])
    both = dot_left(table, spectra)
    both = both[:quarter] - sign * swap(both[quarter:])
    sign = sign[:, :width]

    def join(values):
        h0, h1, h2, h3 = [twiddle(twiddles, residue, value, -sign) for residue, value in enumerate(values)]
        even, odd = h0 + h2, h1 + h3
        diff, turned = h0 - h2, sign * swap(h1 - h3)
        return even + odd, diff - turned, even - odd, diff + turned

    packed = both[:, 4 * width :]
    unpacked = [packed]
    for residue in range(1, 4):
        pieces = [pltpu.roll(packed[:, k : k + lanes], lanes - residue, 1) for k in range(0, width, lanes)]
        unpacked.append(jnp.concatenate(pieces, 1))
    lane = lax.broadcasted_iota(jnp.int32, (1, width), 1) % lanes
    edge = jnp.logical_and(is_special, lane == lanes // 2)
    whole = join([both[:, residue * width : (residue + 1) * width] for residue in range(4)])
    for a, (value, other) in enumerate(zip(whole, join(unpacked))):
        final = jnp.where(edge, other, value)
        for f in range(fields):
            out[a * per : (a + 1) * per, f] = final[:, f * lanes : (f + 1) * lanes].reshape(per, rows, lanes)


def holds_edge(slots, z_cells):
    return lax.axis_index("gx") * slots == z_cells // 4


def x_forward_kernel(table, twiddles, own, got, *rest):
    moved, (out, data) = rest[:-2], rest[-2:]
    collect(own, got, moved, data)
    fields, lanes = data.shape[1], data.shape[3]
    for residue, spectrum in enumerate(x_forward(data, table, twiddles)):
        for f in range(fields):
            out[residue, f] = spectrum[:, f * lanes : (f + 1) * lanes]


def green_rows(x_cells, z_cells, chunk, moduli, mean, load, new):
    quarter, lanes = new.shape[0], new.shape[1] // (5 * len(chunk))
    slots = lanes // 2
    place, mine = lax.axis_index("gz"), lax.axis_index("gx")
    inplane = functools.reduce(jnp.logical_or, [place == k for k in INPLANE])
    lame_ref = 0.5 * (moduli[0] + moduli[2])
    shear_ref = 0.5 * (moduli[1] + moduli[3])
    half_inverse = 0.5 / shear_ref
    coupling = (lame_ref + shear_ref) / (shear_ref * (lame_ref + 2.0 * shear_ref))
    c1 = jnp.where(inplane, coupling, 0.0)
    k1 = jnp.where(inplane, 2.0 * half_inverse, half_inverse)
    k2 = jnp.where(inplane, half_inverse, 0.0)
    ka = jnp.where(inplane, 0.0, half_inverse)
    total = float(x_cells * z_cells)
    means = (
        total * jnp.where(inplane, mean[XX], mean[XY]),
        total * jnp.where(inplane, mean[ZZ], mean[YZ]),
        total * mean[XZ],
    )

    def store(field, residue, rows, value):
        block = residue * len(chunk) + chunk.index(field)
        new[rows, block * lanes : (block + 1) * lanes] = value

    def green(kx, kz, odd_kx, s, anchored=False):
        radius = kx * kx + kz * kz
        if anchored:
            radius = jnp.where(radius == 0.0, 1.0, radius)
        inverse = 1.0 / radius
        a, b = kx * kx * inverse, kz * kz * inverse
        d = odd_kx * kz * inverse
        ab = c1 * (a * b)
        ca, cb = c1 * a, c1 * b
        h02, h12 = d * (ca - k2), d * (cb - k2)
        m01 = ab - ka * d
        twice = 2.0 * s[2]
        rows = (
            lambda: a * (ca - k1) * s[0] + m01 * s[1] + h02 * twice,
            lambda: m01 * s[0] + b * (cb - k1) * s[1] + h12 * twice,
            lambda: h02 * s[0] + h12 * s[1] + (2.0 * ab - k2) * s[2],
        )
        return {f: rows[f]() for f in chunk}

    lane = lax.broadcasted_iota(jnp.int32, (1, lanes), 1)
    slot_of = lane % slots
    order = mine * slots + slot_of
    zeros_at, twos_at = z_cells // 4, z_cells // 4 + z_cells // 8
    kz = jnp.where(
        order < zeros_at,
        4 * order + 1,
        jnp.where(order < twos_at, 4 * (order - zeros_at), 4 * (order - twos_at) + 2),
    )
    kz = jnp.where(kz < z_cells // 2, kz, kz - z_cells).astype(F32)
    special = order == zeros_at
    size = 32
    for start in range(0, quarter, size):
        rows = pl.ds(start, size)
        row = lax.broadcasted_iota(jnp.int32, (size, lanes), 0) + start
        full_kz = jnp.broadcast_to(kz, (size, lanes))
        first_kx = (4 * row - (x_cells if 2 * start >= quarter else 0)).astype(F32)
        mirror = 2 * start == quarter
        edge = [None] * FIELDS
        for residue in range(4):
            s = [load(f, residue, rows) for f in range(FIELDS)]
            for f in range(FIELDS):
                moved = s[f] if residue == 0 else pltpu.roll(s[f], residue, 1)
                edge[f] = moved if residue == 0 else jnp.where(slot_of == residue, moved, edge[f])
            kx = first_kx + float(residue)
            odd_kx = jnp.where(row == start, 0.0, kx) if mirror and residue == 0 else kx
            with_anchor = residue == 0 and start == 0
            fresh = green(kx, full_kz, odd_kx, s, with_anchor)
            if with_anchor:
                anchor = jnp.logical_and(row == 0, special)
                for f in chunk:
                    fresh[f] = jnp.where(anchor, jnp.where(lane < slots, means[f], 0.0), fresh[f])
            for f in chunk:
                store(f, residue, rows, fresh[f])
        kx = first_kx + slot_of.astype(F32)
        odd_kx = jnp.where(jnp.logical_and(row == start, slot_of == 0), kx, 0.0) if mirror else jnp.zeros_like(kx)
        fresh = green(kx, jnp.full((size, lanes), -0.5 * z_cells, F32), odd_kx, edge)
        for f in chunk:
            store(f, 4, rows, fresh[f])


def loader(chunks, early, late):
    def load(field, residue, rows):
        spectra, chunk = (early, chunks[0]) if field in chunks[0] else (late, chunks[1])
        return spectra[residue, chunk.index(field), rows, :]

    return load


def early_inverse_kernel(x_cells, z_cells, chunks, moduli, mean, table, twiddles, early, late, own, swapped, out, new):
    green_rows(x_cells, z_cells, chunks[0], moduli, mean, loader(chunks, early, late), new)
    x_inverse(new[...], table, twiddles, holds_edge(out.shape[3] // 2, z_cells), out)
    deal(out, own, swapped)


def late_kernel(x_cells, z_cells, chunks, moduli, mean, table, twiddles, early, own_in, got, *rest):
    chips = own_in.shape[0]
    moved, rest = rest[: chips - 1], rest[chips - 1 :]
    own_out, swapped, late, data, out, new = rest
    collect(own_in, got, moved, data)
    lanes = data.shape[3]
    for residue, spectrum in enumerate(x_forward(data, table, twiddles)):
        for slot in range(data.shape[1]):
            late[residue, slot] = spectrum[:, slot * lanes : (slot + 1) * lanes]
    green_rows(x_cells, z_cells, chunks[1], moduli, mean, loader(chunks, early, late), new)
    x_inverse(new[...], table, twiddles, holds_edge(lanes // 2, z_cells), out)
    deal(out, own_out, swapped)


def z_inverse_kernel(table, data, *rest):
    outs, held = rest[:-1], rest[-1]
    parts = len(GROUPS)
    place = lax.axis_index("gz")
    sources, fields, rows, lanes = data.shape
    half = sources // 2
    fourth = sources // 4

    def columns(begin, end):
        return jnp.concatenate([data[k].reshape(fields * rows, lanes) for k in range(begin, end)], 1)

    first = dot_right(columns(0, half), table, 0)
    zero = dot_right(columns(half, half + fourth), table, 1)
    two = dot_right(columns(half + fourth, sources), table, 2)
    width = zero.shape[1]
    real, imag = first[:, :width], first[:, width:]
    plus, minus = zero + two, zero - two
    for k, value in enumerate((plus + real, minus - imag, plus - real, minus + imag)):
        held[k] = value.reshape(fields, rows, width)
    for step in range(parts):
        target = lax.rem(place + step, parts)
        for slot in range(fields):
            outs[slot * parts + step][...] = held[target, slot]


def stress_kernel(slots, strain_parts, stress_parts, moduli, mean, labels, normals, *rest):
    parts = len(GROUPS)
    arrived = rest[: len(slots) * parts]
    strain_to, stress_to, held, strain_out, stress_out, sems = rest[-6:]
    place = lax.axis_index("gz")
    sections, cells_x, cells_z = labels.shape
    size = cells_x // normals.shape[1]
    for step in range(parts):
        source = lax.rem(place + parts - step, parts)
        needed = functools.reduce(jnp.logical_or, [source == g for g in INPLANE]) if XZ in strain_parts else True

        @pl.when(needed)
        def _(source=source, step=step):
            for k, slot in enumerate(slots):
                held[source, slot] = arrived[k * parts + step][...]

    copies = []
    for section in range(sections):
        squares = tilt(normals, section, cells_z)
        for block in range(cells_x // size):
            rows = pl.ds(block * size, size)
            local = {c: jnp.zeros((size, cells_z), F32) for c in range(6)}
            local[YY] = jnp.full((size, cells_z), mean[YY], F32)
            for group, fields in enumerate(GROUPS):
                for slot, (component, of) in enumerate(fields):
                    if of == section and slot in slots and (group in INPLANE or XZ not in strain_parts):
                        local[component] = held[group, slot, rows, :]
            value = law(
                local,
                labels[section, rows, :],
                row_of(squares, block, size),
                (moduli[0], moduli[2]),
                (moduli[1], moduli[3]),
                moduli[4],
            )
            for component in strain_parts:
                strain_out[component, section, rows, :] = local[component]
            for component in stress_parts:
                stress_out[component, section, rows, :] = value[component]
        for here, there, chosen in ((strain_out, strain_to, strain_parts), (stress_out, stress_to, stress_parts)):
            for c in chosen:
                copy = pltpu.make_async_copy(here.at[c, section], there.at[c, section], sems.at[len(copies)])
                copy.start()
                copies.append(copy)
    for copy in copies:
        copy.wait()


def call(kernel, outs, scratch, args, limit, hbm=(), smem=0, hbm_out=(), aliases={}):
    def space(k):
        return pltpu.HBM if k in hbm else pltpu.SMEM if k < smem else pltpu.VMEM

    args = [pltpu.with_memory_space_constraint(a, pltpu.HBM) if k in hbm else a for k, a in enumerate(args)]
    moved = sum(a.size * a.dtype.itemsize for a in args) + sum(math.prod(o) * 4 for o in outs)
    return pl.pallas_call(
        kernel,
        out_shape=[
            pltpu.HBM(o, F32) if k in hbm_out else jax.ShapeDtypeStruct(o, F32) for k, o in enumerate(outs)
        ],
        in_specs=[pl.BlockSpec(memory_space=space(k)) for k in range(len(args))],
        out_specs=[
            pl.BlockSpec(memory_space=pltpu.HBM if k in hbm_out else pltpu.VMEM) for k in range(len(outs))
        ],
        scratch_shapes=scratch,
        input_output_aliases=aliases,
        compiler_params=pltpu.CompilerParams(vmem_limit_bytes=limit * MIB),
        cost_estimate=pl.CostEstimate(flops=0, bytes_accessed=moved, transcendentals=0),
    )(*args)


def shards(strain, labels, normals, moduli, mean_strain):
    parts = lax.axis_size("gz")
    x_devices = lax.axis_size("gx")
    _, sections, cells_x, cells_z = strain.shape
    x_total, z_total = cells_x * x_devices, cells_z * parts
    slots = z_total // 2 // x_devices
    lanes = 2 * slots
    z_fwd, z_inv = z_tables(z_total, slots, 1.0 / (x_total * z_total))
    x_tab = x_tables(x_total)
    block = (cells_x, cells_z)
    everyone = range(parts)

    def travel(field, blocks, gather):
        ends = INPLANE if field == 2 else everyone
        moved = [blocks[0]]
        for step in range(1, parts):
            way = [(k, (k + step) % parts) for k in range(parts)]
            way = [(a, b) for a, b in way if (b if gather else a) in ends]
            moved.append(lax.ppermute(blocks[step], "gz", way))
        return moved

    def held(fields):
        return pltpu.VMEM((parts, fields, cells_x, cells_z), F32)

    blocks = call(
        polarize_kernel,
        [block] * (FIELDS * parts),
        [
            held(FIELDS),
            pltpu.VMEM(strain.shape, F32),
            pltpu.VMEM(labels.shape, jnp.int32),
            pltpu.VMEM(normals.shape, jnp.int32),
            pltpu.SMEM(moduli.shape, F32),
            pltpu.SemaphoreType.DMA((2 + 2 * sections,)),
        ],
        (moduli, strain, labels, normals),
        16,
        range(4),
    )
    blocks = {f: list(blocks[f * parts : (f + 1) * parts]) for f in range(FIELDS)}
    quarter = x_total // 4
    chips = x_devices // 2
    early, late = CHUNKS
    size = len(early)
    grid = (x_devices, size, cells_x, lanes)
    tile = (chips, 1, cells_x, lanes)
    tile_early = (chips, size, cells_x, lanes)
    tiles = pltpu.VMEM((x_devices, 1, cells_x, lanes), F32)

    def exchange(own, swapped, after):
        got = lax.ppermute(swapped, "gx", [(k, k ^ 1) for k in range(x_devices)])
        merged = call(merge_kernel, [(2, *own.shape[1:])] * (chips - 1), [], (own, got), 8)
        merged, after = lax.optimization_barrier((merged, after))
        moved = [
            lax.ppermute(block, "gx", [(k, k ^ (2 * step)) for k in range(x_devices)])
            for step, block in enumerate(merged, 1)
        ]
        return (own, got, *moved), after

    args = [a for f in early for a in travel(f, blocks[f], True)]
    args, blocks = lax.optimization_barrier((args, blocks))
    scratch = [held(size), pltpu.VMEM(grid, F32)]
    dealt = call(z_forward_deal_kernel, [tile_early] * 2, scratch, (z_fwd, *args), 16)
    rows, blocks = exchange(*dealt, blocks)
    args = travel(late[0], blocks[late[0]], True)
    args, rows = lax.optimization_barrier((args, rows))
    own, swapped = call(z_forward_deal_kernel, [tile] * 2, [held(1), tiles], (z_fwd, *args), 16)
    last, rows = exchange(own, swapped, rows)
    (spectrum,) = call(
        x_forward_kernel, [(4, size, quarter, lanes)], [pltpu.VMEM(grid, F32)], (*x_tab, *rows), 24
    )
    own, swapped, late_spectrum = call(
        functools.partial(late_kernel, x_total, z_total, CHUNKS),
        [tile, tile, (4, 1, quarter, lanes)],
        [tiles, tiles, pltpu.VMEM((quarter, 5 * lanes), F32)],
        (moduli, mean_strain, *x_tab, spectrum, *last),
        24,
        smem=2,
    )
    last, late_spectrum = exchange(own, swapped, late_spectrum)
    rest = call(
        functools.partial(early_inverse_kernel, x_total, z_total, CHUNKS),
        [tile_early] * 2,
        [pltpu.VMEM(grid, F32), pltpu.VMEM((quarter, 5 * size * lanes), F32)],
        (moduli, mean_strain, *x_tab, spectrum, late_spectrum),
        24,
        smem=2,
    )
    rest, last = lax.optimization_barrier((rest, last))
    blocks = call(z_inverse_collect_kernel, [block] * parts, [held(1), tiles], (z_inv, *last), 16)
    rest, blocks = exchange(*rest, list(blocks))
    arrived = {late[0]: travel(late[0], blocks, False)}
    scratch = [held(size), pltpu.VMEM(grid, F32)]
    blocks = call(z_inverse_collect_kernel, [block] * (size * parts), scratch, (z_inv, *rest), 16)
    for slot, f in enumerate(early):
        arrived[f] = travel(f, blocks[slot * parts : (slot + 1) * parts], False)
    full = (6, sections, cells_x, cells_z)
    results = ()
    for slots, strains, stresses in (((0, 1), (XX, YY, ZZ, YZ, XY), (YY, YZ, XY)), ((0, 1, 2), (XZ,), (XX, ZZ, XZ))):
        args = (moduli, mean_strain, labels, normals, *[a for f in slots for a in arrived[f]], *results)
        hbm = range(len(args) - len(results), len(args))
        count = sections * (len(strains) + len(stresses))
        results = call(
            functools.partial(stress_kernel, slots, strains, stresses),
            [full, full],
            [held(FIELDS), pltpu.VMEM(full, F32), pltpu.VMEM(full, F32), pltpu.SemaphoreType.DMA((count,))],
            args,
            16,
            hbm,
            smem=2,
            hbm_out=(0, 1),
            aliases={k: out for out, k in enumerate(hbm)},
        )
    return tuple(results)


def orientation(normals, blk):
    tilt_angle = math.pi / ANGLES * normals.astype(jnp.float32)
    tilt_angle = jnp.repeat(jnp.repeat(tilt_angle, blk, axis=1), blk, axis=2)
    return (jnp.cos(tilt_angle), jnp.sin(tilt_angle))


def stress_law(strain_field, labels, cosine_tilt, sine_tilt, moduli):
    laminate = labels == 1
    lame_local = jnp.where(laminate, moduli[2], moduli[0])
    shear_local = jnp.where(laminate, moduli[3], moduli[1])
    trace_sum = strain_field[0] + strain_field[1] + strain_field[2]
    normal_part = (
        cosine_tilt * cosine_tilt * strain_field[0]
        + sine_tilt * sine_tilt * strain_field[2]
        + 2.0 * cosine_tilt * sine_tilt * strain_field[4]
    )
    laminate_term = moduli[4] * labels.astype(jnp.float32) * normal_part
    dyad = [
        cosine_tilt * cosine_tilt,
        None,
        sine_tilt * sine_tilt,
        None,
        cosine_tilt * sine_tilt,
        None,
    ]
    result = []
    for slot in range(6):
        value = 2.0 * shear_local * strain_field[slot]
        if slot < 3:
            value = value + lame_local * trace_sum
        if dyad[slot] is not None:
            value = value + laminate_term * dyad[slot]
        result.append(value)
    return jnp.stack(result)


def polarize(stresses, strain_field, lame_ref, shear_ref):
    trace_sum = strain_field[0] + strain_field[1] + strain_field[2]
    result = []
    for slot in range(6):
        value = stresses[slot] - 2.0 * shear_ref * strain_field[slot]
        if slot < 3:
            value = value - lame_ref * trace_sum
        result.append(value)
    return jnp.stack(result)


def green_apply(spectrum, unit_x, unit_z, lame_ref, shear_ref):
    coupling = (lame_ref + shear_ref) / (shear_ref * (lame_ref + 2.0 * shear_ref))
    traction_x = spectrum[0] * unit_x + spectrum[4] * unit_z
    traction_y = spectrum[5] * unit_x + spectrum[3] * unit_z
    traction_z = spectrum[4] * unit_x + spectrum[2] * unit_z
    normal_load = unit_x * traction_x + unit_z * traction_z
    half_inverse = 0.5 / shear_ref
    result = [
        2.0 * half_inverse * unit_x * traction_x - coupling * normal_load * unit_x * unit_x,
        jnp.zeros_like(traction_x),
        2.0 * half_inverse * unit_z * traction_z - coupling * normal_load * unit_z * unit_z,
        half_inverse * unit_z * traction_y,
        half_inverse * (unit_z * traction_x + unit_x * traction_z)
        - coupling * normal_load * unit_x * unit_z,
        half_inverse * unit_x * traction_y,
    ]
    return -jnp.stack(result)


def phases(left_ids, right_ids, length):
    product = left_ids[:, None] * right_ids[None, :] % length
    phase_angle = 2.0 * math.pi / length * product.astype(jnp.float32)
    return (jnp.cos(phase_angle), jnp.sin(phase_angle))


def contract(form, left_side, right_side):
    return jnp.einsum(
        form,
        left_side,
        right_side,
        precision=lax.Precision.HIGHEST,
        preferred_element_type=jnp.float32,
    )


def signed_value(counter, length):
    return jnp.where(counter < length // 2, counter, counter - length).astype(jnp.float32)


def shards_general(strain, labels, normals, moduli, mean_strain):
    z_devices = lax.axis_size("gz")
    x_devices = lax.axis_size("gx")
    z_index = lax.axis_index("gz")
    x_index = lax.axis_index("gx")
    sections = strain.shape[1]
    cells_x = strain.shape[2]
    cells_z = strain.shape[3]
    x_total = cells_x * x_devices
    z_total = cells_z * z_devices
    line_count = sections * cells_x
    kz_share = cells_z // x_devices
    cosine_tilt, sine_tilt = orientation(normals, strain.shape[2] // normals.shape[1])
    lame_ref = 0.5 * (moduli[0] + moduli[2])
    shear_ref = 0.5 * (moduli[1] + moduli[3])
    stresses = stress_law(strain, labels, cosine_tilt, sine_tilt, moduli)
    polarized = polarize(stresses, strain, lame_ref, shear_ref)
    flattened = polarized.reshape(6, line_count, cells_z)
    own_block = z_index * cells_z + jnp.arange(cells_z, dtype=jnp.int32)
    empty_sum = jnp.zeros((6, cells_z, line_count), jnp.float32)
    pieces = lax.all_gather(flattened, "gz", axis=2, tiled=True)
    z_ids = jnp.arange(pieces.shape[2], dtype=jnp.int32)
    cos_table, sin_table = phases(z_ids, own_block, z_total)
    real_part = contract("cmz,zk->ckm", pieces, cos_table)
    imag_part = (empty_sum, empty_sum)[1] - contract("cmz,zk->ckm", pieces, sin_table)
    real_rows, imag_rows = (
        lax.all_to_all(real_part, "gx", split_axis=1, concat_axis=2, tiled=True),
        lax.all_to_all(imag_part, "gx", split_axis=1, concat_axis=2, tiled=True),
    )
    grid_shape = (6, kz_share, x_devices, sections, cells_x)
    real_rows = real_rows.reshape(grid_shape)
    imag_rows = imag_rows.reshape(grid_shape)
    every_x = jnp.arange(x_total, dtype=jnp.int32)
    cos_x, sin_x = phases(every_x, every_x, x_total)
    cos_x = cos_x.reshape(x_devices, cells_x, x_total)
    sin_x = sin_x.reshape(x_devices, cells_x, x_total)
    spec_real = contract("ckgsx,gxq->cksq", real_rows, cos_x) + contract(
        "ckgsx,gxq->cksq", imag_rows, sin_x
    )
    spec_imag = contract("ckgsx,gxq->cksq", imag_rows, cos_x) - contract(
        "ckgsx,gxq->cksq", real_rows, sin_x
    )
    kz_ids = z_index * cells_z + x_index * kz_share + jnp.arange(kz_share, dtype=jnp.int32)
    freq_z = signed_value(kz_ids, z_total)[:, None, None]
    freq_x = signed_value(every_x, x_total)[None, None, :]
    radius_sq = freq_x * freq_x + freq_z * freq_z
    at_anchor = radius_sq == 0.0
    safe_radius = jnp.sqrt(jnp.where(at_anchor, 1.0, radius_sq))
    unit_x = freq_x / safe_radius
    unit_z = freq_z / safe_radius
    anchor_term = jnp.where(at_anchor, float(x_total * z_total), 0.0)
    new_real = green_apply(spec_real, unit_x, unit_z, lame_ref, shear_ref)
    new_real = new_real + mean_strain[:, None, None, None] * anchor_term[None]
    new_imag = green_apply(spec_imag, unit_x, unit_z, lame_ref, shear_ref)
    back_real = contract("cksq,gxq->ckgsx", new_real, cos_x) - contract(
        "cksq,gxq->ckgsx", new_imag, sin_x
    )
    back_imag = contract("cksq,gxq->ckgsx", new_real, sin_x) + contract(
        "cksq,gxq->ckgsx", new_imag, cos_x
    )
    back_real = back_real.reshape(6, kz_share, x_devices * line_count)
    back_imag = back_imag.reshape(6, kz_share, x_devices * line_count)
    real_part, imag_part = (
        lax.all_to_all(back_real, "gx", split_axis=2, concat_axis=1, tiled=True),
        lax.all_to_all(back_imag, "gx", split_axis=2, concat_axis=1, tiled=True),
    )
    z_ids = jnp.arange(lax.axis_size("gz") * cells_z, dtype=jnp.int32)
    cos_table, sin_table = phases(own_block, z_ids, z_total)
    summed = lax.psum_scatter(
        contract("ckm,kz->zcm", real_part, cos_table)
        - contract("ckm,kz->zcm", imag_part, sin_table),
        "gz",
        scatter_dimension=0,
        tiled=True,
    )
    field_lines = jnp.transpose(summed, (1, 2, 0))
    strain_next = (field_lines * (1.0 / (x_total * z_total))).reshape(6, sections, cells_x, cells_z)
    stress_next = stress_law(strain_next, labels, cosine_tilt, sine_tilt, moduli)
    return (strain_next, stress_next)


def solution(mesh):
    in_specs = (P(None, None, "gx", "gz"), P(None, "gx", "gz"), P(None, "gx", "gz"), P(), P())
    out_specs = (P(None, None, "gx", "gz"), P(None, None, "gx", "gz"))

    def run(strain, labels, normals, moduli, mean_strain):
        _, sections, x_total, z_total = strain.shape
        parts, x_devices = mesh.shape["gz"], mesh.shape["gx"]
        grouped = (
            sections == 2
            and parts == len(GROUPS)
            and x_devices == 8
            and z_total == 128 * x_devices
            and x_total % (128 * x_devices) == 0
        )
        body = shards if grouped else shards_general
        mapped = jax.shard_map(body, mesh=mesh, in_specs=in_specs, out_specs=out_specs, check_vma=False)
        return mapped(strain, labels, normals, moduli, mean_strain)

    return run
```
